32 devices in a mesh: ens: 4 (over x, core), pix: 8 (over z, y).
Axes of the slice: x: 2, y: 2, z: 4, core: 2. Of those that a mesh axis runs over, the one named last changes fastest.
Arguments:
- sample_layer_feed: bfloat16 [4, 1024, 1024], P('ens', 'pix'), may hold values from -54 to 54
- gain: float32 [1024], replicated, may hold values from 0.1 to 1.9
- w_query: bfloat16 [1024, 512], P('ens'), may hold values from -15 to 15
- w_key: bfloat16 [1024, 512], P('ens'), may hold values from -0.1875 to 0.1875
- w_value: bfloat16 [1024, 512], P('ens'), may hold values from -0.1875 to 0.1875
- w_out: bfloat16 [512, 1024], P(None, 'ens'), may hold values from -0.25 to 0.25
- readout_matrix: bfloat16 [1024, 128], replicated, may hold values from -0.1875 to 0.1875
- target: float32 [1024, 128], P('pix'), may hold values from -6 to 6
- pixel_weight: float32 [1024], P('pix'), may hold values from 0.25 to 6
- pix_mask: int32 [1024], replicated, may hold values from 0 to 1, as said below
- neighbours: int32 [8, 9], P('pix'), may hold values from 0 to 7, as said below
- neighbour_mask: int32 [8, 9], P('pix'), may hold values from 0 to 1, as said below
Outputs:
- loss: float32 [], replicated
- grad_w_out: float32 [512, 1024], P(None, 'ens')
- grad_w_value: float32 [1024, 512], P('ens')
The draws below stay inside these ranges and needn't reach their ends.
Inputs may be any that keep to these rules, and one draw needn't show every extreme that they name: `neighbours`: slot 0 of tile t names t itself; every slot names tile t, t - 1 or t + 1 (the tiles of the same and the neighbouring pix devices). `neighbour_mask`: slot 0 is live in every tile. `pix_mask`: in every tile the real pixels come first, and they are half of the tile or more.
All inputs are finite; a program needn't handle non-finite values.
Results may differ from the reference program's by a relative error of at most 0.025.
The reference program's roundings to bfloat16 on the way count: a program that leaves them out, or rounds other values in their place, can miss the bound.
Values may be sent and summed in bfloat16 or wider, within the bound.
No kernel may reach another device: no remote copies, remote signals or barrier semaphores. Data moves between devices by JAX's collectives and lax.ppermute only.
A program may use at most 64 MiB of HBM per device.

```python
import math
import jax
import jax.numpy as jnp
from jax import lax

D = 1024
HEADS = 8
HD = 64
VARS = 128
TILE = 128
NB = 9
PIX_DEV = 128
INNER = 512
MEMBERS = 4
PIX = 1024
TILES = 8


def neighbour_table(key):
    blocks = PIX_DEV // TILE
    span_tiles = 3 * blocks
    tile_ids = jnp.arange(TILES, dtype=jnp.int32)
    block_ids = tile_ids // blocks
    offsets = jnp.arange(span_tiles, dtype=jnp.int32)
    candidate = (block_ids[:, None] - 1) * blocks + offsets[None, :]
    usable_all = (candidate >= 0) & (candidate < TILES) & (candidate != tile_ids[:, None])
    ranking = jax.random.randint(key, (TILES, span_tiles), 0, 4096, dtype=jnp.int32) * span_tiles + offsets[None, :]
    ranking = jnp.where(usable_all, ranking, 4096 * span_tiles + offsets[None, :])
    order = jnp.argsort(ranking, axis=1)
    taken = min(NB - 1, span_tiles)
    picked = jnp.take_along_axis(candidate, order[:, :taken], axis=1)
    usable = jnp.take_along_axis(usable_all, order[:, :taken], axis=1)
    if taken < NB - 1:
        picked = jnp.concatenate([picked, jnp.broadcast_to(tile_ids[:, None], (TILES, NB - 1 - taken))], axis=1)
        usable = jnp.concatenate([usable, jnp.zeros((TILES, NB - 1 - taken), dtype=bool)], axis=1)
    picked = jnp.where(usable, picked, tile_ids[:, None])
    extra = jax.random.randint(jax.random.fold_in(key, 3), (TILES, NB - 1), 0, 8, dtype=jnp.int32) > 0
    live_slots = (usable & extra).astype(jnp.int32)
    table = jnp.concatenate([tile_ids[:, None], picked], axis=1).astype(jnp.int32)
    slot_mask = jnp.concatenate([jnp.ones((TILES, 1), jnp.int32), live_slots], axis=1)
    return (table, slot_mask)


def draw_neighbours(key, part):
    return neighbour_table(jax.random.fold_in(key, 11))[0]


def draw_neighbour_mask(key, part):
    return neighbour_table(jax.random.fold_in(key, 11))[1]


def draw_pix_mask(key, part):
    live_count = jax.random.randint(jax.random.fold_in(key, 5), (TILES,), TILE // 2, TILE + 1, dtype=jnp.int32)
    position = jnp.arange(TILE, dtype=jnp.int32)
    return (position[None, :] < live_count[:, None]).astype(jnp.int32).reshape(PIX)


def draw_pixel_weight(key, part):
    position = jnp.arange(PIX, dtype=jnp.float32)
    ramp = 1.0 + 2.0 * position / (PIX - 1)
    factor = jax.random.uniform(jax.random.fold_in(key, 2), (PIX,), jnp.float32, 0.5, 1.5)
    return (ramp * factor).astype(jnp.float32)


def draw_w_query(key, part):
    base = jnp.clip(jax.random.normal(jax.random.fold_in(key, 1), (D, INNER), jnp.float32), -4.0, 4.0) * D ** (-0.5)
    return base.astype(jnp.bfloat16)


def draw_sample_layer_feed(key, part):
    member_pos = jnp.arange(MEMBERS, dtype=jnp.float32) / (MEMBERS - 1)
    entries = jnp.clip(jax.random.normal(jax.random.fold_in(key, 21), (MEMBERS, PIX, D), jnp.float32), -3.0, 3.0)
    member_scale = jnp.exp(member_pos * math.log(6.0))
    pairing = jax.random.permutation(jax.random.fold_in(key, 23), MEMBERS).astype(jnp.int32)
    feature_block = jnp.arange(D, dtype=jnp.int32) // (D // MEMBERS)
    spike = jnp.where(feature_block[None, :] == pairing[:, None], 3.0, 1.0).astype(jnp.float32)
    values = entries * member_scale[:, None, None] * spike[:, None, :]
    return values.astype(jnp.bfloat16)


def level_of(own_key, extent, pieces, smallest, high):
    def one(dim, shards_of):
        steps = jax.random.uniform(jax.random.fold_in(jax.random.fold_in(own_key, 6), dim), (shards_of,), jnp.float32, smallest / len(pieces), high / len(pieces))
        return jnp.repeat(jnp.exp(steps), extent[dim] // shards_of).reshape((-1,) + (1,) * (len(extent) - dim - 1))

    factor_of = one(*pieces[0])
    for cut in pieces[1:]:
        factor_of = factor_of * one(*cut)
    return factor_of


def scatter_about(stream_key, extent, spread, limit, split=(), kind=jnp.bfloat16):
    array = jax.random.normal(stream_key, extent, jnp.float32) * spread
    if len(split) > 0:
        array = level_of(stream_key, extent, split, -0.22, 0.18) * array
    return jnp.clip(array, min=-limit, max=limit).astype(kind)


def setup_inputs(seed: int = 0) -> dict:
    arg_keys = jax.random.split(jax.random.key(seed), 13)
    sample_layer_feed = draw_sample_layer_feed(jax.random.fold_in(arg_keys[12], 71), 0)
    gain = jnp.clip(1.0 + 0.18 * jax.random.normal(arg_keys[1], (D,), jnp.float32), 0.1, 1.9)
    w_query = draw_w_query(jax.random.fold_in(arg_keys[12], 71), 0)
    w_key = scatter_about(arg_keys[3], (D, INNER), D ** -0.5, 0.1875, ((0, 4),))
    w_value = scatter_about(arg_keys[4], (D, INNER), D ** -0.5, 0.1875, ((0, 4),))
    w_out = scatter_about(arg_keys[5], (INNER, D), INNER ** -0.5, 0.25, ((1, 4),))
    readout_matrix = scatter_about(arg_keys[6], (D, VARS), D ** -0.5, 0.1875)
    target = scatter_about(arg_keys[7], (PIX, VARS), 1.0, 6.0, ((0, 8),), jnp.float32)
    pixel_weight = draw_pixel_weight(jax.random.fold_in(arg_keys[12], 71), 0)
    pix_mask = draw_pix_mask(jax.random.fold_in(arg_keys[12], 71), 0)
    neighbours = draw_neighbours(jax.random.fold_in(arg_keys[12], 71), 0)
    neighbour_mask = draw_neighbour_mask(jax.random.fold_in(arg_keys[12], 71), 0)
    return dict(sample_layer_feed=sample_layer_feed, gain=gain, w_query=w_query, w_key=w_key, w_value=w_value, w_out=w_out, readout_matrix=readout_matrix, target=target, pixel_weight=pixel_weight, pix_mask=pix_mask, neighbours=neighbours, neighbour_mask=neighbour_mask)


eps_norm = 1e-06
easing_breadth = 0.1

def rms_scaled(member_rows, gain):
    values_f = member_rows.astype(jnp.float32)
    inverse = lax.rsqrt(lax.optimization_barrier(jnp.mean(values_f * values_f, axis=-1, keepdims=True)) + eps_norm)
    return (values_f * inverse * gain.astype(jnp.float32)).astype(jnp.bfloat16)

def eased_magnitude(sample_dispersion):
    return easing_breadth * (jax.nn.softplus(sample_dispersion / easing_breadth) + jax.nn.softplus(-sample_dispersion / easing_breadth))

def reference(sample_layer_feed, gain, w_query, w_key, w_value, w_out, readout_matrix, target, pixel_weight, pix_mask, neighbours, neighbour_mask):
    sample_sequence = sample_layer_feed.shape[0]
    normed = rms_scaled(sample_layer_feed, gain)

    def project(weights):
        return lax.map(lambda present_tile_piece: jnp.dot(present_tile_piece, weights, preferred_element_type=jnp.float32).astype(jnp.bfloat16), normed)
    queries = project(w_query)
    key_rows = project(w_key)
    value_rows = project(w_value)
    key_tiles = key_rows.reshape(sample_sequence, TILES, TILE, INNER)
    value_tiles = value_rows.reshape(sample_sequence, TILES, TILE, INNER)
    query_tiles = queries.reshape(sample_sequence, TILES, TILE, INNER)
    live_tiles = pix_mask.reshape(TILES, TILE) > 0

    def tile_weights(tile):
        slots = neighbours[tile]
        live_keys = (live_tiles[slots] & (neighbour_mask[tile][:, None] > 0)).reshape(NB * TILE)
        near_keys = key_tiles[:, slots].reshape(sample_sequence, NB * TILE, HEADS, HD).astype(jnp.float32)
        query_tile = query_tiles[:, tile].reshape(sample_sequence, TILE, HEADS, HD).astype(jnp.float32)
        scores = jnp.einsum('mqhd,mkhd->mhqk', query_tile, near_keys) * HD ** (-0.5)
        scores = jnp.where(live_keys[None, None, None, :], scores, -1e+30)
        row_max = lax.optimization_barrier(jnp.max(scores, axis=-1, keepdims=True))
        expos = jnp.exp(scores - row_max)
        return ((expos / lax.optimization_barrier(jnp.sum(expos, axis=-1, keepdims=True))).astype(jnp.bfloat16), slots)

    def attend(tile):
        weights, slots = tile_weights(tile)
        near_values = value_tiles[:, slots].reshape(sample_sequence, NB * TILE, HEADS, HD).astype(jnp.float32)
        mixture = jnp.einsum('mhqk,mkhd->mqhd', weights.astype(jnp.float32), near_values)
        return mixture.reshape(sample_sequence, TILE, INNER).astype(jnp.bfloat16)
    neighbour_mixing_vector = lax.map(attend, jnp.arange(TILES, dtype=jnp.int32))
    neighbour_mixing_vector = jnp.transpose(neighbour_mixing_vector, (1, 0, 2, 3)).reshape(sample_sequence, PIX, INNER)

    def later_layers_pass(inputs):
        member_rows, mixed_rows = inputs
        projected = jnp.dot(mixed_rows, w_out, preferred_element_type=jnp.float32)
        hidden_state = (member_rows.astype(jnp.float32) + projected).astype(jnp.bfloat16)
        return jnp.dot(hidden_state, readout_matrix, preferred_element_type=jnp.float32).astype(jnp.bfloat16)
    sample_prediction = lax.map(later_layers_pass, (sample_layer_feed, neighbour_mixing_vector))
    lone_prediction = sample_prediction.astype(jnp.float32)
    observed_entries = target[None]
    matrix_vertical_vector = (pixel_weight * pix_mask.astype(jnp.float32))[None, :, None]

    def extend_sample_entries(totals, sample_ordinal):
        eased_aggregate, accrued_tangent_amount = totals
        sample_dispersion = lone_prediction - sample_ordinal.astype(jnp.float32)[None]
        return ((eased_aggregate + eased_magnitude(sample_dispersion), accrued_tangent_amount + jnp.tanh(sample_dispersion / (2.0 * easing_breadth))), None)
    blank_tile_filler = jnp.zeros_like(lone_prediction)
    (eased_aggregate, accrued_tangent_amount), discarded_yield = lax.scan(extend_sample_entries, (blank_tile_filler, blank_tile_filler), sample_prediction)
    null_discrepancy = eased_magnitude(jnp.zeros((), jnp.float32))
    penalty_term_series = matrix_vertical_vector * (eased_magnitude(lone_prediction - observed_entries) - (eased_aggregate - null_discrepancy) / (2.0 * (sample_sequence - 1)))
    loss = jnp.sum(penalty_term_series) / (sample_sequence * PIX * VARS)
    derivative_factor = 1.0 / math.sqrt(sample_sequence * PIX)
    prediction_derivative = (matrix_vertical_vector * (jnp.tanh((lone_prediction - observed_entries) / (2.0 * easing_breadth)) - accrued_tangent_amount / (sample_sequence - 1)) * derivative_factor).astype(jnp.bfloat16)
    latent_derivative = lax.map(lambda present_tile_piece: jnp.dot(present_tile_piece, readout_matrix.T, preferred_element_type=jnp.float32).astype(jnp.bfloat16), prediction_derivative)
    grad_attended = lax.map(lambda present_tile_piece: jnp.dot(present_tile_piece, w_out.T, preferred_element_type=jnp.float32).astype(jnp.bfloat16), latent_derivative)
    grad_tiles = grad_attended.reshape(sample_sequence, TILES, TILE, HEADS, HD)

    def collect(accumulated, tile):
        weights, slots = tile_weights(tile)
        grad_tile = grad_tiles[:, tile].astype(jnp.float32)
        contrib = jnp.einsum('mhqk,mqhd->mkhd', weights.astype(jnp.float32), grad_tile).reshape(sample_sequence, NB, TILE, INNER)
        return (accumulated.at[:, slots].add(contrib), None)
    start_acc = jnp.zeros((sample_sequence, TILES, TILE, INNER), jnp.float32)
    accumulated, discarded_yield = lax.scan(collect, start_acc, jnp.arange(TILES, dtype=jnp.int32))
    grad_values = accumulated.reshape(sample_sequence, PIX, INNER).astype(jnp.bfloat16)

    def add_grads(totals, inputs):
        normed_rows, value_grads, mixed_rows, hidden_grads = inputs
        value_sum, output_sum = totals
        value_sum = value_sum + jnp.dot(normed_rows.T, value_grads, preferred_element_type=jnp.float32)
        output_sum = output_sum + jnp.dot(mixed_rows.T, hidden_grads, preferred_element_type=jnp.float32)
        return ((value_sum, output_sum), None)
    start_grads = (jnp.zeros((D, INNER), jnp.float32), jnp.zeros((INNER, D), jnp.float32))
    (grad_w_value, grad_w_out), discarded_yield = lax.scan(add_grads, start_grads, (normed, grad_values, neighbour_mixing_vector, latent_derivative))
    return (loss, grad_w_out, grad_w_value)
```

```python
import functools
import math

import jax
import jax.numpy as jnp
from jax import lax
from jax.experimental import pallas as pl
from jax.experimental.pallas import tpu as pltpu
from jax.sharding import PartitionSpec as P

HEADS = 8
HD = 64
TILE = 128
NB = 9
LANES = 128
EPS = 1e-06
BREADTH = 0.1

F32 = jnp.float32
BF16 = jnp.bfloat16
VMEM = pl.BlockSpec(memory_space=pltpu.VMEM)
SMEM = pl.BlockSpec(memory_space=pltpu.SMEM)
NN = (((1,), (0,)), ((), ()))
NT = (((1,), (1,)), ((), ()))
TN = (((0,), (0,)), ((), ()))


def dot(a, b, dims=NN):
    return lax.dot_general(a, b, dims, preferred_element_type=F32)


def call(body, outs, ins, flops, name, scratch=(), vmem=32):
    specs = [SMEM if s == "s" else VMEM for s, _ in ins]
    return pl.pallas_call(
        body,
        out_shape=[jax.ShapeDtypeStruct(s, d) for s, d in outs],
        in_specs=specs,
        out_specs=[VMEM] * len(outs),
        scratch_shapes=list(scratch),
        compiler_params=pltpu.CompilerParams(vmem_limit_bytes=vmem * 2**20),
        cost_estimate=pl.CostEstimate(flops=flops, bytes_accessed=2**20, transcendentals=0),
        name=name,
    )(*[a for _, a in ins])


def xor_permute(value, axis, mask):
    size = lax.axis_size(axis)
    return lax.ppermute(value, axis, [(i, i ^ mask) for i in range(size)])


def normed_body(n_ens, dsh, x_ref, up_ref, down_ref, gain_ref, n_ref, keep_ref, send_ref, turned_ref):
    core = lax.axis_index("ens") % 2
    gain = gain_ref[...]
    for i, ref in enumerate((up_ref, x_ref, down_ref)):
        rows = ref[0].astype(F32)
        inv = lax.rsqrt(jnp.mean(rows * rows, axis=-1, keepdims=True) + EPS)
        n_ref[i * TILE : (i + 1) * TILE, :] = (rows * inv * gain).astype(BF16)
    turned_ref[...] = n_ref[...].T
    for b in range(n_ens // 2):
        mine = pl.multiple_of((2 * b + core) * dsh, dsh)
        theirs = pl.multiple_of((2 * b + 1 - core) * dsh, dsh)
        keep_ref[b * dsh : (b + 1) * dsh, :] = turned_ref[pl.ds(mine, dsh), :]
        send_ref[b * dsh : (b + 1) * dsh, :] = turned_ref[pl.ds(theirs, dsh), :]


def counts_of(nb_ref, nm_ref, position):
    counts = []
    for d in (-1, 0, 1):
        total = jnp.int32(0)
        for s in range(NB):
            hit = (nb_ref[0, s] == position + d) & (nm_ref[0, s] > 0)
            total = total + jnp.where(hit, 1, 0)
        counts.append(total.astype(F32))
    return counts


def assembled(pieces, scratch, dsh):
    me = lax.axis_index("ens")
    for j, ref in enumerate(pieces):
        start = pl.multiple_of((me ^ j) * dsh, dsh)
        scratch[pl.ds(start, dsh), :] = ref[...]
    return scratch[...]


def weights_body(n_ens, dsh, n_ref, *refs):
    q_refs, k_refs = refs[:n_ens], refs[n_ens : 2 * n_ens]
    mask_ref, nb_ref, nm_ref, w_ref, scratch = refs[2 * n_ens :]
    position = lax.axis_index("pix")
    n_pix = mask_ref.shape[0]
    counts = counts_of(nb_ref, nm_ref, position)
    lanes = []
    for i, d in enumerate((-1, 0, 1)):
        row = jnp.clip(position + d, 0, n_pix - 1)
        lanes.append(jnp.where(mask_ref[pl.ds(row, 1), :] > 0, 1.0, 0.0) * counts[i])
    times = jnp.concatenate(lanes, axis=1)
    bias = jnp.where(times > 0, 0.0, -1e30)
    queries = dot(n_ref[TILE : 2 * TILE, :], assembled(q_refs, scratch, dsh)).astype(BF16)
    keys = dot(n_ref[...], assembled(k_refs, scratch, dsh)).astype(BF16)
    lane = lax.broadcasted_iota(jnp.int32, (TILE, LANES), 1)
    for h in range(HEADS):
        cols = slice(h // 2 * LANES, (h // 2 + 1) * LANES)
        own = (lane < HD) if h % 2 == 0 else (lane >= HD)
        query = jnp.where(own, queries[:, cols], jnp.zeros((), BF16))
        scores = dot(query, keys[:, cols], NT) * HD ** (-0.5) + bias
        top = jnp.max(scores, axis=-1, keepdims=True)
        expos = jnp.exp(scores - top)
        total = jnp.sum(expos * times, axis=-1, keepdims=True)
        w_ref[h] = (expos / total).astype(BF16)


def attend_body(n_ens, dsh, n_ref, *refs):
    v_refs = refs[:n_ens]
    w_ref, nb_ref, nm_ref, att_ref, scratch = refs[n_ens:]
    counts = counts_of(nb_ref, nm_ref, lax.axis_index("pix"))
    values = dot(n_ref[...], assembled(v_refs, scratch, dsh)).astype(BF16)
    lane = lax.broadcasted_iota(jnp.int32, (TILE, LANES), 1)
    for g in range(HEADS // 2):
        cols = slice(g * LANES, (g + 1) * LANES)
        halves = []
        for h in (2 * g, 2 * g + 1):
            total = jnp.zeros((TILE, LANES), F32)
            for i in range(3):
                rows = slice(i * TILE, (i + 1) * TILE)
                total = total + counts[i] * dot(w_ref[h, :, rows], values[rows, cols])
            halves.append(total)
        att_ref[:, cols] = jnp.where(lane < HD, halves[0], halves[1]).astype(BF16)


def forecast_body(n_ens, dsh, x_ref, att_ref, read_ref, *refs):
    o_refs = refs[:n_ens]
    f_ref, scratch = refs[n_ens:]
    hidden = x_ref[0].astype(F32) + dot(att_ref[...], assembled(o_refs, scratch, dsh), NT)
    f_ref[...] = dot(hidden.astype(BF16), read_ref[...]).astype(BF16)


def sabs(a):
    mag = jnp.abs(a)
    return mag + 2.0 * BREADTH * jnp.log1p(jnp.exp(mag * (-1.0 / BREADTH)))


def backward_body(n_ens, dsh, factor, *refs):
    f_refs, o_refs = refs[:n_ens], refs[n_ens : 2 * n_ens]
    target_ref, pw_ref, mask_ref, read_ref, w_ref, nb_ref, nm_ref = refs[2 * n_ens : 2 * n_ens + 7]
    gf_ref, con_ref, loss_ref, scratch = refs[2 * n_ens + 7 :]
    position = lax.axis_index("pix")
    counts = counts_of(nb_ref, nm_ref, position)
    live = jnp.where(mask_ref[pl.ds(position, 1), :] > 0, 1.0, 0.0)
    lw = jnp.broadcast_to(pw_ref[...] * live, (LANES, TILE)).T
    target = target_ref[...]
    fc = [ref[...].astype(F32) for ref in f_refs]
    sums = [jnp.zeros((TILE, LANES), F32) for _ in range(n_ens)]
    for i in range(n_ens):
        for j in range(i + 1, n_ens):
            t = jnp.tanh((fc[i] - fc[j]) / (2.0 * BREADTH))
            sums[i] = sums[i] + t
            sums[j] = sums[j] - t
    for i in range(n_ens):
        t = jnp.tanh((fc[i] - target) / (2.0 * BREADTH))
        gf_ref[i * TILE : (i + 1) * TILE, :] = (lw * (t - sums[i] / (n_ens - 1)) * factor).astype(BF16)
    others = jnp.zeros((TILE, LANES), F32)
    for j in range(1, n_ens):
        others = others + sabs(fc[0] - fc[j])
    terms = lw * (sabs(fc[0] - target) - others / (2.0 * (n_ens - 1)))
    loss_ref[...] = jnp.full((8, LANES), jnp.sum(terms), F32)
    grad_hidden = dot(gf_ref[:TILE, :], read_ref[...], NT).astype(BF16)
    grad_att = dot(grad_hidden, assembled(o_refs, scratch, dsh)).astype(BF16)
    lane = lax.broadcasted_iota(jnp.int32, (TILE, LANES), 1)
    zero = jnp.zeros((), BF16)
    for g in range(HEADS // 2):
        cols = slice(g * LANES, (g + 1) * LANES)
        pair = grad_att[:, cols]
        both = dot(w_ref[2 * g], jnp.where(lane < HD, pair, zero), TN)
        both = both + dot(w_ref[2 * g + 1], jnp.where(lane < HD, zero, pair), TN)
        for i in range(3):
            rows = slice(i * TILE, (i + 1) * TILE)
            con_ref[rows, cols] = (both[rows] * counts[i]).astype(BF16)


def value_body(blocks, dsh, keep_ref, sib_ref, own_con, sib_con, v_ref):
    term = dot(keep_ref[...], own_con[...]) + dot(sib_ref[...], sib_con[...])
    for b in range(blocks):
        for cb in range(term.shape[1] // LANES):
            v_ref[b, cb * dsh : (cb + 1) * dsh, :] = term[
                b * dsh : (b + 1) * dsh, cb * LANES : (cb + 1) * LANES
            ]


def output_body(n_ens, dsh, gf_ref, read_ref, *refs):
    att_refs = refs[:n_ens]
    o_ref, scratch = refs[n_ens:]
    start = pl.multiple_of(lax.axis_index("ens") * dsh, dsh)
    for j in range(n_ens):
        scratch[j * TILE : (j + 1) * TILE, :] = att_refs[j][...]
    turned = dot(read_ref[pl.ds(start, dsh), :], gf_ref[...], NT).astype(BF16)
    term = dot(turned, scratch[...])
    for cb in range(term.shape[1] // LANES):
        o_ref[cb * dsh : (cb + 1) * dsh, :] = term[:, cb * LANES : (cb + 1) * LANES]


def finish_body(n_pix, dsh, *refs):
    pieces = refs[:n_pix]
    gv_ref, go_ref, scratch = refs[n_pix:]
    rows = scratch.shape[1] // n_pix
    position = lax.axis_index("pix")
    for j in range(n_pix):
        start = pl.multiple_of((position ^ j) * rows, rows)
        scratch[:, pl.ds(start, rows), :] = pieces[j][...].astype(F32)
    for cb in range(scratch.shape[1] // dsh):
        gv_ref[:, cb * LANES : (cb + 1) * LANES] = scratch[0, cb * dsh : (cb + 1) * dsh, :]
        go_ref[cb * LANES : (cb + 1) * LANES, :] = scratch[1, cb * dsh : (cb + 1) * dsh, :].T


def in_parts(total):
    first = lax.reduce_precision(total, 8, 7)
    second = lax.reduce_precision(total - first, 8, 7)
    third = total - first - second
    return jnp.stack([first, second, third]).astype(BF16)


def from_parts(parts):
    parts = parts.astype(F32)
    return parts[0] + parts[1] + parts[2]


def gathered(value, axis, bits):
    pieces = {0: value}
    for bit in bits:
        pieces.update({j ^ bit: xor_permute(piece, axis, bit) for j, piece in list(pieces.items())})
    return [pieces[j] for j in sorted(pieces)]


def at(blocks, index):
    return lax.dynamic_index_in_dim(blocks, index, 0, keepdims=False)


def part_of(split, index):
    return lax.dynamic_index_in_dim(split, index, 1, keepdims=False).reshape(-1, LANES)


def with_loss(block, total):
    rows = jnp.broadcast_to(in_parts(total)[:, None], (3, LANES))
    rows = jnp.pad(rows, ((0, 13), (0, 0)))
    return jnp.concatenate([block.reshape(-1, LANES).astype(BF16), rows], axis=0)


def split_loss(message):
    return message[:-16], from_parts(message[-16:-13, 0])


def per_device(
    sample_layer_feed,
    gain,
    w_query,
    w_key,
    w_value,
    w_out,
    readout_matrix,
    target,
    pixel_weight,
    pix_mask,
    neighbours,
    neighbour_mask,
):
    n_ens, n_pix = lax.axis_size("ens"), lax.axis_size("pix")
    dsh, inner = w_query.shape
    d_model = dsh * n_ens
    n_out = readout_matrix.shape[1]
    ens_bits = [1 << b for b in reversed(range(n_ens.bit_length() - 1))]
    e, p = lax.axis_index("ens"), lax.axis_index("pix")
    rows = sample_layer_feed.shape[1]
    assert rows == TILE and n_out == LANES

    q_parts = gathered(w_query, "ens", ens_bits)
    k_parts = gathered(w_key, "ens", ens_bits)
    up = lax.ppermute(sample_layer_feed, "pix", [(i, i + 1) for i in range(n_pix - 1)])
    down = lax.ppermute(sample_layer_feed, "pix", [(i + 1, i) for i in range(n_pix - 1)])
    v_parts = gathered(w_value, "ens", ens_bits)
    o_parts = gathered(w_out.T, "ens", ens_bits)

    mask_rows = pix_mask.reshape(n_pix, TILE)
    half = ((d_model // 2, 3 * TILE), BF16)
    normed, turned_keep, turned_send = call(
        functools.partial(normed_body, n_ens, dsh),
        [((3 * TILE, d_model), BF16), half, half],
        [("v", sample_layer_feed), ("v", up), ("v", down), ("v", gain.reshape(1, -1))],
        10**7,
        "normed",
        scratch=[pltpu.VMEM((d_model, 3 * TILE), BF16)],
    )
    turned_sib = xor_permute(turned_send, "ens", 1)

    full = pltpu.VMEM((d_model, inner), BF16)
    (weights,) = call(
        functools.partial(weights_body, n_ens, dsh),
        [((HEADS, TILE, 3 * TILE), BF16)],
        [("v", normed)]
        + [("v", a) for a in q_parts + k_parts]
        + [("v", mask_rows), ("s", neighbours), ("s", neighbour_mask)],
        2 * 10**9,
        "weights",
        scratch=[full],
    )
    (attended,) = call(
        functools.partial(attend_body, n_ens, dsh),
        [((TILE, inner), BF16)],
        [("v", normed)]
        + [("v", a) for a in v_parts]
        + [("v", weights), ("s", neighbours), ("s", neighbour_mask)],
        10**9,
        "attend",
        scratch=[full],
    )
    (forecast,) = call(
        functools.partial(forecast_body, n_ens, dsh),
        [((TILE, LANES), BF16)],
        [("v", sample_layer_feed), ("v", attended), ("v", readout_matrix)] + [("v", a) for a in o_parts],
        10**9,
        "forecast",
        scratch=[full],
    )
    forecasts = gathered(forecast, "ens", ens_bits)
    attended_all = gathered(attended, "ens", ens_bits)

    factor = 1.0 / math.sqrt(n_ens * n_pix * TILE)
    grads, contrib, loss_rows = call(
        functools.partial(backward_body, n_ens, dsh, factor),
        [((n_ens * TILE, LANES), BF16), ((3 * TILE, inner), BF16), ((8, LANES), F32)],
        [("v", a) for a in forecasts + o_parts]
        + [("v", target), ("v", pixel_weight.reshape(1, TILE)), ("v", mask_rows), ("v", readout_matrix)]
        + [("v", weights), ("s", neighbours), ("s", neighbour_mask)],
        10**9,
        "backward",
        scratch=[full],
    )
    contrib_sib = xor_permute(contrib, "ens", 1)
    blocks = n_ens // 2
    (value_term,) = call(
        functools.partial(value_body, blocks, dsh),
        [((blocks, dsh * inner // LANES, LANES), F32)],
        [("v", turned_keep), ("v", turned_sib), ("v", contrib), ("v", contrib_sib)],
        10**9,
        "value_term",
    )
    (output_term,) = call(
        functools.partial(output_body, n_ens, dsh),
        [((dsh * inner // LANES, LANES), F32)],
        [("v", grads), ("v", readout_matrix)] + [("v", a) for a in attended_all],
        10**9,
        "output_term",
        scratch=[pltpu.VMEM((n_ens * TILE, inner), BF16)],
    )

    loss = loss_rows[0, 0]
    loss = loss + xor_permute(loss.reshape(1, 1), "ens", 1)[0, 0]
    for bit in ens_bits[:-1]:
        upper = (e // bit) % 2
        halves = value_term.reshape(2, -1, LANES)
        kept = at(halves, upper)
        message = with_loss(at(halves, 1 - upper), loss)
        got, other = split_loss(xor_permute(message, "ens", bit))
        value_term = kept + got.astype(F32)
        loss = loss + other
    value_term = value_term.reshape(-1, LANES)

    n_bits = n_pix.bit_length() - 1
    groups = [[1]] + [[1 << b for b in range(s, min(s + 2, n_bits))] for s in range(1, n_bits, 2)]
    terms = [value_term, output_term]
    for group in groups:
        size = 1 << len(group)
        low = group[0]
        pos = (p // low) % size
        shape = (n_pix // (low * size), size, -1, LANES)
        split = [t.reshape(shape) for t in terms]
        kept = [part_of(s, pos) for s in split]
        losses = [None] * size
        for d in range(1, size):
            message = with_loss(jnp.concatenate([part_of(s, pos ^ d) for s in split], axis=0), loss)
            got, other = split_loss(xor_permute(message, "pix", d * low))
            got = got.astype(F32).reshape(2, -1, LANES)
            kept = [kept[0] + got[0], kept[1] + got[1]]
            losses[d] = other
        losses[0] = loss
        ordered = jnp.stack(losses)
        loss = functools.reduce(jnp.add, [at(ordered, pos ^ i) for i in range(size)])
        terms = kept
    piece = jnp.stack(terms).astype(BF16)
    pieces = {0: piece}
    for group in reversed(groups):
        stack = jnp.stack([pieces[j] for j in sorted(pieces)])
        keys = sorted(pieces)
        new = dict(pieces)
        for d in range(1, 1 << len(group)):
            got = xor_permute(stack, "pix", d * group[0])
            for i, j in enumerate(keys):
                new[j ^ (d * group[0])] = got[i]
        pieces = new
    grad_w_value, grad_w_out = call(
        functools.partial(finish_body, n_pix, dsh),
        [((dsh, inner), F32), ((inner, dsh), F32)],
        [("v", pieces[j]) for j in range(n_pix)],
        10**6,
        "finish",
        scratch=[pltpu.VMEM((2, dsh * inner // LANES, LANES), F32)],
    )
    loss = loss / (n_ens * n_pix * TILE * n_out)
    return (loss, grad_w_out, grad_w_value)


def solution(mesh):
    in_specs = (
        P("ens", "pix", None),
        P(),
        P("ens", None),
        P("ens", None),
        P("ens", None),
        P(None, "ens"),
        P(),
        P("pix", None),
        P("pix"),
        P(),
        P("pix", None),
        P("pix", None),
    )
    out_specs = (P(), P(None, "ens"), P("ens", None))
    return jax.shard_map(
        per_device, mesh=mesh, in_specs=in_specs, out_specs=out_specs, check_vma=False
    )
```

```python
import functools
import math

import jax
import jax.numpy as jnp
from jax import lax
from jax.experimental import pallas as pl
from jax.experimental.pallas import tpu as pltpu
from jax.sharding import PartitionSpec as P

HEADS = 8
HD = 64
TILE = 128
NB = 9
LANES = 128
EPS = 1e-06
BREADTH = 0.1

F32 = jnp.float32
BF16 = jnp.bfloat16
VMEM = pl.BlockSpec(memory_space=pltpu.VMEM)
SMEM = pl.BlockSpec(memory_space=pltpu.SMEM)
NN = (((1,), (0,)), ((), ()))
NT = (((1,), (1,)), ((), ()))
TN = (((0,), (0,)), ((), ()))


def dot(a, b, dims=NN):
    return lax.dot_general(a, b, dims, preferred_element_type=F32)


def call(body, outs, ins, flops, name, scratch=(), vmem=32):
    specs = [SMEM if s == "s" else VMEM for s, _ in ins]
    return pl.pallas_call(
        body,
        out_shape=[jax.ShapeDtypeStruct(s, d) for s, d in outs],
        in_specs=specs,
        out_specs=[VMEM] * len(outs),
        scratch_shapes=list(scratch),
        compiler_params=pltpu.CompilerParams(vmem_limit_bytes=vmem * 2**20),
        cost_estimate=pl.CostEstimate(flops=flops, bytes_accessed=2**20, transcendentals=0),
        name=name,
    )(*[a for _, a in ins])


def xor_permute(value, axis, mask):
    size = lax.axis_size(axis)
    return lax.ppermute(value, axis, [(i, i ^ mask) for i in range(size)])


def normed_body(n_ens, dsh, x_ref, up_ref, down_ref, gain_ref, n_ref, keep_ref, send_ref, turned_ref):
    core = lax.axis_index("ens") % 2
    gain = gain_ref[...]
    for i, ref in enumerate((up_ref, x_ref, down_ref)):
        rows = ref[0].astype(F32)
        inv = lax.rsqrt(jnp.mean(rows * rows, axis=-1, keepdims=True) + EPS)
        n_ref[i * TILE : (i + 1) * TILE, :] = (rows * inv * gain).astype(BF16)
    turned_ref[...] = n_ref[...].T
    for b in range(n_ens // 2):
        mine = pl.multiple_of((2 * b + core) * dsh, dsh)
        theirs = pl.multiple_of((2 * b + 1 - core) * dsh, dsh)
        keep_ref[b * dsh : (b + 1) * dsh, :] = turned_ref[pl.ds(mine, dsh), :]
        send_ref[b * dsh : (b + 1) * dsh, :] = turned_ref[pl.ds(theirs, dsh), :]


def counts_of(nb_ref, nm_ref, position):
    counts = []
    for d in (-1, 0, 1):
        total = jnp.int32(0)
        for s in range(NB):
            hit = (nb_ref[0, s] == position + d) & (nm_ref[0, s] > 0)
            total = total + jnp.where(hit, 1, 0)
        counts.append(total.astype(F32))
    return counts


def assembled(pieces, scratch, dsh):
    me = lax.axis_index("ens")
    for j, ref in enumerate(pieces):
        start = pl.multiple_of((me ^ j) * dsh, dsh)
        scratch[pl.ds(start, dsh), :] = ref[...]
    return scratch[...]


def weights_body(n_ens, dsh, n_ref, *refs):
    q_refs, k_refs = refs[:n_ens], refs[n_ens : 2 * n_ens]
    mask_ref, nb_ref, nm_ref, w_ref, scratch = refs[2 * n_ens :]
    position = lax.axis_index("pix")
    n_pix = mask_ref.shape[0]
    counts = counts_of(nb_ref, nm_ref, position)
    lanes = []
    for i, d in enumerate((-1, 0, 1)):
        row = jnp.clip(position + d, 0, n_pix - 1)
        lanes.append(jnp.where(mask_ref[pl.ds(row, 1), :] > 0, 1.0, 0.0) * counts[i])
    times = jnp.concatenate(lanes, axis=1)
    bias = jnp.where(times > 0, 0.0, -1e30)
    queries = dot(n_ref[TILE : 2 * TILE, :], assembled(q_refs, scratch, dsh)).astype(BF16)
    keys = dot(n_ref[...], assembled(k_refs, scratch, dsh)).astype(BF16)
    lane = lax.broadcasted_iota(jnp.int32, (TILE, LANES), 1)
    for h in range(HEADS):
        cols = slice(h // 2 * LANES, (h // 2 + 1) * LANES)
        own = (lane < HD) if h % 2 == 0 else (lane >= HD)
        query = jnp.where(own, queries[:, cols], jnp.zeros((), BF16))
        scores = dot(query, keys[:, cols], NT) * HD ** (-0.5) + bias
        top = jnp.max(scores, axis=-1, keepdims=True)
        expos = jnp.exp(scores - top)
        total = jnp.sum(expos * times, axis=-1, keepdims=True)
        w_ref[h] = (expos / total).astype(BF16)


def attend_body(n_ens, dsh, n_ref, *refs):
    v_refs = refs[:n_ens]
    w_ref, nb_ref, nm_ref, att_ref, scratch = refs[n_ens:]
    counts = counts_of(nb_ref, nm_ref, lax.axis_index("pix"))
    values = dot(n_ref[...], assembled(v_refs, scratch, dsh)).astype(BF16)
    lane = lax.broadcasted_iota(jnp.int32, (TILE, LANES), 1)
    for g in range(HEADS // 2):
        cols = slice(g * LANES, (g + 1) * LANES)
        halves = []
        for h in (2 * g, 2 * g + 1):
            total = jnp.zeros((TILE, LANES), F32)
            for i in range(3):
                rows = slice(i * TILE, (i + 1) * TILE)
                total = total + counts[i] * dot(w_ref[h, :, rows], values[rows, cols])
            halves.append(total)
        att_ref[:, cols] = jnp.where(lane < HD, halves[0], halves[1]).astype(BF16)


def forecast_body(n_ens, dsh, x_ref, att_ref, read_ref, *refs):
    o_refs = refs[:n_ens]
    f_ref, scratch = refs[n_ens:]
    hidden = x_ref[0].astype(F32) + dot(att_ref[...], assembled(o_refs, scratch, dsh), NT)
    f_ref[...] = dot(hidden.astype(BF16), read_ref[...]).astype(BF16)


def sabs(a):
    mag = jnp.abs(a)
    return mag + 2.0 * BREADTH * jnp.log1p(jnp.exp(mag * (-1.0 / BREADTH)))


def backward_body(n_ens, dsh, factor, *refs):
    f_refs, o_refs = refs[:n_ens], refs[n_ens : 2 * n_ens]
    target_ref, pw_ref, mask_ref, read_ref, w_ref, nb_ref, nm_ref = refs[2 * n_ens : 2 * n_ens + 7]
    gf_ref, con_ref, scratch = refs[2 * n_ens + 7 :]
    position = lax.axis_index("pix")
    counts = counts_of(nb_ref, nm_ref, position)
    live = jnp.where(mask_ref[pl.ds(position, 1), :] > 0, 1.0, 0.0)
    lw = jnp.broadcast_to(pw_ref[...] * live, (LANES, TILE)).T
    target = target_ref[...]
    fc = [ref[...].astype(F32) for ref in f_refs]
    sums = [jnp.zeros((TILE, LANES), F32) for _ in range(n_ens)]
    for i in range(n_ens):
        for j in range(i + 1, n_ens):
            t = jnp.tanh((fc[i] - fc[j]) / (2.0 * BREADTH))
            sums[i] = sums[i] + t
            sums[j] = sums[j] - t
    for i in range(n_ens):
        t = jnp.tanh((fc[i] - target) / (2.0 * BREADTH))
        gf_ref[i * TILE : (i + 1) * TILE, :] = (lw * (t - sums[i] / (n_ens - 1)) * factor).astype(BF16)
    others = jnp.zeros((TILE, LANES), F32)
    for j in range(1, n_ens):
        others = others + sabs(fc[0] - fc[j])
    terms = lw * (sabs(fc[0] - target) - others / (2.0 * (n_ens - 1)))
    loss = jnp.full((16, LANES), jnp.sum(terms), F32)
    for i in range(con_ref.shape[1] // LANES):
        part = loss.astype(BF16)
        con_ref[3 * TILE :, i * LANES : (i + 1) * LANES] = part
        loss = loss - part.astype(F32)
    grad_hidden = dot(gf_ref[:TILE, :], read_ref[...], NT).astype(BF16)
    grad_att = dot(grad_hidden, assembled(o_refs, scratch, dsh)).astype(BF16)
    lane = lax.broadcasted_iota(jnp.int32, (TILE, LANES), 1)
    zero = jnp.zeros((), BF16)
    for g in range(HEADS // 2):
        cols = slice(g * LANES, (g + 1) * LANES)
        pair = grad_att[:, cols]
        both = dot(w_ref[2 * g], jnp.where(lane < HD, pair, zero), TN)
        both = both + dot(w_ref[2 * g + 1], jnp.where(lane < HD, zero, pair), TN)
        for i in range(3):
            rows = slice(i * TILE, (i + 1) * TILE)
            con_ref[rows, cols] = (both[rows] * counts[i]).astype(BF16)


def value_body(blocks, dsh, keep_ref, sib_ref, own_con, sib_con, v_ref, loss_ref):
    rows = 3 * TILE
    term = dot(keep_ref[...], own_con[:rows, :]) + dot(sib_ref[...], sib_con[:rows, :])
    parts = []
    for ref in (own_con, sib_con):
        part = ref[rows:, :].astype(F32)
        parts.append(part[:, :LANES] + part[:, LANES : 2 * LANES] + part[:, 2 * LANES : 3 * LANES])
    loss_ref[...] = (parts[0] + parts[1])[:8]
    for b in range(blocks):
        for cb in range(term.shape[1] // LANES):
            v_ref[b, cb * dsh : (cb + 1) * dsh, :] = term[
                b * dsh : (b + 1) * dsh, cb * LANES : (cb + 1) * LANES
            ]


def output_body(n_ens, dsh, gf_ref, read_ref, *refs):
    att_refs = refs[:n_ens]
    o_ref, scratch = refs[n_ens:]
    start = pl.multiple_of(lax.axis_index("ens") * dsh, dsh)
    for j in range(n_ens):
        scratch[j * TILE : (j + 1) * TILE, :] = att_refs[j][...]
    turned = dot(read_ref[pl.ds(start, dsh), :], gf_ref[...], NT).astype(BF16)
    term = dot(turned, scratch[...])
    for cb in range(term.shape[1] // LANES):
        o_ref[cb * dsh : (cb + 1) * dsh, :] = term[:, cb * LANES : (cb + 1) * LANES]


def finish_body(n_pix, dsh, scale, *refs):
    pieces = refs[:n_pix]
    total_ref, gv_ref, go_ref, loss_ref, scratch = refs[n_pix:]
    loss_ref[...] = total_ref[:1, :1] * scale
    rows = scratch.shape[1] // n_pix
    position = lax.axis_index("pix")
    for j in range(n_pix):
        start = pl.multiple_of((position ^ j) * rows, rows)
        scratch[:, pl.ds(start, rows), :] = pieces[j][...].astype(F32)
    for cb in range(scratch.shape[1] // dsh):
        gv_ref[:, cb * LANES : (cb + 1) * LANES] = scratch[0, cb * dsh : (cb + 1) * dsh, :]
        go_ref[cb * LANES : (cb + 1) * LANES, :] = scratch[1, cb * dsh : (cb + 1) * dsh, :].T


def in_parts(total):
    first = lax.reduce_precision(total, 8, 7)
    second = lax.reduce_precision(total - first, 8, 7)
    third = total - first - second
    return [part.astype(BF16) for part in (first, second, third, jnp.zeros_like(total))]


def with_loss(block, total):
    return jnp.concatenate([block.reshape(-1, LANES).astype(BF16)] + in_parts(total), axis=0)


def split_loss(message):
    parts = message[-32:].astype(F32).reshape(4, 8, LANES)
    return message[:-32], parts[0] + parts[1] + parts[2]


def gathered(value, axis, bits):
    pieces = {0: value}
    for bit in bits:
        held = lax.optimization_barrier(pieces)
        pieces = held | {j ^ bit: xor_permute(piece, axis, bit) for j, piece in held.items()}
    return [pieces[j] for j in sorted(pieces)]


def at(blocks, index):
    return lax.dynamic_index_in_dim(blocks, index, 0, keepdims=False)


def part_of(split, index):
    return lax.dynamic_index_in_dim(split, index, 1, keepdims=False).reshape(-1, LANES)


def per_device(
    sample_layer_feed,
    gain,
    w_query,
    w_key,
    w_value,
    w_out,
    readout_matrix,
    target,
    pixel_weight,
    pix_mask,
    neighbours,
    neighbour_mask,
):
    n_ens, n_pix = lax.axis_size("ens"), lax.axis_size("pix")
    dsh, inner = w_query.shape
    d_model = dsh * n_ens
    n_out = readout_matrix.shape[1]
    ens_bits = [1 << b for b in reversed(range(n_ens.bit_length() - 1))]
    e, p = lax.axis_index("ens"), lax.axis_index("pix")
    rows = sample_layer_feed.shape[1]
    assert rows == TILE and n_out == LANES

    q_parts = gathered(w_query, "ens", ens_bits)
    k_parts = gathered(w_key, "ens", ens_bits)
    up = lax.ppermute(sample_layer_feed, "pix", [(i, i + 1) for i in range(n_pix - 1)])
    down = lax.ppermute(sample_layer_feed, "pix", [(i + 1, i) for i in range(n_pix - 1)])
    v_parts = gathered(w_value, "ens", ens_bits)
    o_parts = gathered(w_out.T, "ens", ens_bits)

    mask_rows = pix_mask.reshape(n_pix, TILE)
    half = ((d_model // 2, 3 * TILE), BF16)
    normed, turned_keep, turned_send = call(
        functools.partial(normed_body, n_ens, dsh),
        [((3 * TILE, d_model), BF16), half, half],
        [("v", sample_layer_feed), ("v", up), ("v", down), ("v", gain.reshape(1, -1))],
        10**7,
        "normed",
        scratch=[pltpu.VMEM((d_model, 3 * TILE), BF16)],
    )
    turned_sib = xor_permute(turned_send, "ens", 1)

    full = pltpu.VMEM((d_model, inner), BF16)
    (weights,) = call(
        functools.partial(weights_body, n_ens, dsh),
        [((HEADS, TILE, 3 * TILE), BF16)],
        [("v", normed)]
        + [("v", a) for a in q_parts + k_parts]
        + [("v", mask_rows), ("s", neighbours), ("s", neighbour_mask)],
        2 * 10**9,
        "weights",
        scratch=[full],
    )
    (attended,) = call(
        functools.partial(attend_body, n_ens, dsh),
        [((TILE, inner), BF16)],
        [("v", normed)]
        + [("v", a) for a in v_parts]
        + [("v", weights), ("s", neighbours), ("s", neighbour_mask)],
        10**9,
        "attend",
        scratch=[full],
    )
    (forecast,) = call(
        functools.partial(forecast_body, n_ens, dsh),
        [((TILE, LANES), BF16)],
        [("v", sample_layer_feed), ("v", attended), ("v", readout_matrix)] + [("v", a) for a in o_parts],
        10**9,
        "forecast",
        scratch=[full],
    )
    forecasts = gathered(forecast, "ens", ens_bits)
    attended_all = gathered(attended, "ens", ens_bits)

    factor = 1.0 / math.sqrt(n_ens * n_pix * TILE)
    grads, contrib = call(
        functools.partial(backward_body, n_ens, dsh, factor),
        [((n_ens * TILE, LANES), BF16), ((3 * TILE + 16, inner), BF16)],
        [("v", a) for a in forecasts + o_parts]
        + [("v", target), ("v", pixel_weight.reshape(1, TILE)), ("v", mask_rows), ("v", readout_matrix)]
        + [("v", weights), ("s", neighbours), ("s", neighbour_mask)],
        10**9,
        "backward",
        scratch=[full],
    )
    contrib_sib = xor_permute(contrib, "ens", 1)
    blocks = n_ens // 2
    value_term, loss = call(
        functools.partial(value_body, blocks, dsh),
        [((blocks, dsh * inner // LANES, LANES), F32), ((8, LANES), F32)],
        [("v", turned_keep), ("v", turned_sib), ("v", contrib), ("v", contrib_sib)],
        10**9,
        "value_term",
    )
    (output_term,) = call(
        functools.partial(output_body, n_ens, dsh),
        [((dsh * inner // LANES, LANES), F32)],
        [("v", grads), ("v", readout_matrix)] + [("v", a) for a in attended_all],
        10**9,
        "output_term",
        scratch=[pltpu.VMEM((n_ens * TILE, inner), BF16)],
    )

    for bit in ens_bits[:-1]:
        upper = (e // bit) % 2
        halves = value_term.reshape(2, -1, LANES)
        kept = at(halves, upper)
        message = with_loss(at(halves, 1 - upper), loss)
        got, other = split_loss(xor_permute(message, "ens", bit))
        value_term = kept + got.astype(F32)
        loss = loss + other
    value_term = value_term.reshape(-1, LANES)

    n_bits = n_pix.bit_length() - 1
    groups = [[1]] + [[1 << b for b in range(s, min(s + 2, n_bits))] for s in range(1, n_bits, 2)]

    def pieces_of(term, group):
        size = 1 << len(group)
        return term.reshape(n_pix // (group[0] * size), size, -1, LANES)

    def exchanged(messages, group):
        return [xor_permute(m, "pix", (d + 1) * group[0]) for d, m in enumerate(messages)]

    split = pieces_of(output_term, groups[0])
    got = exchanged([part_of(split, 1 - p % 2).astype(BF16)], groups[0])[0]
    output_term = part_of(split, p % 2) + got.astype(F32)
    for group in groups:
        size, pos = 1 << len(group), (p // group[0]) % (1 << len(group))
        moving = [value_term] if group == groups[0] else [value_term, output_term]
        split = [pieces_of(t, group) for t in moving]
        messages = [
            with_loss(jnp.concatenate([part_of(s, pos ^ d) for s in split]), loss) for d in range(1, size)
        ]
        received = [split_loss(m) for m in exchanged(messages, group)]
        kept = [part_of(s, pos) for s in split]
        for block, _ in received:
            block = block.astype(F32).reshape(len(kept), -1, LANES)
            kept = [k + block[i] for i, k in enumerate(kept)]
        value_term = kept[0]
        output_term = kept[1] if len(kept) > 1 else output_term
        losses = jnp.stack([loss] + [other for _, other in received])
        loss = functools.reduce(jnp.add, [at(losses, pos ^ i) for i in range(size)])
    terms = [value_term, output_term]
    piece = jnp.stack(terms).astype(BF16)
    pieces = {0: piece}
    for group in reversed(groups):
        stack = jnp.stack([pieces[j] for j in sorted(pieces)])
        keys = sorted(pieces)
        new = dict(pieces)
        for d in range(1, 1 << len(group)):
            got = xor_permute(stack, "pix", d * group[0])
            for i, j in enumerate(keys):
                new[j ^ (d * group[0])] = got[i]
        pieces = new
    scale = 1.0 / (n_ens * n_pix * TILE * n_out)
    grad_w_value, grad_w_out, loss = call(
        functools.partial(finish_body, n_pix, dsh, scale),
        [((dsh, inner), F32), ((inner, dsh), F32), ((1, 1), F32)],
        [("v", pieces[j]) for j in range(n_pix)] + [("v", loss)],
        10**6,
        "finish",
        scratch=[pltpu.VMEM((2, dsh * inner // LANES, LANES), F32)],
    )
    return (loss.reshape(()), grad_w_out, grad_w_value)


def solution(mesh):
    in_specs = (
        P("ens", "pix", None),
        P(),
        P("ens", None),
        P("ens", None),
        P("ens", None),
        P(None, "ens"),
        P(),
        P("pix", None),
        P("pix"),
        P(),
        P("pix", None),
        P("pix", None),
    )
    out_specs = (P(), P(None, "ens"), P("ens", None))
    return jax.shard_map(
        per_device, mesh=mesh, in_specs=in_specs, out_specs=out_specs, check_vma=False
    )
```

```python
import functools
import math

import jax
import jax.numpy as jnp
from jax import lax
from jax.experimental import pallas as pl
from jax.experimental.pallas import tpu as pltpu
from jax.sharding import PartitionSpec as P

HEADS = 8
HD = 64
TILE = 128
NB = 9
LANES = 128
EPS = 1e-06
BREADTH = 0.1

F32 = jnp.float32
BF16 = jnp.bfloat16
VMEM = pl.BlockSpec(memory_space=pltpu.VMEM)
SMEM = pl.BlockSpec(memory_space=pltpu.SMEM)
NN = (((1,), (0,)), ((), ()))
NT = (((1,), (1,)), ((), ()))
TN = (((0,), (0,)), ((), ()))


def dot(a, b, dims=NN):
    return lax.dot_general(a, b, dims, preferred_element_type=F32)


def call(body, outs, ins, flops, name, scratch=(), vmem=32):
    specs = [SMEM if s == "s" else VMEM for s, _ in ins]
    return pl.pallas_call(
        body,
        out_shape=[jax.ShapeDtypeStruct(s, d) for s, d in outs],
        in_specs=specs,
        out_specs=[VMEM] * len(outs),
        scratch_shapes=list(scratch),
        compiler_params=pltpu.CompilerParams(vmem_limit_bytes=vmem * 2**20),
        cost_estimate=pl.CostEstimate(flops=flops, bytes_accessed=2**20, transcendentals=0),
        name=name,
    )(*[a for _, a in ins])


def xor_permute(value, axis, mask):
    size = lax.axis_size(axis)
    return lax.ppermute(value, axis, [(i, i ^ mask) for i in range(size)])


def normed_body(n_ens, dsh, x_ref, up_ref, down_ref, gain_ref, n_ref, keep_ref, send_ref, turned_ref):
    core = lax.axis_index("ens") % 2
    gain = gain_ref[...]
    for i, ref in enumerate((up_ref, x_ref, down_ref)):
        rows = ref[0].astype(F32)
        inv = lax.rsqrt(jnp.mean(rows * rows, axis=-1, keepdims=True) + EPS)
        n_ref[i * TILE : (i + 1) * TILE, :] = (rows * inv * gain).astype(BF16)
    turned_ref[...] = n_ref[...].T
    for b in range(n_ens // 2):
        mine = pl.multiple_of((2 * b + core) * dsh, dsh)
        theirs = pl.multiple_of((2 * b + 1 - core) * dsh, dsh)
        keep_ref[b * dsh : (b + 1) * dsh, :] = turned_ref[pl.ds(mine, dsh), :]
        send_ref[b * dsh : (b + 1) * dsh, :] = turned_ref[pl.ds(theirs, dsh), :]


def counts_of(nb_ref, nm_ref, position):
    counts = []
    for d in (-1, 0, 1):
        total = jnp.int32(0)
        for s in range(NB):
            hit = (nb_ref[0, s] == position + d) & (nm_ref[0, s] > 0)
            total = total + jnp.where(hit, 1, 0)
        counts.append(total.astype(F32))
    return counts


def assembled(refs, layout, scratch, dsh):
    me = lax.axis_index("ens")
    for which, first, j in layout:
        start = pl.multiple_of((me ^ j) * dsh, dsh)
        scratch[pl.ds(start, dsh), :] = refs[which][first : first + dsh, :]
    return scratch[...]


def weights_body(q_layout, k_layout, dsh, n_ref, mask_ref, nb_ref, nm_ref, *refs):
    pieces, (w_ref, scratch) = refs[:-2], refs[-2:]
    position = lax.axis_index("pix")
    n_pix = mask_ref.shape[0]
    counts = counts_of(nb_ref, nm_ref, position)
    lanes = []
    for i, d in enumerate((-1, 0, 1)):
        row = jnp.clip(position + d, 0, n_pix - 1)
        lanes.append(jnp.where(mask_ref[pl.ds(row, 1), :] > 0, 1.0, 0.0) * counts[i])
    times = jnp.concatenate(lanes, axis=1)
    bias = jnp.where(times > 0, 0.0, -1e30)
    queries = dot(n_ref[TILE : 2 * TILE, :], assembled(pieces, q_layout, scratch, dsh)).astype(BF16)
    keys = dot(n_ref[...], assembled(pieces, k_layout, scratch, dsh)).astype(BF16)
    lane = lax.broadcasted_iota(jnp.int32, (TILE, LANES), 1)
    for h in range(HEADS):
        cols = slice(h // 2 * LANES, (h // 2 + 1) * LANES)
        own = (lane < HD) if h % 2 == 0 else (lane >= HD)
        query = jnp.where(own, queries[:, cols], jnp.zeros((), BF16))
        scores = dot(query, keys[:, cols], NT) * HD ** (-0.5) + bias
        top = jnp.max(scores, axis=-1, keepdims=True)
        expos = jnp.exp(scores - top)
        total = jnp.sum(expos * times, axis=-1, keepdims=True)
        w_ref[h] = (expos / total).astype(BF16)


def attend_body(layout, dsh, n_ref, w_ref, nb_ref, nm_ref, *refs):
    pieces, (att_ref, scratch) = refs[:-2], refs[-2:]
    counts = counts_of(nb_ref, nm_ref, lax.axis_index("pix"))
    values = dot(n_ref[...], assembled(pieces, layout, scratch, dsh)).astype(BF16)
    lane = lax.broadcasted_iota(jnp.int32, (TILE, LANES), 1)
    for g in range(HEADS // 2):
        cols = slice(g * LANES, (g + 1) * LANES)
        halves = []
        for h in (2 * g, 2 * g + 1):
            total = jnp.zeros((TILE, LANES), F32)
            for i in range(3):
                rows = slice(i * TILE, (i + 1) * TILE)
                total = total + counts[i] * dot(w_ref[h, :, rows], values[rows, cols])
            halves.append(total)
        att_ref[:, cols] = jnp.where(lane < HD, halves[0], halves[1]).astype(BF16)


def forecast_body(layout, dsh, x_ref, att_ref, read_ref, *refs):
    pieces, (f_ref, wo_ref) = refs[:-2], refs[-2:]
    hidden = x_ref[0].astype(F32) + dot(att_ref[...], assembled(pieces, layout, wo_ref, dsh), NT)
    f_ref[...] = dot(hidden.astype(BF16), read_ref[...]).astype(BF16)


def sabs(a):
    mag = jnp.abs(a)
    return mag + 2.0 * BREADTH * jnp.log1p(jnp.exp(mag * (-1.0 / BREADTH)))


def backward_body(n_ens, factor, *refs):
    f_refs = refs[:n_ens]
    wo_ref, target_ref, pw_ref, mask_ref, read_ref, w_ref, nb_ref, nm_ref, gf_ref, con_ref = refs[n_ens:]
    position = lax.axis_index("pix")
    counts = counts_of(nb_ref, nm_ref, position)
    live = jnp.where(mask_ref[pl.ds(position, 1), :] > 0, 1.0, 0.0)
    lw = jnp.broadcast_to(pw_ref[...] * live, (LANES, TILE)).T
    target = target_ref[...]
    fc = [ref[...].astype(F32) for ref in f_refs]
    sums = [jnp.zeros((TILE, LANES), F32) for _ in range(n_ens)]
    for i in range(n_ens):
        for j in range(i + 1, n_ens):
            t = jnp.tanh((fc[i] - fc[j]) / (2.0 * BREADTH))
            sums[i] = sums[i] + t
            sums[j] = sums[j] - t
    for i in range(n_ens):
        t = jnp.tanh((fc[i] - target) / (2.0 * BREADTH))
        gf_ref[i * TILE : (i + 1) * TILE, :] = (lw * (t - sums[i] / (n_ens - 1)) * factor).astype(BF16)
    others = jnp.zeros((TILE, LANES), F32)
    for j in range(1, n_ens):
        others = others + sabs(fc[0] - fc[j])
    terms = lw * (sabs(fc[0] - target) - others / (2.0 * (n_ens - 1)))
    loss = jnp.full((16, LANES), jnp.sum(terms), F32)
    for i in range(con_ref.shape[1] // LANES):
        part = loss.astype(BF16)
        con_ref[3 * TILE :, i * LANES : (i + 1) * LANES] = part
        loss = loss - part.astype(F32)
    grad_hidden = dot(gf_ref[:TILE, :], read_ref[...], NT).astype(BF16)
    grad_att = dot(grad_hidden, wo_ref[...]).astype(BF16)
    lane = lax.broadcasted_iota(jnp.int32, (TILE, LANES), 1)
    zero = jnp.zeros((), BF16)
    for g in range(HEADS // 2):
        cols = slice(g * LANES, (g + 1) * LANES)
        pair = grad_att[:, cols]
        both = dot(w_ref[2 * g], jnp.where(lane < HD, pair, zero), TN)
        both = both + dot(w_ref[2 * g + 1], jnp.where(lane < HD, zero, pair), TN)
        for i in range(3):
            rows = slice(i * TILE, (i + 1) * TILE)
            con_ref[rows, cols] = (both[rows] * counts[i]).astype(BF16)


def value_body(blocks, dsh, keep_ref, sib_ref, own_con, sib_con, v_ref, loss_ref):
    rows = 3 * TILE
    term = dot(keep_ref[...], own_con[:rows, :]) + dot(sib_ref[...], sib_con[:rows, :])
    parts = []
    for ref in (own_con, sib_con):
        part = ref[rows:, :].astype(F32)
        parts.append(part[:, :LANES] + part[:, LANES : 2 * LANES] + part[:, 2 * LANES : 3 * LANES])
    loss_ref[...] = (parts[0] + parts[1])[:8]
    for b in range(blocks):
        for cb in range(term.shape[1] // LANES):
            v_ref[b, cb * dsh : (cb + 1) * dsh, :] = term[
                b * dsh : (b + 1) * dsh, cb * LANES : (cb + 1) * LANES
            ]


def output_body(n_ens, dsh, gf_ref, read_ref, *refs):
    att_refs = refs[:n_ens]
    o_ref, scratch = refs[n_ens:]
    start = pl.multiple_of(lax.axis_index("ens") * dsh, dsh)
    for j in range(n_ens):
        scratch[j * TILE : (j + 1) * TILE, :] = att_refs[j][...]
    turned = dot(read_ref[pl.ds(start, dsh), :], gf_ref[...], NT).astype(BF16)
    term = dot(turned, scratch[...])
    for cb in range(term.shape[1] // LANES):
        o_ref[cb * dsh : (cb + 1) * dsh, :] = term[:, cb * LANES : (cb + 1) * LANES]


def finish_body(n_pix, dsh, scale, *refs):
    pieces = refs[:n_pix]
    total_ref, gv_ref, go_ref, loss_ref, scratch = refs[n_pix:]
    loss_ref[...] = total_ref[:1, :1] * scale
    rows = scratch.shape[1] // n_pix
    position = lax.axis_index("pix")
    for j in range(n_pix):
        start = pl.multiple_of((position ^ j) * rows, rows)
        scratch[:, pl.ds(start, rows), :] = pieces[j][...].astype(F32)
    for cb in range(scratch.shape[1] // dsh):
        gv_ref[:, cb * LANES : (cb + 1) * LANES] = scratch[0, cb * dsh : (cb + 1) * dsh, :]
        go_ref[cb * LANES : (cb + 1) * LANES, :] = scratch[1, cb * dsh : (cb + 1) * dsh, :].T


def in_parts(total):
    first = lax.reduce_precision(total, 8, 7)
    second = lax.reduce_precision(total - first, 8, 7)
    third = total - first - second
    return [part.astype(BF16) for part in (first, second, third, jnp.zeros_like(total))]


def with_loss(block, total):
    return jnp.concatenate([block.reshape(-1, LANES).astype(BF16)] + in_parts(total), axis=0)


def split_loss(message):
    parts = message[-32:].astype(F32).reshape(4, 8, LANES)
    return message[:-32], parts[0] + parts[1] + parts[2]


def gathered(value, axis, bits):
    pieces = {0: value}
    for bit in bits:
        held = lax.optimization_barrier(pieces)
        pieces = held | {j ^ bit: xor_permute(piece, axis, bit) for j, piece in held.items()}
    return pieces


def in_order(pieces):
    return [pieces[j] for j in sorted(pieces)]


def joined(arrays):
    return arrays[0] if len(arrays) == 1 else jnp.concatenate(arrays)


def both_cores(pieces):
    held = lax.optimization_barrier(pieces)
    return in_order(held | {j ^ 1: xor_permute(piece, "ens", 1) for j, piece in held.items()})


def at(blocks, index):
    return lax.dynamic_index_in_dim(blocks, index, 0, keepdims=False)


def part_of(split, index):
    return lax.dynamic_index_in_dim(split, index, 1, keepdims=False).reshape(-1, LANES)


def per_device(
    sample_layer_feed,
    gain,
    w_query,
    w_key,
    w_value,
    w_out,
    readout_matrix,
    target,
    pixel_weight,
    pix_mask,
    neighbours,
    neighbour_mask,
):
    n_ens, n_pix = lax.axis_size("ens"), lax.axis_size("pix")
    dsh, inner = w_query.shape
    d_model = dsh * n_ens
    n_out = readout_matrix.shape[1]
    ens_bits = [1 << b for b in reversed(range(n_ens.bit_length() - 1))]
    e, p = lax.axis_index("ens"), lax.axis_index("pix")
    rows = sample_layer_feed.shape[1]
    assert rows == TILE and n_out == LANES

    far = ens_bits[:-1]
    w_out_t = w_out.T
    qkv = jnp.concatenate([w_query, w_key, w_value])
    qkv_far = gathered(qkv, "ens", far)
    up = lax.ppermute(sample_layer_feed, "pix", [(i, i + 1) for i in range(n_pix - 1)])
    down = lax.ppermute(sample_layer_feed, "pix", [(i + 1, i) for i in range(n_pix - 1)])
    qkv_near = xor_permute(qkv, "ens", 1)
    o_near = xor_permute(w_out_t, "ens", 1)
    o_far = gathered(w_out_t, "ens", far)
    up, down, qkv_near, o_near, qkv_far = lax.optimization_barrier((up, down, qkv_near, o_near, qkv_far))
    shards = sorted(j for j in qkv_far if j)
    qkv_far = joined([qkv_far[j] for j in shards])
    qkv_cross = xor_permute(qkv_far, "ens", 1)

    def shard_layout(width, first):
        table = [(0, first, 0), (1, first, 1)]
        for i, j in enumerate(shards):
            table += [(2, i * width * dsh + first, j), (3, i * width * dsh + first, j ^ 1)]
        return table

    q_layout, k_layout, v_layout = (shard_layout(3, i * dsh) for i in range(3))
    o_layout = shard_layout(1, 0)
    qkv_parts = [("v", a) for a in (qkv, qkv_near, qkv_far, qkv_cross)]

    mask_rows = pix_mask.reshape(n_pix, TILE)
    half = ((d_model // 2, 3 * TILE), BF16)
    normed, turned_keep, turned_send = call(
        functools.partial(normed_body, n_ens, dsh),
        [((3 * TILE, d_model), BF16), half, half],
        [("v", sample_layer_feed), ("v", up), ("v", down), ("v", gain.reshape(1, -1))],
        10**7,
        "normed",
        scratch=[pltpu.VMEM((d_model, 3 * TILE), BF16)],
    )

    full = pltpu.VMEM((d_model, inner), BF16)
    (weights,) = call(
        functools.partial(weights_body, q_layout, k_layout, dsh),
        [((HEADS, TILE, 3 * TILE), BF16)],
        [("v", normed), ("v", mask_rows), ("s", neighbours), ("s", neighbour_mask)]
        + qkv_parts,
        10**9,
        "weights",
        scratch=[full],
    )
    weights, o_far, turned_send = lax.optimization_barrier((weights, o_far, turned_send))
    o_far = joined([o_far[j] for j in shards])
    o_cross = xor_permute(o_far, "ens", 1)
    turned_sib = xor_permute(turned_send, "ens", 1)
    (attended,) = call(
        functools.partial(attend_body, v_layout, dsh),
        [((TILE, inner), BF16)],
        [("v", normed), ("v", weights), ("s", neighbours), ("s", neighbour_mask)]
        + qkv_parts,
        10**9,
        "attend",
        scratch=[full],
    )
    forecast, w_out_full = call(
        functools.partial(forecast_body, o_layout, dsh),
        [((TILE, LANES), BF16), ((d_model, inner), BF16)],
        [("v", sample_layer_feed), ("v", attended), ("v", readout_matrix)]
        + [("v", a) for a in (w_out_t, o_near, o_far, o_cross)],
        10**9,
        "forecast",
    )
    forecasts = in_order(gathered(forecast, "ens", ens_bits))
    forecast, attended = lax.optimization_barrier((forecast, attended))
    attended_near = gathered(attended, "ens", far)

    factor = 1.0 / math.sqrt(n_ens * n_pix * TILE)
    grads, contrib = call(
        functools.partial(backward_body, n_ens, factor),
        [((n_ens * TILE, LANES), BF16), ((3 * TILE + 16, inner), BF16)],
        [("v", a) for a in forecasts + [w_out_full]]
        + [("v", target), ("v", pixel_weight.reshape(1, TILE)), ("v", mask_rows), ("v", readout_matrix)]
        + [("v", weights), ("s", neighbours), ("s", neighbour_mask)],
        10**9,
        "backward",
    )
    contrib, attended_near = lax.optimization_barrier((contrib, attended_near))
    contrib_sib = xor_permute(contrib, "ens", 1)
    attended_all = both_cores(attended_near)
    blocks = n_ens // 2
    value_term, loss = call(
        functools.partial(value_body, blocks, dsh),
        [((blocks, dsh * inner // LANES, LANES), F32), ((8, LANES), F32)],
        [("v", turned_keep), ("v", turned_sib), ("v", contrib), ("v", contrib_sib)],
        10**9,
        "value_term",
    )
    value_term, loss, grads = lax.optimization_barrier((value_term, loss, grads))
    (output_term,) = call(
        functools.partial(output_body, n_ens, dsh),
        [((dsh * inner // LANES, LANES), F32)],
        [("v", grads), ("v", readout_matrix)] + [("v", a) for a in attended_all],
        10**9,
        "output_term",
        scratch=[pltpu.VMEM((n_ens * TILE, inner), BF16)],
    )

    for bit in far[:-1]:
        upper = (e // bit) % 2
        halves = value_term.reshape(2, -1, LANES)
        got, other = split_loss(xor_permute(with_loss(at(halves, 1 - upper), loss), "ens", bit))
        value_term = at(halves, upper) + got.astype(F32)
        loss = loss + other

    n_bits = n_pix.bit_length() - 1
    groups = [[1]] + [[1 << b for b in range(s, min(s + 2, n_bits))] for s in range(1, n_bits, 2)]

    def pieces_of(term, group):
        size = 1 << len(group)
        return term.reshape(n_pix // (group[0] * size), size, -1, LANES)

    def exchanged(messages, group):
        return [xor_permute(m, "pix", (d + 1) * group[0]) for d, m in enumerate(messages)]

    split = pieces_of(output_term, groups[0])
    got = exchanged([part_of(split, 1 - p % 2).astype(BF16)], groups[0])[0]
    output_term = part_of(split, p % 2) + got.astype(F32)
    upper, low = (e // far[-1]) % 2, p % 2
    quarters = [pieces_of(h, groups[0]) for h in value_term.reshape(2, -1, LANES)]
    quarters = jnp.stack([part_of(q, i) for q in quarters for i in range(2)])
    pos = 2 * upper + low
    received = []
    for d in (2, 1, 3):
        pairs = [
            (i * n_pix + k, (i ^ (far[-1] * (d // 2))) * n_pix + (k ^ (d % 2)))
            for i in range(n_ens)
            for k in range(n_pix)
        ]
        message = with_loss(at(quarters, pos ^ d), loss)
        received.append((d, split_loss(lax.ppermute(message, ("ens", "pix"), pairs))))
    value_term = at(quarters, pos)
    losses = {0: loss}
    for d, (block, other) in received:
        value_term = value_term + block.astype(F32)
        losses[d] = other
    losses = jnp.stack([losses[d] for d in range(4)])
    loss = functools.reduce(jnp.add, [at(losses, pos ^ i) for i in range(4)])

    for group in groups[1:]:
        size, pos = 1 << len(group), (p // group[0]) % (1 << len(group))
        split = [pieces_of(t, group) for t in (value_term, output_term)]
        messages = [
            with_loss(jnp.concatenate([part_of(s, pos ^ d) for s in split]), loss) for d in range(1, size)
        ]
        received = [split_loss(m) for m in exchanged(messages, group)]
        kept = [part_of(s, pos) for s in split]
        for block, _ in received:
            block = block.astype(F32).reshape(2, -1, LANES)
            kept = [k + block[i] for i, k in enumerate(kept)]
        value_term, output_term = kept
        losses = jnp.stack([loss] + [other for _, other in received])
        loss = functools.reduce(jnp.add, [at(losses, pos ^ i) for i in range(size)])
    terms = [value_term, output_term]
    piece = jnp.stack(terms).astype(BF16)
    pieces = {0: piece}
    pair = {1: xor_permute(piece, "pix", 1)}
    for group in reversed(groups[1:]):
        keys = sorted(pieces)
        stack = jnp.stack([pieces[j] for j in keys])
        new = {d: xor_permute(stack, "pix", d * group[0]) for d in range(1, 1 << len(group))}
        for i, j in enumerate(keys):
            pieces.update({j ^ (d * group[0]): got[i] for d, got in new.items()})
    later = [j for j in sorted(pieces) if j]
    for batch in (later[: len(later) // 3], later[len(later) // 3 :]):
        got = xor_permute(jnp.stack([pieces[j] for j in batch]), "pix", 1)
        pair.update({j ^ 1: got[i] for i, j in enumerate(batch)})
    pieces.update(pair)
    scale = 1.0 / (n_ens * n_pix * TILE * n_out)
    grad_w_value, grad_w_out, loss = call(
        functools.partial(finish_body, n_pix, dsh, scale),
        [((dsh, inner), F32), ((inner, dsh), F32), ((1, 1), F32)],
        [("v", pieces[j]) for j in range(n_pix)] + [("v", loss)],
        10**6,
        "finish",
        scratch=[pltpu.VMEM((2, dsh * inner // LANES, LANES), F32)],
    )
    return (loss.reshape(()), grad_w_out, grad_w_value)


def solution(mesh):
    in_specs = (
        P("ens", "pix", None),
        P(),
        P("ens", None),
        P("ens", None),
        P("ens", None),
        P(None, "ens"),
        P(),
        P("pix", None),
        P("pix"),
        P(),
        P("pix", None),
        P("pix", None),
    )
    out_specs = (P(), P(None, "ens"), P("ens", None))
    return jax.shard_map(
        per_device, mesh=mesh, in_specs=in_specs, out_specs=out_specs, check_vma=False
    )
```

```python
import functools
import math

import jax
import jax.numpy as jnp
from jax import lax
from jax.experimental import pallas as pl
from jax.experimental.pallas import tpu as pltpu
from jax.sharding import PartitionSpec as P

HEADS = 8
HD = 64
TILE = 128
NB = 9
LANES = 128
EPS = 1e-06
BREADTH = 0.1

F32 = jnp.float32
BF16 = jnp.bfloat16
VMEM = pl.BlockSpec(memory_space=pltpu.VMEM)
SMEM = pl.BlockSpec(memory_space=pltpu.SMEM)
NN = (((1,), (0,)), ((), ()))
NT = (((1,), (1,)), ((), ()))
TN = (((0,), (0,)), ((), ()))


def dot(a, b, dims=NN):
    return lax.dot_general(a, b, dims, preferred_element_type=F32)


def call(body, outs, ins, flops, name, scratch=(), vmem=32):
    specs = [SMEM if s == "s" else VMEM for s, _ in ins]
    return pl.pallas_call(
        body,
        out_shape=[jax.ShapeDtypeStruct(s, d) for s, d in outs],
        in_specs=specs,
        out_specs=[VMEM] * len(outs),
        scratch_shapes=list(scratch),
        compiler_params=pltpu.CompilerParams(vmem_limit_bytes=vmem * 2**20),
        cost_estimate=pl.CostEstimate(flops=flops, bytes_accessed=2**20, transcendentals=0),
        name=name,
    )(*[a for _, a in ins])


def xor_permute(value, axis, mask):
    size = lax.axis_size(axis)
    return lax.ppermute(value, axis, [(i, i ^ mask) for i in range(size)])


def normed_body(n_ens, dsh, x_ref, up_ref, down_ref, gain_ref, n_ref, keep_ref, send_ref, turned_ref):
    core = lax.axis_index("ens") % 2
    gain = gain_ref[...]
    for i, ref in enumerate((up_ref, x_ref, down_ref)):
        rows = ref[0].astype(F32)
        inv = lax.rsqrt(jnp.mean(rows * rows, axis=-1, keepdims=True) + EPS)
        n_ref[i * TILE : (i + 1) * TILE, :] = (rows * inv * gain).astype(BF16)
    turned_ref[...] = n_ref[...].T
    for b in range(n_ens // 2):
        mine = pl.multiple_of((2 * b + core) * dsh, dsh)
        theirs = pl.multiple_of((2 * b + 1 - core) * dsh, dsh)
        keep_ref[b * dsh : (b + 1) * dsh, :] = turned_ref[pl.ds(mine, dsh), :]
        send_ref[b * dsh : (b + 1) * dsh, :] = turned_ref[pl.ds(theirs, dsh), :]


def counts_of(nb_ref, nm_ref, position):
    counts = []
    for d in (-1, 0, 1):
        total = jnp.int32(0)
        for s in range(NB):
            hit = (nb_ref[0, s] == position + d) & (nm_ref[0, s] > 0)
            total = total + jnp.where(hit, 1, 0)
        counts.append(total.astype(F32))
    return counts


def assembled(refs, layout, scratch, dsh):
    me, side = lax.axis_index("ens"), (lax.axis_index("pix") // 2) % 2
    for which, first, rows, j, place in layout:
        offset = place * rows if place < 2 else (side ^ (place - 2)) * rows
        start = pl.multiple_of((me ^ j) * dsh + offset, rows)
        scratch[pl.ds(start, rows), :] = refs[which][first : first + rows, :]
    return scratch[...]


def weights_body(q_layout, k_layout, dsh, n_ref, mask_ref, nb_ref, nm_ref, *refs):
    pieces, (w_ref, scratch) = refs[:-2], refs[-2:]
    position = lax.axis_index("pix")
    n_pix = mask_ref.shape[0]
    counts = counts_of(nb_ref, nm_ref, position)
    lanes = []
    for i, d in enumerate((-1, 0, 1)):
        row = jnp.clip(position + d, 0, n_pix - 1)
        lanes.append(jnp.where(mask_ref[pl.ds(row, 1), :] > 0, 1.0, 0.0) * counts[i])
    times = jnp.concatenate(lanes, axis=1)
    bias = jnp.where(times > 0, 0.0, -1e30)
    queries = dot(n_ref[TILE : 2 * TILE, :], assembled(pieces, q_layout, scratch, dsh)).astype(BF16)
    keys = dot(n_ref[...], assembled(pieces, k_layout, scratch, dsh)).astype(BF16)
    lane = lax.broadcasted_iota(jnp.int32, (TILE, LANES), 1)
    for h in range(HEADS):
        cols = slice(h // 2 * LANES, (h // 2 + 1) * LANES)
        own = (lane < HD) if h % 2 == 0 else (lane >= HD)
        query = jnp.where(own, queries[:, cols], jnp.zeros((), BF16))
        scores = dot(query, keys[:, cols], NT) * HD ** (-0.5) + bias
        top = jnp.max(scores, axis=-1, keepdims=True)
        expos = jnp.exp(scores - top)
        total = jnp.sum(expos * times, axis=-1, keepdims=True)
        w_ref[h] = (expos / total).astype(BF16)


def attend_body(layout, dsh, n_ref, w_ref, nb_ref, nm_ref, *refs):
    pieces, (att_ref, scratch) = refs[:-2], refs[-2:]
    counts = counts_of(nb_ref, nm_ref, lax.axis_index("pix"))
    values = dot(n_ref[...], assembled(pieces, layout, scratch, dsh)).astype(BF16)
    lane = lax.broadcasted_iota(jnp.int32, (TILE, LANES), 1)
    for g in range(HEADS // 2):
        cols = slice(g * LANES, (g + 1) * LANES)
        halves = []
        for h in (2 * g, 2 * g + 1):
            total = jnp.zeros((TILE, LANES), F32)
            for i in range(3):
                rows = slice(i * TILE, (i + 1) * TILE)
                total = total + counts[i] * dot(w_ref[h, :, rows], values[rows, cols])
            halves.append(total)
        att_ref[:, cols] = jnp.where(lane < HD, halves[0], halves[1]).astype(BF16)


def forecast_body(layout, dsh, x_ref, att_ref, read_ref, *refs):
    pieces, (f_ref, wo_ref) = refs[:-2], refs[-2:]
    hidden = x_ref[0].astype(F32) + dot(att_ref[...], assembled(pieces, layout, wo_ref, dsh), NT)
    f_ref[...] = dot(hidden.astype(BF16), read_ref[...]).astype(BF16)


def sabs(a):
    mag = jnp.abs(a)
    return mag + 2.0 * BREADTH * jnp.log1p(jnp.exp(mag * (-1.0 / BREADTH)))


def backward_body(n_ens, factor, *refs):
    f_refs = refs[:n_ens]
    wo_ref, target_ref, pw_ref, mask_ref, read_ref, w_ref, nb_ref, nm_ref, gf_ref, con_ref = refs[n_ens:]
    position = lax.axis_index("pix")
    counts = counts_of(nb_ref, nm_ref, position)
    live = jnp.where(mask_ref[pl.ds(position, 1), :] > 0, 1.0, 0.0)
    lw = jnp.broadcast_to(pw_ref[...] * live, (LANES, TILE)).T
    target = target_ref[...]
    fc = [ref[...].astype(F32) for ref in f_refs]
    sums = [jnp.zeros((TILE, LANES), F32) for _ in range(n_ens)]
    for i in range(n_ens):
        for j in range(i + 1, n_ens):
            t = jnp.tanh((fc[i] - fc[j]) / (2.0 * BREADTH))
            sums[i] = sums[i] + t
            sums[j] = sums[j] - t
    for i in range(n_ens):
        t = jnp.tanh((fc[i] - target) / (2.0 * BREADTH))
        gf_ref[i * TILE : (i + 1) * TILE, :] = (lw * (t - sums[i] / (n_ens - 1)) * factor).astype(BF16)
    others = jnp.zeros((TILE, LANES), F32)
    for j in range(1, n_ens):
        others = others + sabs(fc[0] - fc[j])
    terms = lw * (sabs(fc[0] - target) - others / (2.0 * (n_ens - 1)))
    loss = jnp.full((16, LANES), jnp.sum(terms), F32)
    for i in range(con_ref.shape[1] // LANES):
        part = loss.astype(BF16)
        con_ref[3 * TILE :, i * LANES : (i + 1) * LANES] = part
        loss = loss - part.astype(F32)
    grad_hidden = dot(gf_ref[:TILE, :], read_ref[...], NT).astype(BF16)
    grad_att = dot(grad_hidden, wo_ref[...]).astype(BF16)
    lane = lax.broadcasted_iota(jnp.int32, (TILE, LANES), 1)
    zero = jnp.zeros((), BF16)
    for g in range(HEADS // 2):
        cols = slice(g * LANES, (g + 1) * LANES)
        pair = grad_att[:, cols]
        both = dot(w_ref[2 * g], jnp.where(lane < HD, pair, zero), TN)
        both = both + dot(w_ref[2 * g + 1], jnp.where(lane < HD, zero, pair), TN)
        for i in range(3):
            rows = slice(i * TILE, (i + 1) * TILE)
            con_ref[rows, cols] = (both[rows] * counts[i]).astype(BF16)


def value_body(blocks, dsh, keep_ref, sib_ref, own_con, sib_con, v_ref, loss_ref):
    rows = 3 * TILE
    term = dot(keep_ref[...], own_con[:rows, :]) + dot(sib_ref[...], sib_con[:rows, :])
    parts = []
    for ref in (own_con, sib_con):
        part = ref[rows:, :].astype(F32)
        parts.append(part[:, :LANES] + part[:, LANES : 2 * LANES] + part[:, 2 * LANES : 3 * LANES])
    loss_ref[...] = (parts[0] + parts[1])[:8]
    for b in range(blocks):
        for cb in range(term.shape[1] // LANES):
            v_ref[b, cb * dsh : (cb + 1) * dsh, :] = term[
                b * dsh : (b + 1) * dsh, cb * LANES : (cb + 1) * LANES
            ]


def output_body(n_ens, dsh, gf_ref, read_ref, *refs):
    att_refs = refs[:n_ens]
    o_ref, scratch = refs[n_ens:]
    start = pl.multiple_of(lax.axis_index("ens") * dsh, dsh)
    for j in range(n_ens):
        scratch[j * TILE : (j + 1) * TILE, :] = att_refs[j][...]
    turned = dot(read_ref[pl.ds(start, dsh), :], gf_ref[...], NT).astype(BF16)
    term = dot(turned, scratch[...])
    for cb in range(term.shape[1] // LANES):
        o_ref[cb * dsh : (cb + 1) * dsh, :] = term[:, cb * LANES : (cb + 1) * LANES]


def finish_body(n_pix, dsh, scale, *refs):
    pieces = refs[:n_pix]
    total_ref, gv_ref, go_ref, loss_ref, scratch = refs[n_pix:]
    loss_ref[...] = total_ref[:1, :1] * scale
    rows = scratch.shape[1] // n_pix
    position = lax.axis_index("pix")
    for j in range(n_pix):
        start = pl.multiple_of((position ^ j) * rows, rows)
        scratch[:, pl.ds(start, rows), :] = pieces[j][...].astype(F32)
    for cb in range(scratch.shape[1] // dsh):
        gv_ref[:, cb * LANES : (cb + 1) * LANES] = scratch[0, cb * dsh : (cb + 1) * dsh, :]
        go_ref[cb * LANES : (cb + 1) * LANES, :] = scratch[1, cb * dsh : (cb + 1) * dsh, :].T


def in_parts(total):
    first = lax.reduce_precision(total, 8, 7)
    second = lax.reduce_precision(total - first, 8, 7)
    third = total - first - second
    return [part.astype(BF16) for part in (first, second, third, jnp.zeros_like(total))]


def with_loss(block, total):
    return jnp.concatenate([block.reshape(-1, LANES).astype(BF16)] + in_parts(total), axis=0)


def split_loss(message):
    parts = message[-32:].astype(F32).reshape(4, 8, LANES)
    return message[:-32], parts[0] + parts[1] + parts[2]


def gathered(value, axis, bits):
    pieces = {0: value}
    for bit in bits:
        held = lax.optimization_barrier(pieces)
        pieces = held | {j ^ bit: xor_permute(piece, axis, bit) for j, piece in held.items()}
    return pieces


def in_order(pieces):
    return [pieces[j] for j in sorted(pieces)]


def joined(arrays):
    return arrays[0] if len(arrays) == 1 else jnp.concatenate(arrays)


def both_cores(pieces):
    held = lax.optimization_barrier(pieces)
    return in_order(held | {j ^ 1: xor_permute(piece, "ens", 1) for j, piece in held.items()})


def at(blocks, index):
    return lax.dynamic_index_in_dim(blocks, index, 0, keepdims=False)


def part_of(split, index):
    return lax.dynamic_index_in_dim(split, index, 1, keepdims=False).reshape(-1, LANES)


def per_device(
    sample_layer_feed,
    gain,
    w_query,
    w_key,
    w_value,
    w_out,
    readout_matrix,
    target,
    pixel_weight,
    pix_mask,
    neighbours,
    neighbour_mask,
):
    n_ens, n_pix = lax.axis_size("ens"), lax.axis_size("pix")
    dsh, inner = w_query.shape
    d_model = dsh * n_ens
    n_out = readout_matrix.shape[1]
    ens_bits = [1 << b for b in reversed(range(n_ens.bit_length() - 1))]
    e, p = lax.axis_index("ens"), lax.axis_index("pix")
    rows = sample_layer_feed.shape[1]
    assert rows == TILE and n_out == LANES

    far = ens_bits[:-1]
    half, side = dsh // 2, (p // 2) % 2
    w_vo = jnp.concatenate([w_value, w_out.T])

    def half_of(w):
        return jnp.where(side == 0, w[:half], w[half:])

    qk_far = gathered(jnp.concatenate([w_query, half_of(w_key)]), "ens", far)
    vo_far = gathered(w_vo, "ens", far)
    up = lax.ppermute(sample_layer_feed, "pix", [(i, i + 1) for i in range(n_pix - 1)])
    down = lax.ppermute(sample_layer_feed, "pix", [(i + 1, i) for i in range(n_pix - 1)])
    w_qk = jnp.concatenate([w_query, w_key])
    qk_near = xor_permute(w_qk, "ens", 1)
    shards = sorted(j for j in qk_far if j)
    pieces = []
    for j in shards:
        whole = qk_far[j].shape[0] // half - 1
        pieces += [(part, i // 2, j, i % 2) for i, part in enumerate(jnp.split(qk_far[j][: whole * half], max(whole, 1))) if whole]
        for m in range(1):
            part = qk_far[j][(whole + m) * half : (whole + m + 1) * half]
            pieces.append((part, 2 - 1 + m, j, 2))
            pieces.append((xor_permute(part, "pix", 2), 2 - 1 + m, j, 3))
    parts = [piece[0] for piece in pieces]
    up, down, qk_near, parts = lax.optimization_barrier((up, down, qk_near, parts))
    parts += [xor_permute(part, "ens", 1) for part in parts]
    qk_layout = [[(0, m * dsh, dsh, 0, 0), (1, m * dsh, dsh, 1, 0)] for m in (0, 1)]
    for i, (_, m, j, place) in enumerate(pieces * 2):
        qk_layout[m].append((2 + i, 0, half, j if i < len(pieces) else j ^ 1, place))

    def layout(first):
        table = [(0, first, dsh, 0, 0), (1, first, dsh, 1, 0)]
        for i, j in enumerate(shards):
            row = 2 * i * dsh + first
            table += [(2, row, dsh, j, 0), (3, row, dsh, j ^ 1, 0)]
        return table

    mask_rows = pix_mask.reshape(n_pix, TILE)
    half = ((d_model // 2, 3 * TILE), BF16)
    normed, turned_keep, turned_send = call(
        functools.partial(normed_body, n_ens, dsh),
        [((3 * TILE, d_model), BF16), half, half],
        [("v", sample_layer_feed), ("v", up), ("v", down), ("v", gain.reshape(1, -1))],
        10**7,
        "normed",
        scratch=[pltpu.VMEM((d_model, 3 * TILE), BF16)],
    )

    full = pltpu.VMEM((d_model, inner), BF16)
    (weights,) = call(
        functools.partial(weights_body, qk_layout[0], qk_layout[1], dsh),
        [((HEADS, TILE, 3 * TILE), BF16)],
        [("v", normed), ("v", mask_rows), ("s", neighbours), ("s", neighbour_mask)]
        + [("v", a) for a in [w_qk, qk_near] + parts],
        10**9,
        "weights",
        scratch=[full],
    )
    weights, vo_far, turned_send, w_vo = lax.optimization_barrier((weights, vo_far, turned_send, w_vo))
    vo_near = xor_permute(w_vo, "ens", 1)
    vo_far = joined([vo_far[j] for j in shards])
    vo_cross = xor_permute(vo_far, "ens", 1)
    turned_sib = xor_permute(turned_send, "ens", 1)
    (attended,) = call(
        functools.partial(attend_body, layout(0), dsh),
        [((TILE, inner), BF16)],
        [("v", normed), ("v", weights), ("s", neighbours), ("s", neighbour_mask)]
        + [("v", a) for a in (w_vo, vo_near, vo_far, vo_cross)],
        10**9,
        "attend",
        scratch=[full],
    )
    forecast, w_out_full = call(
        functools.partial(forecast_body, layout(dsh), dsh),
        [((TILE, LANES), BF16), ((d_model, inner), BF16)],
        [("v", sample_layer_feed), ("v", attended), ("v", readout_matrix)]
        + [("v", a) for a in (w_vo, vo_near, vo_far, vo_cross)],
        10**9,
        "forecast",
    )
    forecasts = in_order(gathered(forecast, "ens", ens_bits))
    forecast, attended = lax.optimization_barrier((forecast, attended))
    attended_near = gathered(attended, "ens", far)

    factor = 1.0 / math.sqrt(n_ens * n_pix * TILE)
    grads, contrib = call(
        functools.partial(backward_body, n_ens, factor),
        [((n_ens * TILE, LANES), BF16), ((3 * TILE + 16, inner), BF16)],
        [("v", a) for a in forecasts + [w_out_full]]
        + [("v", target), ("v", pixel_weight.reshape(1, TILE)), ("v", mask_rows), ("v", readout_matrix)]
        + [("v", weights), ("s", neighbours), ("s", neighbour_mask)],
        10**9,
        "backward",
    )
    contrib, attended_near = lax.optimization_barrier((contrib, attended_near))
    contrib_sib = xor_permute(contrib, "ens", 1)
    attended_all = both_cores(attended_near)
    blocks = n_ens // 2
    value_term, loss = call(
        functools.partial(value_body, blocks, dsh),
        [((blocks, dsh * inner // LANES, LANES), F32), ((8, LANES), F32)],
        [("v", turned_keep), ("v", turned_sib), ("v", contrib), ("v", contrib_sib)],
        10**9,
        "value_term",
    )
    value_term, loss, grads = lax.optimization_barrier((value_term, loss, grads))
    (output_term,) = call(
        functools.partial(output_body, n_ens, dsh),
        [((dsh * inner // LANES, LANES), F32)],
        [("v", grads), ("v", readout_matrix)] + [("v", a) for a in attended_all],
        10**9,
        "output_term",
        scratch=[pltpu.VMEM((n_ens * TILE, inner), BF16)],
    )

    for bit in far[:-1]:
        upper = (e // bit) % 2
        halves = value_term.reshape(2, -1, LANES)
        got, other = split_loss(xor_permute(with_loss(at(halves, 1 - upper), loss), "ens", bit))
        value_term = at(halves, upper) + got.astype(F32)
        loss = loss + other

    n_bits = n_pix.bit_length() - 1
    groups = [[1]] + [[1 << b for b in range(s, min(s + 2, n_bits))] for s in range(1, n_bits, 2)]

    def pieces_of(term, group, higher=None):
        size = 1 << len(group)
        higher = n_pix // (group[0] * size) if higher is None else higher
        return term.reshape(higher, size, -1, LANES)

    def exchanged(messages, group):
        return [xor_permute(m, "pix", (d + 1) * group[0]) for d, m in enumerate(messages)]

    def sent(term, group, total=None, higher=None):
        size, pos = 1 << len(group), (p // group[0]) % (1 << len(group))
        split = pieces_of(term, group, higher)
        messages = [part_of(split, pos ^ d).astype(BF16) for d in range(1, size)]
        if total is not None:
            messages = [with_loss(m, total) for m in messages]
        return part_of(split, pos), exchanged(messages, group)

    def added(kept, received):
        return functools.reduce(jnp.add, [m.astype(F32) for m in received], kept)

    def added_with_loss(kept, received, total, group):
        size, pos = 1 << len(group), (p // group[0]) % (1 << len(group))
        received = [split_loss(m) for m in received]
        totals = jnp.stack([total] + [other for _, other in received])
        total = functools.reduce(jnp.add, [at(totals, pos ^ i) for i in range(size)])
        return added(kept, [m for m, _ in received]), total

    for bit in [bit for group in groups[1:] for bit in group]:
        output_term = added(*sent(output_term, [bit]))
    upper, low = (e // far[-1]) % 2, p % 2
    quarters = [pieces_of(h, groups[0]) for h in value_term.reshape(2, -1, LANES)]
    quarters = jnp.stack([part_of(q, i) for q in quarters for i in range(2)])
    pos = 2 * upper + low
    received = []
    for d in (2, 1, 3):
        pairs = [
            (i * n_pix + k, (i ^ (far[-1] * (d // 2))) * n_pix + (k ^ (d % 2)))
            for i in range(n_ens)
            for k in range(n_pix)
        ]
        message = with_loss(at(quarters, pos ^ d), loss)
        received.append((d, split_loss(lax.ppermute(message, ("ens", "pix"), pairs))))
    value_term = at(quarters, pos)
    losses = {0: loss}
    for d, (block, other) in received:
        value_term = value_term + block.astype(F32)
        losses[d] = other
    losses = jnp.stack([losses[d] for d in range(4)])
    loss = functools.reduce(jnp.add, [at(losses, pos ^ i) for i in range(4)])

    output_term = added(*sent(output_term, groups[0], higher=1))
    for group in groups[1:]:
        kept, received = sent(value_term, group, loss)
        output_term, received = lax.optimization_barrier((output_term, received))
        value_term, loss = added_with_loss(kept, received, loss, group)
    terms = [value_term, output_term]
    piece = jnp.stack(terms).astype(BF16)
    pieces = {0: piece}
    pair = {1: xor_permute(piece, "pix", 1)}
    for group in reversed(groups[1:]):
        keys = sorted(pieces)
        stack = jnp.stack([pieces[j] for j in keys])
        new = {d: xor_permute(stack, "pix", d * group[0]) for d in range(1, 1 << len(group))}
        for i, j in enumerate(keys):
            pieces.update({j ^ (d * group[0]): got[i] for d, got in new.items()})
    later = [j for j in sorted(pieces) if j]
    got = xor_permute(jnp.stack([pieces[j] for j in later]), "pix", 1)
    pair.update({j ^ 1: got[i] for i, j in enumerate(later)})
    pieces.update(pair)
    scale = 1.0 / (n_ens * n_pix * TILE * n_out)
    grad_w_value, grad_w_out, loss = call(
        functools.partial(finish_body, n_pix, dsh, scale),
        [((dsh, inner), F32), ((inner, dsh), F32), ((1, 1), F32)],
        [("v", pieces[j]) for j in range(n_pix)] + [("v", loss)],
        10**6,
        "finish",
        scratch=[pltpu.VMEM((2, dsh * inner // LANES, LANES), F32)],
    )
    return (loss.reshape(()), grad_w_out, grad_w_value)


def solution(mesh):
    in_specs = (
        P("ens", "pix", None),
        P(),
        P("ens", None),
        P("ens", None),
        P("ens", None),
        P(None, "ens"),
        P(),
        P("pix", None),
        P("pix"),
        P(),
        P("pix", None),
        P("pix", None),
    )
    out_specs = (P(), P(None, "ens"), P("ens", None))
    return jax.shard_map(
        per_device, mesh=mesh, in_specs=in_specs, out_specs=out_specs, check_vma=False
    )
```

```python
import functools
import math

import jax
import jax.numpy as jnp
from jax import lax
from jax.experimental import pallas as pl
from jax.experimental.pallas import tpu as pltpu
from jax.sharding import PartitionSpec as P

HEADS = 8
HD = 64
TILE = 128
NB = 9
LANES = 128
EPS = 1e-06
BREADTH = 0.1

F32 = jnp.float32
BF16 = jnp.bfloat16
VMEM = pl.BlockSpec(memory_space=pltpu.VMEM)
SMEM = pl.BlockSpec(memory_space=pltpu.SMEM)
NN = (((1,), (0,)), ((), ()))
NT = (((1,), (1,)), ((), ()))
TN = (((0,), (0,)), ((), ()))


def dot(a, b, dims=NN):
    return lax.dot_general(a, b, dims, preferred_element_type=F32)


def call(body, outs, ins, flops, name, scratch=(), vmem=32):
    specs = [SMEM if s == "s" else VMEM for s, _ in ins]
    return pl.pallas_call(
        body,
        out_shape=[jax.ShapeDtypeStruct(s, d) for s, d in outs],
        in_specs=specs,
        out_specs=[VMEM] * len(outs),
        scratch_shapes=list(scratch),
        compiler_params=pltpu.CompilerParams(vmem_limit_bytes=vmem * 2**20),
        cost_estimate=pl.CostEstimate(flops=flops, bytes_accessed=flops // 1000, transcendentals=0),
        name=name,
    )(*[a for _, a in ins])


def xor_permute(value, axis, mask):
    size = lax.axis_size(axis)
    return lax.ppermute(value, axis, [(i, i ^ mask) for i in range(size)])


def normed_body(
    n_ens, dsh, x_ref, up_ref, down_ref, gain_ref, pw_ref, mask_ref, n_ref, keep_ref, send_ref, lw_ref, turned_ref
):
    core = lax.axis_index("ens") % 2
    live = jnp.where(mask_ref[pl.ds(lax.axis_index("pix"), 1), :] > 0, 1.0, 0.0)
    lw_ref[...] = jnp.broadcast_to(pw_ref[...] * live, (LANES, TILE)).T
    gain = gain_ref[...]
    for i, ref in enumerate((up_ref, x_ref, down_ref)):
        rows = ref[0].astype(F32)
        inv = lax.rsqrt(jnp.mean(rows * rows, axis=-1, keepdims=True) + EPS)
        n_ref[i * TILE : (i + 1) * TILE, :] = (rows * inv * gain).astype(BF16)
    turned_ref[...] = n_ref[...].T
    for b in range(n_ens // 2):
        mine = pl.multiple_of((2 * b + core) * dsh, dsh)
        theirs = pl.multiple_of((2 * b + 1 - core) * dsh, dsh)
        keep_ref[b * dsh : (b + 1) * dsh, :] = turned_ref[pl.ds(mine, dsh), :]
        send_ref[b * dsh : (b + 1) * dsh, :] = turned_ref[pl.ds(theirs, dsh), :]


def counts_of(nb_ref, nm_ref, position):
    counts = []
    for d in (-1, 0, 1):
        total = jnp.int32(0)
        for s in range(NB):
            hit = (nb_ref[0, s] == position + d) & (nm_ref[0, s] > 0)
            total = total + jnp.where(hit, 1, 0)
        counts.append(total.astype(F32))
    return counts


def assembled(refs, layout, scratch, dsh):
    me, side = lax.axis_index("ens"), (lax.axis_index("pix") // 2) % 2
    for which, first, rows, j, place in layout:
        offset = place * rows if place < 2 else (side ^ (place - 2)) * rows
        start = pl.multiple_of((me ^ j) * dsh + offset, rows)
        scratch[pl.ds(start, rows), :] = refs[which][first : first + rows, :]
    return scratch[...]


def weights_body(q_layout, k_layout, dsh, n_ref, mask_ref, nb_ref, nm_ref, *refs):
    pieces, (w_ref, scratch) = refs[:-2], refs[-2:]
    position = lax.axis_index("pix")
    n_pix = mask_ref.shape[0]
    counts = counts_of(nb_ref, nm_ref, position)
    lanes = []
    for i, d in enumerate((-1, 0, 1)):
        row = jnp.clip(position + d, 0, n_pix - 1)
        lanes.append(jnp.where(mask_ref[pl.ds(row, 1), :] > 0, 1.0, 0.0) * counts[i])
    times = jnp.concatenate(lanes, axis=1)
    bias = jnp.where(times > 0, 0.0, -1e30)
    queries = dot(n_ref[TILE : 2 * TILE, :], assembled(pieces, q_layout, scratch, dsh)).astype(BF16)
    keys = dot(n_ref[...], assembled(pieces, k_layout, scratch, dsh)).astype(BF16)
    lane = lax.broadcasted_iota(jnp.int32, (TILE, LANES), 1)
    for h in range(HEADS):
        cols = slice(h // 2 * LANES, (h // 2 + 1) * LANES)
        own = (lane < HD) if h % 2 == 0 else (lane >= HD)
        query = jnp.where(own, queries[:, cols], jnp.zeros((), BF16))
        scores = dot(query, keys[:, cols], NT) * HD ** (-0.5) + bias
        top = jnp.max(scores, axis=-1, keepdims=True)
        expos = jnp.exp(scores - top)
        total = jnp.sum(expos * times, axis=-1, keepdims=True)
        w_ref[h] = (expos / total).astype(BF16)


def attend_body(layout, dsh, n_ref, w_ref, nb_ref, nm_ref, *refs):
    pieces, (att_ref, scratch) = refs[:-2], refs[-2:]
    counts = counts_of(nb_ref, nm_ref, lax.axis_index("pix"))
    values = dot(n_ref[...], assembled(pieces, layout, scratch, dsh)).astype(BF16)
    lane = lax.broadcasted_iota(jnp.int32, (TILE, LANES), 1)
    for g in range(HEADS // 2):
        cols = slice(g * LANES, (g + 1) * LANES)
        halves = []
        for h in (2 * g, 2 * g + 1):
            total = jnp.zeros((TILE, LANES), F32)
            for i in range(3):
                rows = slice(i * TILE, (i + 1) * TILE)
                total = total + counts[i] * dot(w_ref[h, :, rows], values[rows, cols])
            halves.append(total)
        att_ref[:, cols] = jnp.where(lane < HD, halves[0], halves[1]).astype(BF16)


def forecast_body(layout, dsh, x_ref, att_ref, read_ref, *refs):
    pieces, (f_ref, wo_ref) = refs[:-2], refs[-2:]
    hidden = x_ref[0].astype(F32) + dot(att_ref[...], assembled(pieces, layout, wo_ref, dsh), NT)
    f_ref[...] = dot(hidden.astype(BF16), read_ref[...]).astype(BF16)


def sabs(a):
    mag = jnp.abs(a)
    return mag + 2.0 * BREADTH * jnp.log1p(jnp.exp(mag * (-1.0 / BREADTH)))


def backward_body(n_ens, factor, *refs):
    f_refs = refs[:n_ens]
    wo_ref, target_ref, lw_ref, read_ref, w_ref, nb_ref, nm_ref, gf_ref, con_ref = refs[n_ens:]
    position = lax.axis_index("pix")
    counts = counts_of(nb_ref, nm_ref, position)
    lw = lw_ref[...]
    target = target_ref[...]
    fc = [ref[...].astype(F32) for ref in f_refs]
    sums = [jnp.zeros((TILE, LANES), F32) for _ in range(n_ens)]
    for i in range(n_ens):
        for j in range(i + 1, n_ens):
            t = jnp.tanh((fc[i] - fc[j]) / (2.0 * BREADTH))
            sums[i] = sums[i] + t
            sums[j] = sums[j] - t
    for i in range(n_ens):
        t = jnp.tanh((fc[i] - target) / (2.0 * BREADTH))
        gf_ref[i * TILE : (i + 1) * TILE, :] = (lw * (t - sums[i] / (n_ens - 1)) * factor).astype(BF16)
    others = jnp.zeros((TILE, LANES), F32)
    for j in range(1, n_ens):
        others = others + sabs(fc[0] - fc[j])
    terms = lw * (sabs(fc[0] - target) - others / (2.0 * (n_ens - 1)))
    loss = jnp.full((16, LANES), jnp.sum(terms), F32)
    for i in range(con_ref.shape[1] // LANES):
        part = loss.astype(BF16)
        con_ref[3 * TILE :, i * LANES : (i + 1) * LANES] = part
        loss = loss - part.astype(F32)
    grad_hidden = dot(gf_ref[:TILE, :], read_ref[...], NT).astype(BF16)
    grad_att = dot(grad_hidden, wo_ref[...]).astype(BF16)
    lane = lax.broadcasted_iota(jnp.int32, (TILE, LANES), 1)
    zero = jnp.zeros((), BF16)
    for g in range(HEADS // 2):
        cols = slice(g * LANES, (g + 1) * LANES)
        pair = grad_att[:, cols]
        both = dot(w_ref[2 * g], jnp.where(lane < HD, pair, zero), TN)
        both = both + dot(w_ref[2 * g + 1], jnp.where(lane < HD, zero, pair), TN)
        for i in range(3):
            rows = slice(i * TILE, (i + 1) * TILE)
            con_ref[rows, cols] = (both[rows] * counts[i]).astype(BF16)


def value_body(blocks, dsh, keep_ref, sib_ref, own_con, sib_con, v_ref, loss_ref):
    rows = 3 * TILE
    term = dot(keep_ref[...], own_con[:rows, :]) + dot(sib_ref[...], sib_con[:rows, :])
    parts = []
    for ref in (own_con, sib_con):
        part = ref[rows:, :].astype(F32)
        parts.append(part[:, :LANES] + part[:, LANES : 2 * LANES] + part[:, 2 * LANES : 3 * LANES])
    loss_ref[...] = (parts[0] + parts[1])[:8]
    for b in range(blocks):
        for cb in range(term.shape[1] // LANES):
            v_ref[b, cb * dsh : (cb + 1) * dsh, :] = term[
                b * dsh : (b + 1) * dsh, cb * LANES : (cb + 1) * LANES
            ]


def output_body(n_ens, dsh, gf_ref, read_ref, *refs):
    att_refs = refs[:n_ens]
    o_ref, scratch = refs[n_ens:]
    start = pl.multiple_of(lax.axis_index("ens") * dsh, dsh)
    for j in range(n_ens):
        scratch[j * TILE : (j + 1) * TILE, :] = att_refs[j][...]
    turned = dot(read_ref[pl.ds(start, dsh), :], gf_ref[...], NT).astype(BF16)
    term = dot(turned, scratch[...])
    for cb in range(term.shape[1] // LANES):
        o_ref[cb * dsh : (cb + 1) * dsh, :] = term[:, cb * LANES : (cb + 1) * LANES]


def finish_body(n_pix, dsh, scale, *refs):
    pieces = refs[:n_pix]
    total_ref, gv_ref, go_ref, loss_ref, scratch = refs[n_pix:]
    loss_ref[...] = total_ref[:1, :1] * scale
    rows = scratch.shape[1] // n_pix
    position = lax.axis_index("pix")
    for j in range(n_pix):
        start = pl.multiple_of((position ^ j) * rows, rows)
        scratch[:, pl.ds(start, rows), :] = pieces[j][...].astype(F32)
    for cb in range(scratch.shape[1] // dsh):
        gv_ref[:, cb * LANES : (cb + 1) * LANES] = scratch[0, cb * dsh : (cb + 1) * dsh, :]
        go_ref[cb * LANES : (cb + 1) * LANES, :] = scratch[1, cb * dsh : (cb + 1) * dsh, :].T


def in_parts(total):
    first = lax.reduce_precision(total, 8, 7)
    second = lax.reduce_precision(total - first, 8, 7)
    third = total - first - second
    return [part.astype(BF16) for part in (first, second, third, jnp.zeros_like(total))]


def with_loss(block, total):
    return jnp.concatenate([block.reshape(-1, LANES).astype(BF16)] + in_parts(total), axis=0)


def split_loss(message):
    parts = message[-32:].astype(F32).reshape(4, 8, LANES)
    return message[:-32], parts[0] + parts[1] + parts[2]


def gathered(value, axis, bits):
    pieces = {0: value}
    for bit in bits:
        held = lax.optimization_barrier(pieces)
        pieces = held | {j ^ bit: xor_permute(piece, axis, bit) for j, piece in held.items()}
    return pieces


def in_order(pieces):
    return [pieces[j] for j in sorted(pieces)]


def joined(arrays):
    return arrays[0] if len(arrays) == 1 else jnp.concatenate(arrays)


def both_cores(pieces):
    held = lax.optimization_barrier(pieces)
    return in_order(held | {j ^ 1: xor_permute(piece, "ens", 1) for j, piece in held.items()})


def at(blocks, index):
    return lax.dynamic_index_in_dim(blocks, index, 0, keepdims=False)


def part_of(split, index):
    return lax.dynamic_index_in_dim(split, index, 1, keepdims=False).reshape(-1, LANES)


def per_device(
    sample_layer_feed,
    gain,
    w_query,
    w_key,
    w_value,
    w_out,
    readout_matrix,
    target,
    pixel_weight,
    pix_mask,
    neighbours,
    neighbour_mask,
):
    n_ens, n_pix = lax.axis_size("ens"), lax.axis_size("pix")
    dsh, inner = w_query.shape
    d_model = dsh * n_ens
    n_out = readout_matrix.shape[1]
    ens_bits = [1 << b for b in reversed(range(n_ens.bit_length() - 1))]
    e, p = lax.axis_index("ens"), lax.axis_index("pix")
    rows = sample_layer_feed.shape[1]
    assert rows == TILE and n_out == LANES

    far = ens_bits[:-1]
    mask_rows = pix_mask.reshape(n_pix, TILE)
    half, side = dsh // 2, (p // 2) % 2
    w_vo = jnp.concatenate([w_value, w_out.T])

    def half_of(w):
        return jnp.where(side == 0, w[:half], w[half:])

    qk_far = gathered(jnp.concatenate([w_query, half_of(w_key)]), "ens", far)
    vo_far = gathered(w_vo, "ens", far)
    up = lax.ppermute(sample_layer_feed, "pix", [(i, i + 1) for i in range(n_pix - 1)])
    down = lax.ppermute(sample_layer_feed, "pix", [(i + 1, i) for i in range(n_pix - 1)])
    w_qk = jnp.concatenate([w_query, w_key])
    qk_near = xor_permute(w_qk, "ens", 1)
    turned = ((d_model // 2, 3 * TILE), BF16)
    normed, turned_keep, turned_send, lw = call(
        functools.partial(normed_body, n_ens, dsh),
        [((3 * TILE, d_model), BF16), turned, turned, ((TILE, LANES), F32)],
        [("v", sample_layer_feed), ("v", up), ("v", down), ("v", gain.reshape(1, -1))]
        + [("v", pixel_weight.reshape(1, TILE)), ("v", mask_rows)],
        10**7,
        "normed",
        scratch=[pltpu.VMEM((d_model, 3 * TILE), BF16)],
    )

    shards = sorted(j for j in qk_far if j)
    qk_far = [qk_far[j] for j in shards]
    k_far = joined([rows[dsh:] for rows in qk_far])
    k_other = xor_permute(k_far, "pix", 2)
    normed, qk_near, k_far, k_other, qk_far = lax.optimization_barrier((normed, qk_near, k_far, k_other, qk_far))
    q_far = joined([rows[:dsh] for rows in qk_far])
    q_cross = [xor_permute(part, "ens", 1) for part in jnp.split(q_far, 2 * len(shards))]
    k_cross, k_other_cross = xor_permute(k_far, "ens", 1), xor_permute(k_other, "ens", 1)
    parts = [q_far, k_far, k_other, k_cross, k_other_cross] + q_cross
    q_layout, k_layout = ([(0, m * dsh, dsh, 0, 0), (1, m * dsh, dsh, 1, 0)] for m in (0, 1))
    for i, j in enumerate(shards):
        q_layout.append((2, i * dsh, dsh, j, 0))
        q_layout += [(7 + 2 * i + m, 0, half, j ^ 1, m) for m in (0, 1)]
        k_layout += [(3 + m, i * half, half, j, 2 + m) for m in (0, 1)]
        k_layout += [(5 + m, i * half, half, j ^ 1, 2 + m) for m in (0, 1)]

    def layout(first):
        table = [(0, first, dsh, 0, 0), (1, first, dsh, 1, 0)]
        for i, j in enumerate(shards):
            row = 2 * i * dsh + first
            table += [(2, row, dsh, j, 0), (3, row, dsh, j ^ 1, 0)]
        return table

    full = pltpu.VMEM((d_model, inner), BF16)
    (weights,) = call(
        functools.partial(weights_body, q_layout, k_layout, dsh),
        [((HEADS, TILE, 3 * TILE), BF16)],
        [("v", normed), ("v", mask_rows), ("s", neighbours), ("s", neighbour_mask)]
        + [("v", a) for a in [w_qk, qk_near] + parts],
        10**3,
        "weights",
        scratch=[full],
    )
    weights, vo_far, turned_send, w_vo = lax.optimization_barrier((weights, vo_far, turned_send, w_vo))
    vo_near = xor_permute(w_vo, "ens", 1)
    vo_far = joined([vo_far[j] for j in shards])
    vo_cross = xor_permute(vo_far, "ens", 1)
    turned_sib = xor_permute(turned_send, "ens", 1)
    (attended,) = call(
        functools.partial(attend_body, layout(0), dsh),
        [((TILE, inner), BF16)],
        [("v", normed), ("v", weights), ("s", neighbours), ("s", neighbour_mask)]
        + [("v", a) for a in (w_vo, vo_near, vo_far, vo_cross)],
        10**9,
        "attend",
        scratch=[full],
    )
    forecast, w_out_full = call(
        functools.partial(forecast_body, layout(dsh), dsh),
        [((TILE, LANES), BF16), ((d_model, inner), BF16)],
        [("v", sample_layer_feed), ("v", attended), ("v", readout_matrix)]
        + [("v", a) for a in (w_vo, vo_near, vo_far, vo_cross)],
        10**9,
        "forecast",
    )
    forecasts = in_order(gathered(forecast, "ens", ens_bits))
    forecast, attended = lax.optimization_barrier((forecast, attended))
    forecasts, turned_sib = lax.optimization_barrier((forecasts, turned_sib))
    attended_near = gathered(attended, "ens", far)

    factor = 1.0 / math.sqrt(n_ens * n_pix * TILE)
    grads, contrib = call(
        functools.partial(backward_body, n_ens, factor),
        [((n_ens * TILE, LANES), BF16), ((3 * TILE + 16, inner), BF16)],
        [("v", a) for a in forecasts + [w_out_full]]
        + [("v", target), ("v", lw), ("v", readout_matrix)]
        + [("v", weights), ("s", neighbours), ("s", neighbour_mask)],
        10**9,
        "backward",
    )
    contrib, attended_near = lax.optimization_barrier((contrib, attended_near))
    contrib_sib = xor_permute(contrib, "ens", 1)
    attended_all = both_cores(attended_near)
    blocks = n_ens // 2
    value_term, loss = call(
        functools.partial(value_body, blocks, dsh),
        [((blocks, dsh * inner // LANES, LANES), F32), ((8, LANES), F32)],
        [("v", turned_keep), ("v", turned_sib), ("v", contrib), ("v", contrib_sib)],
        10**9,
        "value_term",
    )
    value_term, loss, grads = lax.optimization_barrier((value_term, loss, grads))
    (output_term,) = call(
        functools.partial(output_body, n_ens, dsh),
        [((dsh * inner // LANES, LANES), F32)],
        [("v", grads), ("v", readout_matrix)] + [("v", a) for a in attended_all],
        10**9,
        "output_term",
        scratch=[pltpu.VMEM((n_ens * TILE, inner), BF16)],
    )

    for bit in far[:-1]:
        upper = (e // bit) % 2
        halves = value_term.reshape(2, -1, LANES)
        got, other = split_loss(xor_permute(with_loss(at(halves, 1 - upper), loss), "ens", bit))
        value_term = at(halves, upper) + got.astype(F32)
        loss = loss + other

    n_bits = n_pix.bit_length() - 1
    groups = [[1]] + [[1 << b for b in range(s, min(s + 2, n_bits))] for s in range(1, n_bits, 2)]

    def pieces_of(term, group, higher=None):
        size = 1 << len(group)
        higher = n_pix // (group[0] * size) if higher is None else higher
        return term.reshape(higher, size, -1, LANES)

    def exchanged(messages, group):
        return [xor_permute(m, "pix", (d + 1) * group[0]) for d, m in enumerate(messages)]

    def sent(term, group, total=None, higher=None):
        size, pos = 1 << len(group), (p // group[0]) % (1 << len(group))
        split = pieces_of(term, group, higher)
        messages = [part_of(split, pos ^ d).astype(BF16) for d in range(1, size)]
        if total is not None:
            messages = [with_loss(m, total) for m in messages]
        return part_of(split, pos), exchanged(messages, group)

    def added(kept, received):
        return functools.reduce(jnp.add, [m.astype(F32) for m in received], kept)

    later = [bit for group in groups[1:] for bit in group]
    for bit in later[:-1]:
        output_term = added(*sent(output_term, [bit]))
    output_kept, output_got = sent(output_term, groups[0], higher=2)
    upper, low = (e // far[-1]) % 2, p % 2
    quarters = [pieces_of(h, groups[0]) for h in value_term.reshape(2, -1, LANES)]
    quarters = jnp.stack([part_of(q, i) for q in quarters for i in range(2)])
    pos = 2 * upper + low
    received = []
    for d in (2, 1, 3):
        pairs = [
            (i * n_pix + k, (i ^ (far[-1] * (d // 2))) * n_pix + (k ^ (d % 2)))
            for i in range(n_ens)
            for k in range(n_pix)
        ]
        message = with_loss(at(quarters, pos ^ d), loss)
        received.append((d, split_loss(lax.ppermute(message, ("ens", "pix"), pairs))))
    value_term = at(quarters, pos)
    losses = {0: loss}
    for d, (block, other) in received:
        value_term = value_term + block.astype(F32)
        losses[d] = other
    losses = jnp.stack([losses[d] for d in range(4)])
    loss = functools.reduce(jnp.add, [at(losses, pos ^ i) for i in range(4)])

    for group in groups[1:]:
        size, pos = 1 << len(group), (p // group[0]) % (1 << len(group))
        split = pieces_of(value_term, group)
        kept, messages = part_of(split, pos), {d: part_of(split, pos ^ d).astype(BF16) for d in range(1, size)}
        top = size // 2
        if group == groups[-1]:
            split = pieces_of(added(output_kept, output_got), [later[-1]], 1)
            own = (p // later[-1]) % 2
            output_kept = part_of(split, own)
            messages[top] = jnp.concatenate([messages[top], part_of(split, 1 - own).astype(BF16)])
        received = {d: split_loss(xor_permute(with_loss(m, loss), "pix", d * group[0])) for d, m in messages.items()}
        if group == groups[-1]:
            both, other = received[top]
            output_term = output_kept + both[-output_kept.shape[0] :].astype(F32)
            received[top] = (both[: kept.shape[0]], other)
        totals = jnp.stack([loss] + [received[d][1] for d in range(1, size)])
        loss = functools.reduce(jnp.add, [at(totals, pos ^ i) for i in range(size)])
        value_term = added(kept, [received[d][0] for d in range(1, size)])
    terms = [value_term, output_term]
    piece = jnp.stack(terms).astype(BF16)
    pieces, near = {0: piece}, groups[1][0]
    pair = {1: xor_permute(piece, "pix", 1), near ^ 1: xor_permute(piece, "pix", near ^ 1)}
    for group in reversed(groups[1:]):
        keys = sorted(pieces)
        stack = jnp.stack([pieces[j] for j in keys])
        new = {d: xor_permute(stack, "pix", d * group[0]) for d in range(1, 1 << len(group))}
        for i, j in enumerate(keys):
            pieces.update({j ^ (d * group[0]): got[i] for d, got in new.items()})
    later = [j for j in sorted(pieces) if j not in (0, near)]
    got = xor_permute(jnp.stack([pieces[j] for j in later]), "pix", 1)
    pair.update({j ^ 1: got[i] for i, j in enumerate(later)})
    pieces.update(pair)
    scale = 1.0 / (n_ens * n_pix * TILE * n_out)
    grad_w_value, grad_w_out, loss = call(
        functools.partial(finish_body, n_pix, dsh, scale),
        [((dsh, inner), F32), ((inner, dsh), F32), ((1, 1), F32)],
        [("v", pieces[j]) for j in range(n_pix)] + [("v", loss)],
        10**6,
        "finish",
        scratch=[pltpu.VMEM((2, dsh * inner // LANES, LANES), F32)],
    )
    return (loss.reshape(()), grad_w_out, grad_w_value)


def solution(mesh):
    in_specs = (
        P("ens", "pix", None),
        P(),
        P("ens", None),
        P("ens", None),
        P("ens", None),
        P(None, "ens"),
        P(),
        P("pix", None),
        P("pix"),
        P(),
        P("pix", None),
        P("pix", None),
    )
    out_specs = (P(), P(None, "ens"), P("ens", None))
    return jax.shard_map(
        per_device, mesh=mesh, in_specs=in_specs, out_specs=out_specs, check_vma=False
    )
```

```python
import functools
import math

import jax
import jax.numpy as jnp
from jax import lax
from jax.experimental import pallas as pl
from jax.experimental.pallas import tpu as pltpu
from jax.sharding import PartitionSpec as P

HEADS = 8
HD = 64
TILE = 128
NB = 9
LANES = 128
EPS = 1e-06
BREADTH = 0.1

F32 = jnp.float32
BF16 = jnp.bfloat16
VMEM = pl.BlockSpec(memory_space=pltpu.VMEM)
SMEM = pl.BlockSpec(memory_space=pltpu.SMEM)
NN = (((1,), (0,)), ((), ()))
NT = (((1,), (1,)), ((), ()))
TN = (((0,), (0,)), ((), ()))


def dot(a, b, dims=NN):
    return lax.dot_general(a, b, dims, preferred_element_type=F32)


def call(body, outs, ins, flops, name, scratch=(), vmem=32):
    specs = [SMEM if s == "s" else VMEM for s, _ in ins]
    return pl.pallas_call(
        body,
        out_shape=[jax.ShapeDtypeStruct(s, d) for s, d in outs],
        in_specs=specs,
        out_specs=[VMEM] * len(outs),
        scratch_shapes=list(scratch),
        compiler_params=pltpu.CompilerParams(vmem_limit_bytes=vmem * 2**20),
        cost_estimate=pl.CostEstimate(flops=flops, bytes_accessed=flops // 1000, transcendentals=0),
        name=name,
    )(*[a for _, a in ins])


def xor_permute(value, axis, mask):
    size = lax.axis_size(axis)
    return lax.ppermute(value, axis, [(i, i ^ mask) for i in range(size)])


def normed_body(
    n_ens, dsh, x_ref, up_ref, down_ref, gain_ref, pw_ref, mask_ref, n_ref, keep_ref, send_ref, lw_ref, turned_ref
):
    core = lax.axis_index("ens") % 2
    live = jnp.where(mask_ref[pl.ds(lax.axis_index("pix"), 1), :] > 0, 1.0, 0.0)
    lw_ref[...] = jnp.broadcast_to(pw_ref[...] * live, (LANES, TILE)).T
    gain = gain_ref[...]
    for i, ref in enumerate((up_ref, x_ref, down_ref)):
        rows = ref[0].astype(F32)
        inv = lax.rsqrt(jnp.mean(rows * rows, axis=-1, keepdims=True) + EPS)
        n_ref[i * TILE : (i + 1) * TILE, :] = (rows * inv * gain).astype(BF16)
    turned_ref[...] = n_ref[...].T
    for b in range(n_ens // 2):
        mine = pl.multiple_of((2 * b + core) * dsh, dsh)
        theirs = pl.multiple_of((2 * b + 1 - core) * dsh, dsh)
        keep_ref[b * dsh : (b + 1) * dsh, :] = turned_ref[pl.ds(mine, dsh), :]
        send_ref[b * dsh : (b + 1) * dsh, :] = turned_ref[pl.ds(theirs, dsh), :]


def counts_of(nb_ref, nm_ref, position):
    counts = []
    for d in (-1, 0, 1):
        total = jnp.int32(0)
        for s in range(NB):
            hit = (nb_ref[0, s] == position + d) & (nm_ref[0, s] > 0)
            total = total + jnp.where(hit, 1, 0)
        counts.append(total.astype(F32))
    return counts


def assembled(refs, layout, scratch, dsh):
    me, side = lax.axis_index("ens"), (lax.axis_index("pix") // 2) % 2
    for which, first, rows, j, place in layout:
        offset = place * rows if place < 2 else (side ^ (place - 2)) * rows
        start = pl.multiple_of((me ^ j) * dsh + offset, rows)
        scratch[pl.ds(start, rows), :] = refs[which][first : first + rows, :]
    return scratch[...]


def weights_body(q_layout, k_layout, dsh, n_ref, mask_ref, nb_ref, nm_ref, *refs):
    pieces, (w_ref, scratch) = refs[:-2], refs[-2:]
    position = lax.axis_index("pix")
    n_pix = mask_ref.shape[0]
    counts = counts_of(nb_ref, nm_ref, position)
    lanes = []
    for i, d in enumerate((-1, 0, 1)):
        row = jnp.clip(position + d, 0, n_pix - 1)
        lanes.append(jnp.where(mask_ref[pl.ds(row, 1), :] > 0, 1.0, 0.0) * counts[i])
    times = jnp.concatenate(lanes, axis=1)
    bias = jnp.where(times > 0, 0.0, -1e30)
    queries = dot(n_ref[TILE : 2 * TILE, :], assembled(pieces, q_layout, scratch, dsh)).astype(BF16)
    keys = dot(n_ref[...], assembled(pieces, k_layout, scratch, dsh)).astype(BF16)
    lane = lax.broadcasted_iota(jnp.int32, (TILE, LANES), 1)
    for h in range(HEADS):
        cols = slice(h // 2 * LANES, (h // 2 + 1) * LANES)
        own = (lane < HD) if h % 2 == 0 else (lane >= HD)
        query = jnp.where(own, queries[:, cols], jnp.zeros((), BF16))
        scores = dot(query, keys[:, cols], NT) * HD ** (-0.5) + bias
        top = jnp.max(scores, axis=-1, keepdims=True)
        expos = jnp.exp(scores - top)
        total = jnp.sum(expos * times, axis=-1, keepdims=True)
        w_ref[h] = (expos / total).astype(BF16)


def attend_body(layout, dsh, n_ref, w_ref, nb_ref, nm_ref, *refs):
    pieces, (att_ref, scratch) = refs[:-2], refs[-2:]
    counts = counts_of(nb_ref, nm_ref, lax.axis_index("pix"))
    values = dot(n_ref[...], assembled(pieces, layout, scratch, dsh)).astype(BF16)
    lane = lax.broadcasted_iota(jnp.int32, (TILE, LANES), 1)
    for g in range(HEADS // 2):
        cols = slice(g * LANES, (g + 1) * LANES)
        halves = []
        for h in (2 * g, 2 * g + 1):
            total = jnp.zeros((TILE, LANES), F32)
            for i in range(3):
                rows = slice(i * TILE, (i + 1) * TILE)
                total = total + counts[i] * dot(w_ref[h, :, rows], values[rows, cols])
            halves.append(total)
        att_ref[:, cols] = jnp.where(lane < HD, halves[0], halves[1]).astype(BF16)


def forecast_body(layout, dsh, x_ref, att_ref, read_ref, *refs):
    pieces, (f_ref, wo_ref) = refs[:-2], refs[-2:]
    hidden = x_ref[0].astype(F32) + dot(att_ref[...], assembled(pieces, layout, wo_ref, dsh), NT)
    f_ref[...] = dot(hidden.astype(BF16), read_ref[...]).astype(BF16)


def sabs(a):
    mag = jnp.abs(a)
    return mag + 2.0 * BREADTH * jnp.log1p(jnp.exp(mag * (-1.0 / BREADTH)))


def backward_body(n_ens, factor, *refs):
    f_refs = refs[:n_ens]
    wo_ref, target_ref, lw_ref, read_ref, w_ref, nb_ref, nm_ref, gf_ref, con_ref = refs[n_ens:]
    position = lax.axis_index("pix")
    counts = counts_of(nb_ref, nm_ref, position)
    lw = lw_ref[...]
    target = target_ref[...]
    fc = [ref[...].astype(F32) for ref in f_refs]
    sums = [jnp.zeros((TILE, LANES), F32) for _ in range(n_ens)]
    for i in range(n_ens):
        for j in range(i + 1, n_ens):
            t = jnp.tanh((fc[i] - fc[j]) / (2.0 * BREADTH))
            sums[i] = sums[i] + t
            sums[j] = sums[j] - t
    for i in range(n_ens):
        t = jnp.tanh((fc[i] - target) / (2.0 * BREADTH))
        gf_ref[i * TILE : (i + 1) * TILE, :] = (lw * (t - sums[i] / (n_ens - 1)) * factor).astype(BF16)
    others = jnp.zeros((TILE, LANES), F32)
    for j in range(1, n_ens):
        others = others + sabs(fc[0] - fc[j])
    terms = lw * (sabs(fc[0] - target) - others / (2.0 * (n_ens - 1)))
    loss = jnp.full((16, LANES), jnp.sum(terms), F32)
    for i in range(con_ref.shape[1] // LANES):
        part = loss.astype(BF16)
        con_ref[3 * TILE :, i * LANES : (i + 1) * LANES] = part
        loss = loss - part.astype(F32)
    grad_hidden = dot(gf_ref[:TILE, :], read_ref[...], NT).astype(BF16)
    grad_att = dot(grad_hidden, wo_ref[...]).astype(BF16)
    lane = lax.broadcasted_iota(jnp.int32, (TILE, LANES), 1)
    zero = jnp.zeros((), BF16)
    for g in range(HEADS // 2):
        cols = slice(g * LANES, (g + 1) * LANES)
        pair = grad_att[:, cols]
        both = dot(w_ref[2 * g], jnp.where(lane < HD, pair, zero), TN)
        both = both + dot(w_ref[2 * g + 1], jnp.where(lane < HD, zero, pair), TN)
        for i in range(3):
            rows = slice(i * TILE, (i + 1) * TILE)
            con_ref[rows, cols] = (both[rows] * counts[i]).astype(BF16)


def value_body(blocks, dsh, keep_ref, sib_ref, own_con, sib_con, v_ref, loss_ref):
    rows = 3 * TILE
    term = dot(keep_ref[...], own_con[:rows, :]) + dot(sib_ref[...], sib_con[:rows, :])
    parts = []
    for ref in (own_con, sib_con):
        part = ref[rows:, :].astype(F32)
        parts.append(part[:, :LANES] + part[:, LANES : 2 * LANES] + part[:, 2 * LANES : 3 * LANES])
    loss_ref[...] = (parts[0] + parts[1])[:8]
    for b in range(blocks):
        for cb in range(term.shape[1] // LANES):
            v_ref[b, cb * dsh : (cb + 1) * dsh, :] = term[
                b * dsh : (b + 1) * dsh, cb * LANES : (cb + 1) * LANES
            ]


def output_body(n_ens, dsh, gf_ref, read_ref, *refs):
    att_refs = refs[:n_ens]
    o_ref, scratch = refs[n_ens:]
    start = pl.multiple_of(lax.axis_index("ens") * dsh, dsh)
    for j in range(n_ens):
        scratch[j * TILE : (j + 1) * TILE, :] = att_refs[j][...]
    turned = dot(read_ref[pl.ds(start, dsh), :], gf_ref[...], NT).astype(BF16)
    term = dot(turned, scratch[...])
    for cb in range(term.shape[1] // LANES):
        o_ref[cb * dsh : (cb + 1) * dsh, :] = term[:, cb * LANES : (cb + 1) * LANES]


def finish_body(n_pix, dsh, scale, *refs):
    pieces = refs[:n_pix]
    total_ref, gv_ref, go_ref, loss_ref, scratch = refs[n_pix:]
    loss_ref[...] = total_ref[:1, :1] * scale
    rows = scratch.shape[1] // n_pix
    position = lax.axis_index("pix")
    for j in range(n_pix):
        start = pl.multiple_of((position ^ j) * rows, rows)
        scratch[:, pl.ds(start, rows), :] = pieces[j][...].astype(F32)
    for cb in range(scratch.shape[1] // dsh):
        gv_ref[:, cb * LANES : (cb + 1) * LANES] = scratch[0, cb * dsh : (cb + 1) * dsh, :]
        go_ref[cb * LANES : (cb + 1) * LANES, :] = scratch[1, cb * dsh : (cb + 1) * dsh, :].T


def in_parts(total):
    first = lax.reduce_precision(total, 8, 7)
    return [first.astype(BF16), (total - first).astype(BF16)]


def with_loss(block, total):
    return jnp.concatenate([block.reshape(-1, LANES).astype(BF16)] + in_parts(total), axis=0)


def split_loss(message):
    parts = message[-16:].astype(F32).reshape(2, 8, LANES)
    return message[:-16], parts[0] + parts[1]


def gathered(value, axis, bits):
    pieces = {0: value}
    for bit in bits:
        held = lax.optimization_barrier(pieces)
        pieces = held | {j ^ bit: xor_permute(piece, axis, bit) for j, piece in held.items()}
    return pieces


def in_order(pieces):
    return [pieces[j] for j in sorted(pieces)]


def joined(arrays):
    return arrays[0] if len(arrays) == 1 else jnp.concatenate(arrays)


def both_cores(pieces):
    held = lax.optimization_barrier(pieces)
    return in_order(held | {j ^ 1: xor_permute(piece, "ens", 1) for j, piece in held.items()})


def at(blocks, index):
    return lax.dynamic_index_in_dim(blocks, index, 0, keepdims=False)


def part_of(split, index):
    return lax.dynamic_index_in_dim(split, index, 1, keepdims=False).reshape(-1, LANES)


def per_device(
    sample_layer_feed,
    gain,
    w_query,
    w_key,
    w_value,
    w_out,
    readout_matrix,
    target,
    pixel_weight,
    pix_mask,
    neighbours,
    neighbour_mask,
):
    n_ens, n_pix = lax.axis_size("ens"), lax.axis_size("pix")
    dsh, inner = w_query.shape
    d_model = dsh * n_ens
    n_out = readout_matrix.shape[1]
    ens_bits = [1 << b for b in reversed(range(n_ens.bit_length() - 1))]
    e, p = lax.axis_index("ens"), lax.axis_index("pix")
    rows = sample_layer_feed.shape[1]
    assert rows == TILE and n_out == LANES

    far = ens_bits[:-1]
    mask_rows = pix_mask.reshape(n_pix, TILE)
    half, side = dsh // 2, (p // 2) % 2
    w_vo = jnp.concatenate([w_value, w_out.T])

    def half_of(w):
        return jnp.where(side == 0, w[:half], w[half:])

    qk_far = gathered(jnp.concatenate([w_query, half_of(w_key)]), "ens", far)
    vo_far = gathered(w_vo, "ens", far)
    up = lax.ppermute(sample_layer_feed, "pix", [(i, i + 1) for i in range(n_pix - 1)])
    down = lax.ppermute(sample_layer_feed, "pix", [(i + 1, i) for i in range(n_pix - 1)])
    w_qk = jnp.concatenate([w_query, w_key])
    qk_near = xor_permute(w_qk, "ens", 1)
    turned = ((d_model // 2, 3 * TILE), BF16)
    normed, turned_keep, turned_send, lw = call(
        functools.partial(normed_body, n_ens, dsh),
        [((3 * TILE, d_model), BF16), turned, turned, ((TILE, LANES), F32)],
        [("v", sample_layer_feed), ("v", up), ("v", down), ("v", gain.reshape(1, -1))]
        + [("v", pixel_weight.reshape(1, TILE)), ("v", mask_rows)],
        10**7,
        "normed",
        scratch=[pltpu.VMEM((d_model, 3 * TILE), BF16)],
    )

    shards = sorted(j for j in qk_far if j)
    qk_far = [qk_far[j] for j in shards]
    k_far = joined([rows[dsh:] for rows in qk_far])
    k_other = xor_permute(k_far, "pix", 2)
    normed, qk_near, k_far, k_other, qk_far = lax.optimization_barrier((normed, qk_near, k_far, k_other, qk_far))
    q_far = joined([rows[:dsh] for rows in qk_far])
    q_cross = [xor_permute(part, "ens", 1) for part in jnp.split(q_far, 2 * len(shards))]
    k_cross, k_other_cross = xor_permute(k_far, "ens", 1), xor_permute(k_other, "ens", 1)
    parts = [q_far, k_far, k_other, k_cross, k_other_cross] + q_cross
    q_layout, k_layout = ([(0, m * dsh, dsh, 0, 0), (1, m * dsh, dsh, 1, 0)] for m in (0, 1))
    for i, j in enumerate(shards):
        q_layout.append((2, i * dsh, dsh, j, 0))
        q_layout += [(7 + 2 * i + m, 0, half, j ^ 1, m) for m in (0, 1)]
        k_layout += [(3 + m, i * half, half, j, 2 + m) for m in (0, 1)]
        k_layout += [(5 + m, i * half, half, j ^ 1, 2 + m) for m in (0, 1)]

    def layout(first):
        table = [(0, first, dsh, 0, 0), (1, 0, dsh, 1, 0)]
        for i, j in enumerate(shards):
            table += [(2, i * dsh, dsh, j, 0), (3, i * dsh, dsh, j ^ 1, 0)]
        return table

    full = pltpu.VMEM((d_model, inner), BF16)
    (weights,) = call(
        functools.partial(weights_body, q_layout, k_layout, dsh),
        [((HEADS, TILE, 3 * TILE), BF16)],
        [("v", normed), ("v", mask_rows), ("s", neighbours), ("s", neighbour_mask)]
        + [("v", a) for a in [w_qk, qk_near] + parts],
        10**3,
        "weights",
        scratch=[full],
    )
    weights, vo_far, turned_send, w_vo = lax.optimization_barrier((weights, vo_far, turned_send, w_vo))
    vo_near = [xor_permute(w_vo[:dsh], "ens", 1), xor_permute(w_vo[dsh:], "ens", 1)]
    vo_far = [joined([vo_far[j][m * dsh : (m + 1) * dsh] for j in shards]) for m in (0, 1)]
    vo_cross = [xor_permute(part, "ens", 1) for part in vo_far]
    turned_sib = xor_permute(turned_send, "ens", 1)
    (attended,) = call(
        functools.partial(attend_body, layout(0), dsh),
        [((TILE, inner), BF16)],
        [("v", normed), ("v", weights), ("s", neighbours), ("s", neighbour_mask)]
        + [("v", a) for a in (w_vo, vo_near[0], vo_far[0], vo_cross[0])],
        10**9,
        "attend",
        scratch=[full],
    )
    forecast, w_out_full = call(
        functools.partial(forecast_body, layout(dsh), dsh),
        [((TILE, LANES), BF16), ((d_model, inner), BF16)],
        [("v", sample_layer_feed), ("v", attended), ("v", readout_matrix)]
        + [("v", a) for a in (w_vo, vo_near[1], vo_far[1], vo_cross[1])],
        10**9,
        "forecast",
    )
    forecasts = in_order(gathered(forecast, "ens", ens_bits))
    forecast, attended = lax.optimization_barrier((forecast, attended))
    forecasts, turned_sib = lax.optimization_barrier((forecasts, turned_sib))
    attended_near = gathered(attended, "ens", far)

    factor = 1.0 / math.sqrt(n_ens * n_pix * TILE)
    grads, contrib = call(
        functools.partial(backward_body, n_ens, factor),
        [((n_ens * TILE, LANES), BF16), ((3 * TILE + 16, inner), BF16)],
        [("v", a) for a in forecasts + [w_out_full]]
        + [("v", target), ("v", lw), ("v", readout_matrix)]
        + [("v", weights), ("s", neighbours), ("s", neighbour_mask)],
        10**9,
        "backward",
    )
    contrib, attended_near = lax.optimization_barrier((contrib, attended_near))
    contrib_sib = xor_permute(contrib, "ens", 1)
    attended_all = both_cores(attended_near)
    blocks = n_ens // 2
    value_term, loss = call(
        functools.partial(value_body, blocks, dsh),
        [((blocks, dsh * inner // LANES, LANES), F32), ((8, LANES), F32)],
        [("v", turned_keep), ("v", turned_sib), ("v", contrib), ("v", contrib_sib)],
        10**9,
        "value_term",
    )
    value_term, loss, grads = lax.optimization_barrier((value_term, loss, grads))
    (output_term,) = call(
        functools.partial(output_body, n_ens, dsh),
        [((dsh * inner // LANES, LANES), F32)],
        [("v", grads), ("v", readout_matrix)] + [("v", a) for a in attended_all],
        10**9,
        "output_term",
        scratch=[pltpu.VMEM((n_ens * TILE, inner), BF16)],
    )

    for bit in far[:-1]:
        upper = (e // bit) % 2
        halves = value_term.reshape(2, -1, LANES)
        got, other = split_loss(xor_permute(with_loss(at(halves, 1 - upper), loss), "ens", bit))
        value_term = at(halves, upper) + got.astype(F32)
        loss = loss + other

    n_bits = n_pix.bit_length() - 1
    groups = [[1]] + [[1 << b for b in range(s, min(s + 2, n_bits))] for s in range(1, n_bits, 2)]

    def pieces_of(term, group, higher=None):
        size = 1 << len(group)
        higher = n_pix // (group[0] * size) if higher is None else higher
        return term.reshape(higher, size, -1, LANES)

    def exchanged(messages, group):
        return [xor_permute(m, "pix", (d + 1) * group[0]) for d, m in enumerate(messages)]

    def sent(term, group, total=None, higher=None):
        size, pos = 1 << len(group), (p // group[0]) % (1 << len(group))
        split = pieces_of(term, group, higher)
        messages = [part_of(split, pos ^ d).astype(BF16) for d in range(1, size)]
        if total is not None:
            messages = [with_loss(m, total) for m in messages]
        return part_of(split, pos), exchanged(messages, group)

    def added(kept, received):
        return functools.reduce(jnp.add, [m.astype(F32) for m in received], kept)

    later = [bit for group in groups[1:] for bit in group]
    for bit in later[:-2]:
        output_term = added(*sent(output_term, [bit]))
    output_kept, output_got = sent(output_term, [later[-2]])
    upper, low = (e // far[-1]) % 2, p % 2
    quarters = [pieces_of(h, groups[0]) for h in value_term.reshape(2, -1, LANES)]
    quarters = jnp.stack([part_of(q, i) for q in quarters for i in range(2)])
    pos = 2 * upper + low
    received = []
    for d in (2, 1, 3):
        pairs = [
            (i * n_pix + k, (i ^ (far[-1] * (d // 2))) * n_pix + (k ^ (d % 2)))
            for i in range(n_ens)
            for k in range(n_pix)
        ]
        message = with_loss(at(quarters, pos ^ d), loss)
        received.append((d, split_loss(lax.ppermute(message, ("ens", "pix"), pairs))))
    value_term = at(quarters, pos)
    losses = {0: loss}
    for d, (block, other) in received:
        value_term = value_term + block.astype(F32)
        losses[d] = other
    losses = jnp.stack([losses[d] for d in range(4)])
    loss = functools.reduce(jnp.add, [at(losses, pos ^ i) for i in range(4)])

    value_term, output_got = lax.optimization_barrier((value_term, output_got))
    output_kept, output_got = sent(added(output_kept, output_got), groups[0], higher=2)
    for group in groups[1:]:
        size, pos = 1 << len(group), (p // group[0]) % (1 << len(group))
        split = pieces_of(value_term, group)
        messages = {d: with_loss(part_of(split, pos ^ d), loss) for d in range(1, size)}
        received = {d: xor_permute(m, "pix", d * group[0]) for d, m in messages.items()}
        if group == groups[-1]:
            output_kept, output_got = sent(added(output_kept, output_got), [later[-1]], higher=1)
            received, output_got = lax.optimization_barrier((received, output_got))
        received = {d: split_loss(m) for d, m in received.items()}
        totals = jnp.stack([loss] + [received[d][1] for d in range(1, size)])
        loss = functools.reduce(jnp.add, [at(totals, pos ^ i) for i in range(size)])
        value_term = added(part_of(split, pos), [received[d][0] for d in range(1, size)])
    output_term = added(output_kept, output_got)
    terms = [value_term, output_term]
    piece = jnp.stack(terms).astype(BF16)
    pieces, near = {0: piece}, groups[1][0]
    pair = {1: xor_permute(piece, "pix", 1), near ^ 1: xor_permute(piece, "pix", near ^ 1)}
    for group in reversed(groups[1:]):
        keys = sorted(pieces)
        stack = jnp.stack([pieces[j] for j in keys])
        new = {d: xor_permute(stack, "pix", d * group[0]) for d in range(1, 1 << len(group))}
        for i, j in enumerate(keys):
            pieces.update({j ^ (d * group[0]): got[i] for d, got in new.items()})
    later = [j for j in sorted(pieces) if j not in (0, near)]
    got = xor_permute(jnp.stack([pieces[j] for j in later]), "pix", 1)
    pair.update({j ^ 1: got[i] for i, j in enumerate(later)})
    pieces.update(pair)
    scale = 1.0 / (n_ens * n_pix * TILE * n_out)
    grad_w_value, grad_w_out, loss = call(
        functools.partial(finish_body, n_pix, dsh, scale),
        [((dsh, inner), F32), ((inner, dsh), F32), ((1, 1), F32)],
        [("v", pieces[j]) for j in range(n_pix)] + [("v", loss)],
        10**6,
        "finish",
        scratch=[pltpu.VMEM((2, dsh * inner // LANES, LANES), F32)],
    )
    return (loss.reshape(()), grad_w_out, grad_w_value)


def solution(mesh):
    in_specs = (
        P("ens", "pix", None),
        P(),
        P("ens", None),
        P("ens", None),
        P("ens", None),
        P(None, "ens"),
        P(),
        P("pix", None),
        P("pix"),
        P(),
        P("pix", None),
        P("pix", None),
    )
    out_specs = (P(), P(None, "ens"), P("ens", None))
    return jax.shard_map(
        per_device, mesh=mesh, in_specs=in_specs, out_specs=out_specs, check_vma=False
    )
```

```python
import functools
import math

import jax
import jax.numpy as jnp
from jax import lax
from jax.experimental import pallas as pl
from jax.experimental.pallas import tpu as pltpu
from jax.sharding import PartitionSpec as P

HEADS = 8
HD = 64
TILE = 128
NB = 9
LANES = 128
EPS = 1e-06
BREADTH = 0.1

F32 = jnp.float32
BF16 = jnp.bfloat16
VMEM = pl.BlockSpec(memory_space=pltpu.VMEM)
SMEM = pl.BlockSpec(memory_space=pltpu.SMEM)
NN = (((1,), (0,)), ((), ()))
NT = (((1,), (1,)), ((), ()))
TN = (((0,), (0,)), ((), ()))


def dot(a, b, dims=NN):
    return lax.dot_general(a, b, dims, preferred_element_type=F32)


def call(body, outs, ins, flops, name, scratch=(), vmem=32):
    specs = [SMEM if s == "s" else VMEM for s, _ in ins]
    return pl.pallas_call(
        body,
        out_shape=[jax.ShapeDtypeStruct(s, d) for s, d in outs],
        in_specs=specs,
        out_specs=[VMEM] * len(outs),
        scratch_shapes=list(scratch),
        compiler_params=pltpu.CompilerParams(vmem_limit_bytes=vmem * 2**20),
        cost_estimate=pl.CostEstimate(flops=flops, bytes_accessed=flops // 1000, transcendentals=0),
        name=name,
    )(*[a for _, a in ins])


def xor_permute(value, axis, mask):
    size = lax.axis_size(axis)
    return lax.ppermute(value, axis, [(i, i ^ mask) for i in range(size)])


def normed_body(
    n_ens, dsh, x_ref, up_ref, down_ref, gain_ref, pw_ref, mask_ref, n_ref, keep_ref, send_ref, lw_ref, turned_ref
):
    core = lax.axis_index("ens") % 2
    live = jnp.where(mask_ref[pl.ds(lax.axis_index("pix"), 1), :] > 0, 1.0, 0.0)
    lw_ref[...] = jnp.broadcast_to(pw_ref[...] * live, (LANES, TILE)).T
    gain = gain_ref[...]
    for i, ref in enumerate((up_ref, x_ref, down_ref)):
        rows = ref[0].astype(F32)
        inv = lax.rsqrt(jnp.mean(rows * rows, axis=-1, keepdims=True) + EPS)
        n_ref[i * TILE : (i + 1) * TILE, :] = (rows * inv * gain).astype(BF16)
    turned_ref[...] = n_ref[...].T
    for b in range(n_ens // 2):
        mine = pl.multiple_of((2 * b + core) * dsh, dsh)
        theirs = pl.multiple_of((2 * b + 1 - core) * dsh, dsh)
        keep_ref[b * dsh : (b + 1) * dsh, :] = turned_ref[pl.ds(mine, dsh), :]
        send_ref[b * dsh : (b + 1) * dsh, :] = turned_ref[pl.ds(theirs, dsh), :]


def counts_of(nb_ref, nm_ref, position):
    counts = []
    for d in (-1, 0, 1):
        total = jnp.int32(0)
        for s in range(NB):
            hit = (nb_ref[0, s] == position + d) & (nm_ref[0, s] > 0)
            total = total + jnp.where(hit, 1, 0)
        counts.append(total.astype(F32))
    return counts


def assembled(refs, layout, scratch, dsh):
    me, side = lax.axis_index("ens"), (lax.axis_index("pix") // 2) % 2
    for which, first, rows, j, place in layout:
        offset = place * rows if place < 2 else (side ^ (place - 2)) * rows
        start = pl.multiple_of((me ^ j) * dsh + offset, rows)
        scratch[pl.ds(start, rows), :] = refs[which][first : first + rows, :]
    return scratch[...]


def weights_body(q_layout, k_layout, dsh, n_ref, mask_ref, nb_ref, nm_ref, *refs):
    pieces, (w_ref, scratch) = refs[:-2], refs[-2:]
    position = lax.axis_index("pix")
    n_pix = mask_ref.shape[0]
    counts = counts_of(nb_ref, nm_ref, position)
    lanes = []
    for i, d in enumerate((-1, 0, 1)):
        row = jnp.clip(position + d, 0, n_pix - 1)
        lanes.append(jnp.where(mask_ref[pl.ds(row, 1), :] > 0, 1.0, 0.0) * counts[i])
    times = jnp.concatenate(lanes, axis=1)
    bias = jnp.where(times > 0, 0.0, -1e30)
    queries = dot(n_ref[TILE : 2 * TILE, :], assembled(pieces, q_layout, scratch, dsh)).astype(BF16)
    keys = dot(n_ref[...], assembled(pieces, k_layout, scratch, dsh)).astype(BF16)
    lane = lax.broadcasted_iota(jnp.int32, (TILE, LANES), 1)
    for h in range(HEADS):
        cols = slice(h // 2 * LANES, (h // 2 + 1) * LANES)
        own = (lane < HD) if h % 2 == 0 else (lane >= HD)
        query = jnp.where(own, queries[:, cols], jnp.zeros((), BF16))
        scores = dot(query, keys[:, cols], NT) * HD ** (-0.5) + bias
        top = jnp.max(scores, axis=-1, keepdims=True)
        expos = jnp.exp(scores - top)
        total = jnp.sum(expos * times, axis=-1, keepdims=True)
        w_ref[h] = (expos / total).astype(BF16)


def attend_body(layout, dsh, n_ref, w_ref, nb_ref, nm_ref, *refs):
    pieces, (att_ref, scratch) = refs[:-2], refs[-2:]
    counts = counts_of(nb_ref, nm_ref, lax.axis_index("pix"))
    values = dot(n_ref[...], assembled(pieces, layout, scratch, dsh)).astype(BF16)
    lane = lax.broadcasted_iota(jnp.int32, (TILE, LANES), 1)
    for g in range(HEADS // 2):
        cols = slice(g * LANES, (g + 1) * LANES)
        halves = []
        for h in (2 * g, 2 * g + 1):
            total = jnp.zeros((TILE, LANES), F32)
            for i in range(3):
                rows = slice(i * TILE, (i + 1) * TILE)
                total = total + counts[i] * dot(w_ref[h, :, rows], values[rows, cols])
            halves.append(total)
        att_ref[:, cols] = jnp.where(lane < HD, halves[0], halves[1]).astype(BF16)


def forecast_body(layout, dsh, x_ref, att_ref, read_ref, *refs):
    pieces, (f_ref, wo_ref) = refs[:-2], refs[-2:]
    hidden = x_ref[0].astype(F32) + dot(att_ref[...], assembled(pieces, layout, wo_ref, dsh), NT)
    f_ref[...] = dot(hidden.astype(BF16), read_ref[...]).astype(BF16)


def sabs(a):
    mag = jnp.abs(a)
    return mag + 2.0 * BREADTH * jnp.log1p(jnp.exp(mag * (-1.0 / BREADTH)))


def backward_body(n_ens, factor, *refs):
    f_refs = refs[:n_ens]
    wo_ref, target_ref, lw_ref, read_ref, w_ref, nb_ref, nm_ref, gf_ref, con_ref = refs[n_ens:]
    position = lax.axis_index("pix")
    counts = counts_of(nb_ref, nm_ref, position)
    lw = lw_ref[...]
    target = target_ref[...]
    fc = [ref[...].astype(F32) for ref in f_refs]
    sums = [jnp.zeros((TILE, LANES), F32) for _ in range(n_ens)]
    for i in range(n_ens):
        for j in range(i + 1, n_ens):
            t = jnp.tanh((fc[i] - fc[j]) / (2.0 * BREADTH))
            sums[i] = sums[i] + t
            sums[j] = sums[j] - t
    for i in range(n_ens):
        t = jnp.tanh((fc[i] - target) / (2.0 * BREADTH))
        gf_ref[i * TILE : (i + 1) * TILE, :] = (lw * (t - sums[i] / (n_ens - 1)) * factor).astype(BF16)
    others = jnp.zeros((TILE, LANES), F32)
    for j in range(1, n_ens):
        others = others + sabs(fc[0] - fc[j])
    terms = lw * (sabs(fc[0] - target) - others / (2.0 * (n_ens - 1)))
    loss = jnp.full((16, LANES), jnp.sum(terms), F32)
    for i in range(con_ref.shape[1] // LANES):
        part = loss.astype(BF16)
        con_ref[3 * TILE :, i * LANES : (i + 1) * LANES] = part
        loss = loss - part.astype(F32)
    grad_hidden = dot(gf_ref[:TILE, :], read_ref[...], NT).astype(BF16)
    grad_att = dot(grad_hidden, wo_ref[...]).astype(BF16)
    lane = lax.broadcasted_iota(jnp.int32, (TILE, LANES), 1)
    zero = jnp.zeros((), BF16)
    for g in range(HEADS // 2):
        cols = slice(g * LANES, (g + 1) * LANES)
        pair = grad_att[:, cols]
        both = dot(w_ref[2 * g], jnp.where(lane < HD, pair, zero), TN)
        both = both + dot(w_ref[2 * g + 1], jnp.where(lane < HD, zero, pair), TN)
        for i in range(3):
            rows = slice(i * TILE, (i + 1) * TILE)
            con_ref[rows, cols] = (both[rows] * counts[i]).astype(BF16)


def value_body(blocks, dsh, rows, keep_ref, sib_ref, own_con, sib_con, v_ref, loss_ref):
    keys = 3 * TILE
    term = dot(keep_ref[...], own_con[:keys, :]) + dot(sib_ref[...], sib_con[:keys, :])
    parts = []
    for ref in (own_con, sib_con):
        part = ref[keys:, :].astype(F32)
        parts.append(part[:, :LANES] + part[:, LANES : 2 * LANES] + part[:, 2 * LANES : 3 * LANES])
    loss_ref[...] = (parts[0] + parts[1])[:8]
    for b in range(blocks):
        for cb in range(term.shape[1] // LANES):
            for first in range(0, dsh, rows):
                piece = (cb * dsh + first) // rows
                part = term[b * dsh + first : b * dsh + first + rows, cb * LANES : (cb + 1) * LANES]
                v_ref[b, piece % 2, piece // 2 * rows : (piece // 2 + 1) * rows, :] = part


def output_body(n_ens, dsh, gf_ref, read_ref, *refs):
    att_refs = refs[:n_ens]
    o_ref, scratch = refs[n_ens:]
    start = pl.multiple_of(lax.axis_index("ens") * dsh, dsh)
    for j in range(n_ens):
        scratch[j * TILE : (j + 1) * TILE, :] = att_refs[j][...]
    turned = dot(read_ref[pl.ds(start, dsh), :], gf_ref[...], NT).astype(BF16)
    term = dot(turned, scratch[...])
    for cb in range(term.shape[1] // LANES):
        o_ref[cb * dsh : (cb + 1) * dsh, :] = term[:, cb * LANES : (cb + 1) * LANES]


def finish_body(n_pix, dsh, scale, *refs):
    top = n_pix // 2
    pieces = refs[:top]
    total_ref, gv_ref, go_ref, loss_ref, scratch = refs[top:]
    loss_ref[...] = total_ref[:1, :1] * scale
    rows = scratch.shape[1] // n_pix
    position = lax.axis_index("pix") % top
    for j, ref in enumerate(pieces):
        for side in (0, 1):
            start = pl.multiple_of(((position ^ j) + side * top) * rows, rows)
            scratch[:, pl.ds(start, rows), :] = ref[:, side * rows : (side + 1) * rows, :].astype(F32)
    for cb in range(scratch.shape[1] // dsh):
        gv_ref[:, cb * LANES : (cb + 1) * LANES] = scratch[0, cb * dsh : (cb + 1) * dsh, :]
        go_ref[cb * LANES : (cb + 1) * LANES, :] = scratch[1, cb * dsh : (cb + 1) * dsh, :].T


def in_parts(total):
    first = lax.reduce_precision(total, 8, 7)
    return [first.astype(BF16), (total - first).astype(BF16)]


def with_loss(block, total):
    return jnp.concatenate([block.reshape(-1, LANES).astype(BF16)] + in_parts(total), axis=0)


def split_loss(message):
    parts = message[-16:].astype(F32).reshape(2, 8, LANES)
    return message[:-16], parts[0] + parts[1]


def gathered(value, axis, bits):
    pieces = {0: value}
    for bit in bits:
        held = lax.optimization_barrier(pieces)
        pieces = held | {j ^ bit: xor_permute(piece, axis, bit) for j, piece in held.items()}
    return pieces


def in_order(pieces):
    return [pieces[j] for j in sorted(pieces)]


def joined(arrays):
    return arrays[0] if len(arrays) == 1 else jnp.concatenate(arrays)


def both_cores(pieces):
    held = lax.optimization_barrier(pieces)
    return in_order(held | {j ^ 1: xor_permute(piece, "ens", 1) for j, piece in held.items()})


def at(blocks, index):
    return lax.dynamic_index_in_dim(blocks, index, 0, keepdims=False)


def part_of(split, index):
    return lax.dynamic_index_in_dim(split, index, 1, keepdims=False).reshape(-1, LANES)


def per_device(
    sample_layer_feed,
    gain,
    w_query,
    w_key,
    w_value,
    w_out,
    readout_matrix,
    target,
    pixel_weight,
    pix_mask,
    neighbours,
    neighbour_mask,
):
    n_ens, n_pix = lax.axis_size("ens"), lax.axis_size("pix")
    dsh, inner = w_query.shape
    d_model = dsh * n_ens
    n_out = readout_matrix.shape[1]
    ens_bits = [1 << b for b in reversed(range(n_ens.bit_length() - 1))]
    e, p = lax.axis_index("ens"), lax.axis_index("pix")
    rows = sample_layer_feed.shape[1]
    assert rows == TILE and n_out == LANES

    far = ens_bits[:-1]
    mask_rows = pix_mask.reshape(n_pix, TILE)
    half, side = dsh // 2, (p // 2) % 2
    w_vo = jnp.concatenate([w_value, w_out.T])

    def half_of(w):
        return jnp.where(side == 0, w[:half], w[half:])

    qk_far = gathered(jnp.concatenate([w_query, half_of(w_key)]), "ens", far)
    vo_far = gathered(w_vo, "ens", far)
    up = lax.ppermute(sample_layer_feed, "pix", [(i, i + 1) for i in range(n_pix - 1)])
    down = lax.ppermute(sample_layer_feed, "pix", [(i + 1, i) for i in range(n_pix - 1)])
    w_qk = jnp.concatenate([w_query, w_key])
    qk_near = xor_permute(w_qk, "ens", 1)
    turned = ((d_model // 2, 3 * TILE), BF16)
    normed, turned_keep, turned_send, lw = call(
        functools.partial(normed_body, n_ens, dsh),
        [((3 * TILE, d_model), BF16), turned, turned, ((TILE, LANES), F32)],
        [("v", sample_layer_feed), ("v", up), ("v", down), ("v", gain.reshape(1, -1))]
        + [("v", pixel_weight.reshape(1, TILE)), ("v", mask_rows)],
        10**7,
        "normed",
        scratch=[pltpu.VMEM((d_model, 3 * TILE), BF16)],
    )

    shards = sorted(j for j in qk_far if j)
    qk_far = [qk_far[j] for j in shards]
    k_far = joined([rows[dsh:] for rows in qk_far])
    k_other = xor_permute(k_far, "pix", 2)
    normed, qk_near, k_far, k_other, qk_far = lax.optimization_barrier((normed, qk_near, k_far, k_other, qk_far))
    q_far = joined([rows[:dsh] for rows in qk_far])
    q_cross = [xor_permute(part, "ens", 1) for part in jnp.split(q_far, 2 * len(shards))]
    k_cross, k_other_cross = xor_permute(k_far, "ens", 1), xor_permute(k_other, "ens", 1)
    parts = [q_far, k_far, k_other, k_cross, k_other_cross] + q_cross
    q_layout, k_layout = ([(0, m * dsh, dsh, 0, 0), (1, m * dsh, dsh, 1, 0)] for m in (0, 1))
    for i, j in enumerate(shards):
        q_layout.append((2, i * dsh, dsh, j, 0))
        q_layout += [(7 + 2 * i + m, 0, half, j ^ 1, m) for m in (0, 1)]
        k_layout += [(3 + m, i * half, half, j, 2 + m) for m in (0, 1)]
        k_layout += [(5 + m, i * half, half, j ^ 1, 2 + m) for m in (0, 1)]

    def layout(first):
        table = [(0, first, dsh, 0, 0), (1, 0, dsh, 1, 0)]
        for i, j in enumerate(shards):
            table += [(2, i * dsh, dsh, j, 0), (3, i * dsh, dsh, j ^ 1, 0)]
        return table

    full = pltpu.VMEM((d_model, inner), BF16)
    (weights,) = call(
        functools.partial(weights_body, q_layout, k_layout, dsh),
        [((HEADS, TILE, 3 * TILE), BF16)],
        [("v", normed), ("v", mask_rows), ("s", neighbours), ("s", neighbour_mask)]
        + [("v", a) for a in [w_qk, qk_near] + parts],
        10**3,
        "weights",
        scratch=[full],
    )
    weights, vo_far, turned_send, w_vo = lax.optimization_barrier((weights, vo_far, turned_send, w_vo))
    vo_near = [xor_permute(w_vo[:dsh], "ens", 1), xor_permute(w_vo[dsh:], "ens", 1)]
    vo_far = [joined([vo_far[j][m * dsh : (m + 1) * dsh] for j in shards]) for m in (0, 1)]
    vo_cross = [xor_permute(part, "ens", 1) for part in vo_far]
    turned_sib = xor_permute(turned_send, "ens", 1)
    (attended,) = call(
        functools.partial(attend_body, layout(0), dsh),
        [((TILE, inner), BF16)],
        [("v", normed), ("v", weights), ("s", neighbours), ("s", neighbour_mask)]
        + [("v", a) for a in (w_vo, vo_near[0], vo_far[0], vo_cross[0])],
        10**9,
        "attend",
        scratch=[full],
    )
    forecast, w_out_full = call(
        functools.partial(forecast_body, layout(dsh), dsh),
        [((TILE, LANES), BF16), ((d_model, inner), BF16)],
        [("v", sample_layer_feed), ("v", attended), ("v", readout_matrix)]
        + [("v", a) for a in (w_vo, vo_near[1], vo_far[1], vo_cross[1])],
        10**9,
        "forecast",
    )
    forecasts = in_order(gathered(forecast, "ens", ens_bits))
    forecast, attended = lax.optimization_barrier((forecast, attended))
    forecasts, turned_sib = lax.optimization_barrier((forecasts, turned_sib))
    attended_near = gathered(attended, "ens", far)

    factor = 1.0 / math.sqrt(n_ens * n_pix * TILE)
    grads, contrib = call(
        functools.partial(backward_body, n_ens, factor),
        [((n_ens * TILE, LANES), BF16), ((3 * TILE + 16, inner), BF16)],
        [("v", a) for a in forecasts + [w_out_full]]
        + [("v", target), ("v", lw), ("v", readout_matrix)]
        + [("v", weights), ("s", neighbours), ("s", neighbour_mask)],
        10**9,
        "backward",
    )
    contrib, attended_near = lax.optimization_barrier((contrib, attended_near))
    contrib_sib = xor_permute(contrib, "ens", 1)
    attended_all = both_cores(attended_near)
    blocks = n_ens // 2
    value_term, loss = call(
        functools.partial(value_body, blocks, dsh, dsh * inner // (LANES * n_pix)),
        [((blocks, 2, dsh * inner // (2 * LANES), LANES), F32), ((8, LANES), F32)],
        [("v", turned_keep), ("v", turned_sib), ("v", contrib), ("v", contrib_sib)],
        10**9,
        "value_term",
    )
    value_term, loss, grads = lax.optimization_barrier((value_term, loss, grads))
    (output_term,) = call(
        functools.partial(output_body, n_ens, dsh),
        [((dsh * inner // LANES, LANES), F32)],
        [("v", grads), ("v", readout_matrix)] + [("v", a) for a in attended_all],
        10**9,
        "output_term",
        scratch=[pltpu.VMEM((n_ens * TILE, inner), BF16)],
    )

    for bit in far[:-1]:
        upper = (e // bit) % 2
        halves = value_term.reshape(2, -1, LANES)
        got, other = split_loss(xor_permute(with_loss(at(halves, 1 - upper), loss), "ens", bit))
        value_term = at(halves, upper) + got.astype(F32)
        loss = loss + other

    n_bits = n_pix.bit_length() - 1
    groups = [[1]] + [[1 << b for b in range(s, min(s + 2, n_bits))] for s in range(1, n_bits, 2)]

    def pieces_of(term, group, higher=None):
        size = 1 << len(group)
        higher = n_pix // (group[0] * size) if higher is None else higher
        return term.reshape(higher, size, -1, LANES)

    def exchanged(messages, group):
        return [xor_permute(m, "pix", (d + 1) * group[0]) for d, m in enumerate(messages)]

    def sent(term, group, total=None, higher=None):
        size, pos = 1 << len(group), (p // group[0]) % (1 << len(group))
        split = pieces_of(term, group, higher)
        messages = [part_of(split, pos ^ d).astype(BF16) for d in range(1, size)]
        if total is not None:
            messages = [with_loss(m, total) for m in messages]
        return part_of(split, pos), exchanged(messages, group)

    def added(kept, received):
        return functools.reduce(jnp.add, [m.astype(F32) for m in received], kept)

    later = [bit for group in groups[1:] for bit in group]
    for bit in later[:-2]:
        output_term = added(*sent(output_term, [bit]))
    output_kept, output_got = sent(output_term, [later[-2]])
    upper, low = (e // far[-1]) % 2, p % 2
    quarters = value_term.reshape(4, -1, LANES)
    pos = 2 * upper + low
    received = []
    for d in (2, 1, 3):
        pairs = [
            (i * n_pix + k, (i ^ (far[-1] * (d // 2))) * n_pix + (k ^ (d % 2)))
            for i in range(n_ens)
            for k in range(n_pix)
        ]
        message = with_loss(at(quarters, pos ^ d), loss)
        received.append((d, split_loss(lax.ppermute(message, ("ens", "pix"), pairs))))
    value_term = at(quarters, pos)
    losses = {0: loss}
    for d, (block, other) in received:
        value_term = value_term + block.astype(F32)
        losses[d] = other
    losses = jnp.stack([losses[d] for d in range(4)])
    loss = functools.reduce(jnp.add, [at(losses, pos ^ i) for i in range(4)])

    value_term, output_got = lax.optimization_barrier((value_term, output_got))
    output_kept, output_got = sent(added(output_kept, output_got), groups[0], higher=2)
    for bit in later[:-1]:
        kept, received = sent(value_term, [bit], loss)
        block, other = split_loss(received[0])
        value_term, loss = added(kept, [block]), loss + other
    output_term = added(output_kept, output_got)
    both = jnp.concatenate([value_term, output_term]).astype(BF16)
    block, other = split_loss(xor_permute(with_loss(both, loss), "pix", later[-1]))
    loss = loss + other
    both = (both.astype(F32) + block.astype(F32)).astype(BF16)
    pieces = {0: both.reshape(2, -1, LANES)}
    rest = [1] + later[:-1]
    for stage in reversed([rest[i : i + 2] for i in range(0, len(rest), 2)]):
        keys = sorted(pieces)
        stack = pieces[0][None] if len(keys) == 1 else jnp.stack([pieces[j] for j in keys])
        for d in range(1, 1 << len(stage)):
            got = xor_permute(stack, "pix", d * stage[0])
            pieces.update({j ^ (d * stage[0]): got[i] for i, j in enumerate(keys)})
    scale = 1.0 / (n_ens * n_pix * TILE * n_out)
    grad_w_value, grad_w_out, loss = call(
        functools.partial(finish_body, n_pix, dsh, scale),
        [((dsh, inner), F32), ((inner, dsh), F32), ((1, 1), F32)],
        [("v", pieces[j]) for j in sorted(pieces)] + [("v", loss)],
        10**6,
        "finish",
        scratch=[pltpu.VMEM((2, dsh * inner // LANES, LANES), F32)],
    )
    return (loss.reshape(()), grad_w_out, grad_w_value)


def solution(mesh):
    in_specs = (
        P("ens", "pix", None),
        P(),
        P("ens", None),
        P("ens", None),
        P("ens", None),
        P(None, "ens"),
        P(),
        P("pix", None),
        P("pix"),
        P(),
        P("pix", None),
        P("pix", None),
    )
    out_specs = (P(), P(None, "ens"), P("ens", None))
    return jax.shard_map(
        per_device, mesh=mesh, in_specs=in_specs, out_specs=out_specs, check_vma=False
    )
```

```python
import functools
import math

import jax
import jax.numpy as jnp
from jax import lax
from jax.experimental import pallas as pl
from jax.experimental.pallas import tpu as pltpu
from jax.sharding import PartitionSpec as P

HEADS = 8
HD = 64
TILE = 128
NB = 9
LANES = 128
EPS = 1e-06
BREADTH = 0.1

F32 = jnp.float32
BF16 = jnp.bfloat16
VMEM = pl.BlockSpec(memory_space=pltpu.VMEM)
SMEM = pl.BlockSpec(memory_space=pltpu.SMEM)
NN = (((1,), (0,)), ((), ()))
NT = (((1,), (1,)), ((), ()))
TN = (((0,), (0,)), ((), ()))


def dot(a, b, dims=NN):
    return lax.dot_general(a, b, dims, preferred_element_type=F32)


def call(body, outs, ins, flops, name, scratch=(), vmem=32):
    specs = [SMEM if s == "s" else VMEM for s, _ in ins]
    return pl.pallas_call(
        body,
        out_shape=[jax.ShapeDtypeStruct(s, d) for s, d in outs],
        in_specs=specs,
        out_specs=[VMEM] * len(outs),
        scratch_shapes=list(scratch),
        compiler_params=pltpu.CompilerParams(vmem_limit_bytes=vmem * 2**20),
        cost_estimate=pl.CostEstimate(flops=flops, bytes_accessed=flops // 1000, transcendentals=0),
        name=name,
    )(*[a for _, a in ins])


def xor_permute(value, axis, mask):
    size = lax.axis_size(axis)
    return lax.ppermute(value, axis, [(i, i ^ mask) for i in range(size)])


def counts_of(nb_ref, nm_ref, position):
    counts = []
    for d in (-1, 0, 1):
        total = jnp.int32(0)
        for s in range(NB):
            hit = (nb_ref[0, s] == position + d) & (nm_ref[0, s] > 0)
            total = total + jnp.where(hit, 1, 0)
        counts.append(total.astype(F32))
    return counts


def normed_body(
    n_ens, dsh, x_ref, up_ref, down_ref, gain_ref, pw_ref, mask_ref, nb_ref, nm_ref, *refs
):
    n_ref, keep_ref, send_ref, lw_ref, rows_ref, turned_ref = refs
    core, position = lax.axis_index("ens") % 2, lax.axis_index("pix")
    counts = counts_of(nb_ref, nm_ref, position)
    for i, d in enumerate((-1, 0, 1)):
        row = jnp.clip(position + d, 0, mask_ref.shape[0] - 1)
        named = jnp.full((1, TILE), counts[i], F32)
        cols = slice(i * TILE, (i + 1) * TILE)
        rows_ref[0:1, cols] = jnp.where(mask_ref[pl.ds(row, 1), :] > 0, named, 0.0)
        rows_ref[1:2, cols] = named
    rows_ref[2:, :] = jnp.zeros((6, 3 * TILE), F32)
    live = jnp.where(mask_ref[pl.ds(position, 1), :] > 0, 1.0, 0.0)
    lw_ref[...] = jnp.broadcast_to(pw_ref[...] * live, (LANES, TILE)).T
    gain = gain_ref[...]
    for i, ref in enumerate((up_ref, x_ref, down_ref)):
        rows = ref[0].astype(F32)
        inv = lax.rsqrt(jnp.mean(rows * rows, axis=-1, keepdims=True) + EPS)
        n_ref[i * TILE : (i + 1) * TILE, :] = (rows * inv * gain).astype(BF16)
    turned_ref[...] = n_ref[...].T
    for b in range(n_ens // 2):
        mine = pl.multiple_of((2 * b + core) * dsh, dsh)
        theirs = pl.multiple_of((2 * b + 1 - core) * dsh, dsh)
        keep_ref[b * dsh : (b + 1) * dsh, :] = turned_ref[pl.ds(mine, dsh), :]
        send_ref[b * dsh : (b + 1) * dsh, :] = turned_ref[pl.ds(theirs, dsh), :]


def assembled(refs, layout, scratch, dsh):
    me, side = lax.axis_index("ens"), (lax.axis_index("pix") // 2) % 2
    for which, first, rows, j, place in layout:
        offset = place * rows if place < 2 else (side ^ (place - 2)) * rows
        start = pl.multiple_of((me ^ j) * dsh + offset, rows)
        scratch[pl.ds(start, rows), :] = refs[which][first : first + rows, :]
    return scratch[...]


def weights_body(q_layout, k_layout, dsh, n_ref, rows_ref, *refs):
    pieces, (w_ref, scratch) = refs[:-2], refs[-2:]
    times = rows_ref[0:1, :]
    bias = jnp.where(times > 0, 0.0, -1e30)
    queries = dot(n_ref[TILE : 2 * TILE, :], assembled(pieces, q_layout, scratch, dsh)).astype(BF16)
    keys = dot(n_ref[...], assembled(pieces, k_layout, scratch, dsh)).astype(BF16)
    lane = lax.broadcasted_iota(jnp.int32, (TILE, LANES), 1)
    zero = jnp.zeros((), BF16)
    for g in range(HEADS // 2):
        cols = slice(g * LANES, (g + 1) * LANES)
        pair = queries[:, cols]
        pair = jnp.concatenate([jnp.where(lane < HD, pair, zero), jnp.where(lane < HD, zero, pair)], axis=0)
        scores = dot(pair, keys[:, cols], NT) * HD ** (-0.5) + bias
        top = jnp.max(scores, axis=-1, keepdims=True)
        expos = jnp.exp(scores - top)
        total = jnp.sum(expos * times, axis=-1, keepdims=True)
        w_ref[2 * g : 2 * g + 2] = (expos / total).astype(BF16).reshape(2, TILE, 3 * TILE)


def attend_body(layout, dsh, n_ref, w_ref, rows_ref, *refs):
    pieces, (att_ref, scratch) = refs[:-2], refs[-2:]
    values = dot(n_ref[...], assembled(pieces, layout, scratch, dsh)).astype(BF16)
    lane = lax.broadcasted_iota(jnp.int32, (TILE, LANES), 1)
    for g in range(HEADS // 2):
        cols = slice(g * LANES, (g + 1) * LANES)
        pair = w_ref[2 * g : 2 * g + 2].reshape(2 * TILE, 3 * TILE)
        total = jnp.zeros((2 * TILE, LANES), F32)
        for i in range(3):
            rows = slice(i * TILE, (i + 1) * TILE)
            total = total + rows_ref[1:2, rows] * dot(pair[:, rows], values[rows, cols])
        att_ref[:, cols] = jnp.where(lane < HD, total[:TILE], total[TILE:]).astype(BF16)


def forecast_body(layout, dsh, x_ref, att_ref, read_ref, *refs):
    pieces, (f_ref, wo_ref) = refs[:-2], refs[-2:]
    hidden = x_ref[0].astype(F32) + dot(att_ref[...], assembled(pieces, layout, wo_ref, dsh), NT)
    f_ref[...] = dot(hidden.astype(BF16), read_ref[...]).astype(BF16)


def sabs(a):
    mag = jnp.abs(a)
    return mag + 2.0 * BREADTH * jnp.log1p(jnp.exp(mag * (-1.0 / BREADTH)))


def backward_body(n_ens, factor, *refs):
    f_refs = refs[:n_ens]
    wo_ref, target_ref, lw_ref, read_ref, w_ref, rows_ref, gf_ref, con_ref = refs[n_ens:]
    lw = lw_ref[...]
    target = target_ref[...]
    fc = [ref[...].astype(F32) for ref in f_refs]
    sums = [jnp.zeros((TILE, LANES), F32) for _ in range(n_ens)]
    for i in range(n_ens):
        for j in range(i + 1, n_ens):
            t = jnp.tanh((fc[i] - fc[j]) / (2.0 * BREADTH))
            sums[i] = sums[i] + t
            sums[j] = sums[j] - t
    for i in range(n_ens):
        t = jnp.tanh((fc[i] - target) / (2.0 * BREADTH))
        gf_ref[i * TILE : (i + 1) * TILE, :] = (lw * (t - sums[i] / (n_ens - 1)) * factor).astype(BF16)
    others = jnp.zeros((TILE, LANES), F32)
    for j in range(1, n_ens):
        others = others + sabs(fc[0] - fc[j])
    terms = lw * (sabs(fc[0] - target) - others / (2.0 * (n_ens - 1)))
    loss = jnp.full((16, LANES), jnp.sum(terms), F32)
    for i in range(con_ref.shape[1] // LANES):
        part = loss.astype(BF16)
        con_ref[3 * TILE :, i * LANES : (i + 1) * LANES] = part
        loss = loss - part.astype(F32)
    grad_hidden = dot(gf_ref[:TILE, :], read_ref[...], NT).astype(BF16)
    grad_att = dot(grad_hidden, wo_ref[...]).astype(BF16)
    lane = lax.broadcasted_iota(jnp.int32, (TILE, LANES), 1)
    zero = jnp.zeros((), BF16)
    for g in range(HEADS // 2):
        cols = slice(g * LANES, (g + 1) * LANES)
        pair = grad_att[:, cols]
        pair = jnp.concatenate([jnp.where(lane < HD, pair, zero), jnp.where(lane < HD, zero, pair)], axis=0)
        both = dot(w_ref[2 * g : 2 * g + 2].reshape(2 * TILE, 3 * TILE), pair, TN)
        for i in range(3):
            rows = slice(i * TILE, (i + 1) * TILE)
            con_ref[rows, cols] = (both[rows] * rows_ref[1:2, rows]).astype(BF16)


def value_body(blocks, dsh, rows, keep_ref, sib_ref, own_con, sib_con, v_ref, loss_ref):
    keys = 3 * TILE
    term = dot(keep_ref[...], own_con[:keys, :]) + dot(sib_ref[...], sib_con[:keys, :])
    parts = []
    for ref in (own_con, sib_con):
        part = ref[keys:, :].astype(F32)
        parts.append(part[:, :LANES] + part[:, LANES : 2 * LANES] + part[:, 2 * LANES : 3 * LANES])
    loss_ref[...] = (parts[0] + parts[1])[:8]
    for b in range(blocks):
        for cb in range(term.shape[1] // LANES):
            for first in range(0, dsh, rows):
                piece = (cb * dsh + first) // rows
                part = term[b * dsh + first : b * dsh + first + rows, cb * LANES : (cb + 1) * LANES]
                v_ref[b, piece % 2, piece // 2 * rows : (piece // 2 + 1) * rows, :] = part


def output_body(n_ens, dsh, gf_ref, read_ref, *refs):
    att_refs = refs[:n_ens]
    o_ref, scratch = refs[n_ens:]
    start = pl.multiple_of(lax.axis_index("ens") * dsh, dsh)
    for j in range(n_ens):
        scratch[j * TILE : (j + 1) * TILE, :] = att_refs[j][...]
    turned = dot(read_ref[pl.ds(start, dsh), :], gf_ref[...], NT).astype(BF16)
    term = dot(turned, scratch[...])
    for cb in range(term.shape[1] // LANES):
        o_ref[cb * dsh : (cb + 1) * dsh, :] = term[:, cb * LANES : (cb + 1) * LANES]


def finish_body(n_pix, dsh, scale, *refs):
    top = n_pix // 2
    pieces = refs[:top]
    total_ref, gv_ref, go_ref, loss_ref, scratch = refs[top:]
    loss_ref[...] = total_ref[:1, :1] * scale
    rows = scratch.shape[1] // n_pix
    position = lax.axis_index("pix") % top
    for j, ref in enumerate(pieces):
        for side in (0, 1):
            start = pl.multiple_of(((position ^ j) + side * top) * rows, rows)
            scratch[:, pl.ds(start, rows), :] = ref[:, side * rows : (side + 1) * rows, :].astype(F32)
    for cb in range(scratch.shape[1] // dsh):
        gv_ref[:, cb * LANES : (cb + 1) * LANES] = scratch[0, cb * dsh : (cb + 1) * dsh, :]
        go_ref[cb * LANES : (cb + 1) * LANES, :] = scratch[1, cb * dsh : (cb + 1) * dsh, :].T


def in_parts(total):
    first = lax.reduce_precision(total, 8, 7)
    return [first.astype(BF16), (total - first).astype(BF16)]


def with_loss(block, total):
    return jnp.concatenate([block.reshape(-1, LANES).astype(BF16)] + in_parts(total), axis=0)


def split_loss(message):
    parts = message[-16:].astype(F32).reshape(2, 8, LANES)
    return message[:-16], parts[0] + parts[1]


def gathered(value, axis, bits):
    pieces = {0: value}
    for bit in bits:
        held = lax.optimization_barrier(pieces)
        pieces = held | {j ^ bit: xor_permute(piece, axis, bit) for j, piece in held.items()}
    return pieces


def in_order(pieces):
    return [pieces[j] for j in sorted(pieces)]


def joined(arrays):
    return arrays[0] if len(arrays) == 1 else jnp.concatenate(arrays)


def both_cores(pieces):
    held = lax.optimization_barrier(pieces)
    return in_order(held | {j ^ 1: xor_permute(piece, "ens", 1) for j, piece in held.items()})


def at(blocks, index):
    return lax.dynamic_index_in_dim(blocks, index, 0, keepdims=False)


def part_of(split, index):
    return lax.dynamic_index_in_dim(split, index, 1, keepdims=False).reshape(-1, LANES)


def per_device(
    sample_layer_feed,
    gain,
    w_query,
    w_key,
    w_value,
    w_out,
    readout_matrix,
    target,
    pixel_weight,
    pix_mask,
    neighbours,
    neighbour_mask,
):
    n_ens, n_pix = lax.axis_size("ens"), lax.axis_size("pix")
    dsh, inner = w_query.shape
    d_model = dsh * n_ens
    n_out = readout_matrix.shape[1]
    ens_bits = [1 << b for b in reversed(range(n_ens.bit_length() - 1))]
    e, p = lax.axis_index("ens"), lax.axis_index("pix")
    rows = sample_layer_feed.shape[1]
    assert rows == TILE and n_out == LANES

    far = ens_bits[:-1]
    mask_rows = pix_mask.reshape(n_pix, TILE)
    half, side = dsh // 2, (p // 2) % 2
    w_vo = jnp.concatenate([w_value, w_out.T])

    def half_of(w):
        return jnp.where(side == 0, w[:half], w[half:])

    qk_far = gathered(jnp.concatenate([w_query, half_of(w_key)]), "ens", far)
    vo_far = gathered(w_vo, "ens", far)
    up = lax.ppermute(sample_layer_feed, "pix", [(i, i + 1) for i in range(n_pix - 1)])
    down = lax.ppermute(sample_layer_feed, "pix", [(i + 1, i) for i in range(n_pix - 1)])
    w_qk = jnp.concatenate([w_query, w_key])
    qk_near = xor_permute(w_qk, "ens", 1)
    turned = ((d_model // 2, 3 * TILE), BF16)
    normed, turned_keep, turned_send, lw, key_rows = call(
        functools.partial(normed_body, n_ens, dsh),
        [((3 * TILE, d_model), BF16), turned, turned, ((TILE, LANES), F32), ((8, 3 * TILE), F32)],
        [("v", sample_layer_feed), ("v", up), ("v", down), ("v", gain.reshape(1, -1))]
        + [("v", pixel_weight.reshape(1, TILE)), ("v", mask_rows), ("s", neighbours), ("s", neighbour_mask)],
        10**7,
        "normed",
        scratch=[pltpu.VMEM((d_model, 3 * TILE), BF16)],
    )

    shards = sorted(j for j in qk_far if j)
    qk_far = [qk_far[j] for j in shards]
    k_far = joined([rows[dsh:] for rows in qk_far])
    k_other = xor_permute(k_far, "pix", 2)
    normed, qk_near, k_far, k_other, qk_far = lax.optimization_barrier((normed, qk_near, k_far, k_other, qk_far))
    q_far = joined([rows[:dsh] for rows in qk_far])
    q_cross = [xor_permute(part, "ens", 1) for part in jnp.split(q_far, 2 * len(shards))]
    k_cross, k_other_cross = xor_permute(k_far, "ens", 1), xor_permute(k_other, "ens", 1)
    parts = [q_far, k_far, k_other, k_cross, k_other_cross] + q_cross
    q_layout, k_layout = ([(0, m * dsh, dsh, 0, 0), (1, m * dsh, dsh, 1, 0)] for m in (0, 1))
    for i, j in enumerate(shards):
        q_layout.append((2, i * dsh, dsh, j, 0))
        q_layout += [(7 + 2 * i + m, 0, half, j ^ 1, m) for m in (0, 1)]
        k_layout += [(3 + m, i * half, half, j, 2 + m) for m in (0, 1)]
        k_layout += [(5 + m, i * half, half, j ^ 1, 2 + m) for m in (0, 1)]

    def layout(first):
        table = [(0, first, dsh, 0, 0), (1, 0, dsh, 1, 0)]
        for i, j in enumerate(shards):
            table += [(2, i * dsh, dsh, j, 0), (3, i * dsh, dsh, j ^ 1, 0)]
        return table

    full = pltpu.VMEM((d_model, inner), BF16)
    (weights,) = call(
        functools.partial(weights_body, q_layout, k_layout, dsh),
        [((HEADS, TILE, 3 * TILE), BF16)],
        [("v", normed), ("v", key_rows)]
        + [("v", a) for a in [w_qk, qk_near] + parts],
        10**3,
        "weights",
        scratch=[full],
    )
    weights, vo_far, turned_send, w_vo = lax.optimization_barrier((weights, vo_far, turned_send, w_vo))
    vo_near = [xor_permute(w_vo[:dsh], "ens", 1), xor_permute(w_vo[dsh:], "ens", 1)]
    vo_far = [joined([vo_far[j][m * dsh : (m + 1) * dsh] for j in shards]) for m in (0, 1)]
    vo_cross = [xor_permute(part, "ens", 1) for part in vo_far]
    turned_sib = xor_permute(turned_send, "ens", 1)
    (attended,) = call(
        functools.partial(attend_body, layout(0), dsh),
        [((TILE, inner), BF16)],
        [("v", normed), ("v", weights), ("v", key_rows)]
        + [("v", a) for a in (w_vo, vo_near[0], vo_far[0], vo_cross[0])],
        10**9,
        "attend",
        scratch=[full],
    )
    forecast, w_out_full = call(
        functools.partial(forecast_body, layout(dsh), dsh),
        [((TILE, LANES), BF16), ((d_model, inner), BF16)],
        [("v", sample_layer_feed), ("v", attended), ("v", readout_matrix)]
        + [("v", a) for a in (w_vo, vo_near[1], vo_far[1], vo_cross[1])],
        10**9,
        "forecast",
    )
    forecasts = in_order(gathered(forecast, "ens", ens_bits))
    forecast, attended = lax.optimization_barrier((forecast, attended))
    forecasts, turned_sib = lax.optimization_barrier((forecasts, turned_sib))
    attended_near = gathered(attended, "ens", far)

    factor = 1.0 / math.sqrt(n_ens * n_pix * TILE)
    grads, contrib = call(
        functools.partial(backward_body, n_ens, factor),
        [((n_ens * TILE, LANES), BF16), ((3 * TILE + 16, inner), BF16)],
        [("v", a) for a in forecasts + [w_out_full]]
        + [("v", target), ("v", lw), ("v", readout_matrix)]
        + [("v", weights), ("v", key_rows)],
        10**9,
        "backward",
    )
    contrib, attended_near = lax.optimization_barrier((contrib, attended_near))
    contrib_sib = xor_permute(contrib, "ens", 1)
    attended_all = both_cores(attended_near)
    blocks = n_ens // 2
    value_term, loss = call(
        functools.partial(value_body, blocks, dsh, dsh * inner // (LANES * n_pix)),
        [((blocks, 2, dsh * inner // (2 * LANES), LANES), F32), ((8, LANES), F32)],
        [("v", turned_keep), ("v", turned_sib), ("v", contrib), ("v", contrib_sib)],
        10**9,
        "value_term",
    )
    value_term, loss, grads = lax.optimization_barrier((value_term, loss, grads))
    (output_term,) = call(
        functools.partial(output_body, n_ens, dsh),
        [((dsh * inner // LANES, LANES), F32)],
        [("v", grads), ("v", readout_matrix)] + [("v", a) for a in attended_all],
        10**9,
        "output_term",
        scratch=[pltpu.VMEM((n_ens * TILE, inner), BF16)],
    )

    for bit in far[:-1]:
        upper = (e // bit) % 2
        halves = value_term.reshape(2, -1, LANES)
        got, other = split_loss(xor_permute(with_loss(at(halves, 1 - upper), loss), "ens", bit))
        value_term = at(halves, upper) + got.astype(F32)
        loss = loss + other

    n_bits = n_pix.bit_length() - 1
    groups = [[1]] + [[1 << b for b in range(s, min(s + 2, n_bits))] for s in range(1, n_bits, 2)]

    def pieces_of(term, group, higher=None):
        size = 1 << len(group)
        higher = n_pix // (group[0] * size) if higher is None else higher
        return term.reshape(higher, size, -1, LANES)

    def exchanged(messages, group):
        return [xor_permute(m, "pix", (d + 1) * group[0]) for d, m in enumerate(messages)]

    def sent(term, group, total=None, higher=None):
        size, pos = 1 << len(group), (p // group[0]) % (1 << len(group))
        split = pieces_of(term, group, higher)
        messages = [part_of(split, pos ^ d).astype(BF16) for d in range(1, size)]
        if total is not None:
            messages = [with_loss(m, total) for m in messages]
        return part_of(split, pos), exchanged(messages, group)

    def added(kept, received):
        return functools.reduce(jnp.add, [m.astype(F32) for m in received], kept)

    later = [bit for group in groups[1:] for bit in group]
    for bit in later[:-2]:
        output_term = added(*sent(output_term, [bit]))
    output_kept, output_got = sent(output_term, [later[-2]])
    upper, low = (e // far[-1]) % 2, p % 2
    quarters = value_term.reshape(4, -1, LANES)
    pos = 2 * upper + low
    received = []
    for d in (2, 1, 3):
        pairs = [
            (i * n_pix + k, (i ^ (far[-1] * (d // 2))) * n_pix + (k ^ (d % 2)))
            for i in range(n_ens)
            for k in range(n_pix)
        ]
        message = with_loss(at(quarters, pos ^ d), loss)
        received.append((d, split_loss(lax.ppermute(message, ("ens", "pix"), pairs))))
    value_term = at(quarters, pos)
    losses = {0: loss}
    for d, (block, other) in received:
        value_term = value_term + block.astype(F32)
        losses[d] = other
    losses = jnp.stack([losses[d] for d in range(4)])
    loss = functools.reduce(jnp.add, [at(losses, pos ^ i) for i in range(4)])

    value_term, output_got = lax.optimization_barrier((value_term, output_got))
    output_kept, output_got = sent(added(output_kept, output_got), groups[0], higher=2)
    for bit in later[:-1]:
        kept, received = sent(value_term, [bit], loss)
        block, other = split_loss(received[0])
        value_term, loss = added(kept, [block]), loss + other
    output_term = added(output_kept, output_got)
    both = jnp.concatenate([value_term, output_term]).astype(BF16)
    block, other = split_loss(xor_permute(with_loss(both, loss), "pix", later[-1]))
    loss = loss + other
    both = (both.astype(F32) + block.astype(F32)).astype(BF16)
    pieces = {0: both.reshape(2, -1, LANES)}
    rest = [1] + later[:-1]
    for stage in reversed([rest[i : i + 2] for i in range(0, len(rest), 2)]):
        keys = sorted(pieces)
        stack = pieces[0][None] if len(keys) == 1 else jnp.stack([pieces[j] for j in keys])
        for d in range(1, 1 << len(stage)):
            got = xor_permute(stack, "pix", d * stage[0])
            pieces.update({j ^ (d * stage[0]): got[i] for i, j in enumerate(keys)})
    scale = 1.0 / (n_ens * n_pix * TILE * n_out)
    grad_w_value, grad_w_out, loss = call(
        functools.partial(finish_body, n_pix, dsh, scale),
        [((dsh, inner), F32), ((inner, dsh), F32), ((1, 1), F32)],
        [("v", pieces[j]) for j in sorted(pieces)] + [("v", loss)],
        10**6,
        "finish",
        scratch=[pltpu.VMEM((2, dsh * inner // LANES, LANES), F32)],
    )
    return (loss.reshape(()), grad_w_out, grad_w_value)


def solution(mesh):
    in_specs = (
        P("ens", "pix", None),
        P(),
        P("ens", None),
        P("ens", None),
        P("ens", None),
        P(None, "ens"),
        P(),
        P("pix", None),
        P("pix"),
        P(),
        P("pix", None),
        P("pix", None),
    )
    out_specs = (P(), P(None, "ens"), P("ens", None))
    return jax.shard_map(
        per_device, mesh=mesh, in_specs=in_specs, out_specs=out_specs, check_vma=False
    )
```

```python
import functools
import math

import jax
import jax.numpy as jnp
from jax import lax
from jax.experimental import pallas as pl
from jax.experimental.pallas import tpu as pltpu
from jax.sharding import PartitionSpec as P

HEADS = 8
HD = 64
TILE = 128
NB = 9
LANES = 128
EPS = 1e-06
BREADTH = 0.1

F32 = jnp.float32
BF16 = jnp.bfloat16
VMEM = pl.BlockSpec(memory_space=pltpu.VMEM)
SMEM = pl.BlockSpec(memory_space=pltpu.SMEM)
NN = (((1,), (0,)), ((), ()))
NT = (((1,), (1,)), ((), ()))
TN = (((0,), (0,)), ((), ()))


def dot(a, b, dims=NN):
    return lax.dot_general(a, b, dims, preferred_element_type=F32)


def call(body, outs, ins, flops, name, scratch=(), vmem=32):
    specs = [SMEM if s == "s" else VMEM for s, _ in ins]
    return pl.pallas_call(
        body,
        out_shape=[jax.ShapeDtypeStruct(s, d) for s, d in outs],
        in_specs=specs,
        out_specs=[VMEM] * len(outs),
        scratch_shapes=list(scratch),
        compiler_params=pltpu.CompilerParams(vmem_limit_bytes=vmem * 2**20),
        cost_estimate=pl.CostEstimate(flops=flops, bytes_accessed=flops // 1000, transcendentals=0),
        name=name,
    )(*[a for _, a in ins])


def xor_permute(value, axis, mask):
    size = lax.axis_size(axis)
    return lax.ppermute(value, axis, [(i, i ^ mask) for i in range(size)])


def counts_of(nb_ref, nm_ref, position):
    counts = []
    for d in (-1, 0, 1):
        total = jnp.int32(0)
        for s in range(NB):
            hit = (nb_ref[0, s] == position + d) & (nm_ref[0, s] > 0)
            total = total + jnp.where(hit, 1, 0)
        counts.append(total.astype(F32))
    return counts


def normed_body(
    n_ens, dsh, x_ref, up_ref, down_ref, gain_ref, pw_ref, mask_ref, nb_ref, nm_ref, *refs
):
    n_ref, keep_ref, send_ref, lw_ref, rows_ref, turned_ref = refs
    core, position = lax.axis_index("ens") % 2, lax.axis_index("pix")
    counts = counts_of(nb_ref, nm_ref, position)
    for i, d in enumerate((-1, 0, 1)):
        row = jnp.clip(position + d, 0, mask_ref.shape[0] - 1)
        named = jnp.full((1, TILE), counts[i], F32)
        cols = slice(i * TILE, (i + 1) * TILE)
        rows_ref[0:1, cols] = jnp.where(mask_ref[pl.ds(row, 1), :] > 0, named, 0.0)
        rows_ref[1:2, cols] = named
    rows_ref[2:, :] = jnp.zeros((6, 3 * TILE), F32)
    live = jnp.where(mask_ref[pl.ds(position, 1), :] > 0, 1.0, 0.0)
    lw_ref[...] = jnp.broadcast_to(pw_ref[...] * live, (LANES, TILE)).T
    gain = gain_ref[...]
    for i, ref in enumerate((up_ref, x_ref, down_ref)):
        rows = ref[0].astype(F32)
        inv = lax.rsqrt(jnp.mean(rows * rows, axis=-1, keepdims=True) + EPS)
        n_ref[i * TILE : (i + 1) * TILE, :] = (rows * inv * gain).astype(BF16)
    turned_ref[...] = n_ref[...].T
    for b in range(n_ens // 2):
        mine = pl.multiple_of((2 * b + core) * dsh, dsh)
        theirs = pl.multiple_of((2 * b + 1 - core) * dsh, dsh)
        keep_ref[b * dsh : (b + 1) * dsh, :] = turned_ref[pl.ds(mine, dsh), :]
        send_ref[b * dsh : (b + 1) * dsh, :] = turned_ref[pl.ds(theirs, dsh), :]


def assembled(refs, layout, scratch, dsh):
    me, side = lax.axis_index("ens"), (lax.axis_index("pix") // 2) % 2
    for which, first, rows, j, place in layout:
        offset = place * rows if place < 2 else (side ^ (place - 2)) * rows
        start = pl.multiple_of((me ^ j) * dsh + offset, rows)
        scratch[pl.ds(start, rows), :] = refs[which][first : first + rows, :]
    return scratch[...]


def weights_body(q_layout, k_layout, dsh, n_ref, rows_ref, *refs):
    pieces, (w_ref, scratch) = refs[:-2], refs[-2:]
    times = rows_ref[0:1, :]
    bias = jnp.where(times > 0, 0.0, -1e30)
    queries = dot(n_ref[TILE : 2 * TILE, :], assembled(pieces, q_layout, scratch, dsh)).astype(BF16)
    keys = dot(n_ref[...], assembled(pieces, k_layout, scratch, dsh)).astype(BF16)
    lane = lax.broadcasted_iota(jnp.int32, (TILE, LANES), 1)
    zero = jnp.zeros((), BF16)
    for g in range(HEADS // 2):
        cols = slice(g * LANES, (g + 1) * LANES)
        pair = queries[:, cols]
        pair = jnp.concatenate([jnp.where(lane < HD, pair, zero), jnp.where(lane < HD, zero, pair)], axis=0)
        scores = dot(pair, keys[:, cols], NT) * HD ** (-0.5) + bias
        top = jnp.max(scores, axis=-1, keepdims=True)
        expos = jnp.exp(scores - top)
        total = jnp.sum(expos * times, axis=-1, keepdims=True)
        w_ref[2 * g : 2 * g + 2] = (expos / total).astype(BF16).reshape(2, TILE, 3 * TILE)


def attend_body(layout, dsh, n_ref, w_ref, rows_ref, *refs):
    pieces, (att_ref, scratch) = refs[:-2], refs[-2:]
    values = dot(n_ref[...], assembled(pieces, layout, scratch, dsh)).astype(BF16)
    lane = lax.broadcasted_iota(jnp.int32, (TILE, LANES), 1)
    for g in range(HEADS // 2):
        cols = slice(g * LANES, (g + 1) * LANES)
        pair = w_ref[2 * g : 2 * g + 2].reshape(2 * TILE, 3 * TILE)
        total = jnp.zeros((2 * TILE, LANES), F32)
        for i in range(3):
            rows = slice(i * TILE, (i + 1) * TILE)
            total = total + rows_ref[1:2, rows] * dot(pair[:, rows], values[rows, cols])
        att_ref[:, cols] = jnp.where(lane < HD, total[:TILE], total[TILE:]).astype(BF16)


def forecast_body(layout, dsh, x_ref, att_ref, read_ref, *refs):
    pieces, (f_ref, wo_ref) = refs[:-2], refs[-2:]
    hidden = x_ref[0].astype(F32) + dot(att_ref[...], assembled(pieces, layout, wo_ref, dsh), NT)
    f_ref[...] = dot(hidden.astype(BF16), read_ref[...]).astype(BF16)


def sabs(a):
    mag = jnp.abs(a)
    return mag + 2.0 * BREADTH * jnp.log1p(jnp.exp(mag * (-1.0 / BREADTH)))


def backward_body(n_ens, factor, *refs):
    f_refs = refs[:n_ens]
    wo_ref, target_ref, lw_ref, read_ref, w_ref, rows_ref, gf_ref, con_ref = refs[n_ens:]
    lw = lw_ref[...]
    target = target_ref[...]
    fc = [ref[...].astype(F32) for ref in f_refs]
    sums = [jnp.zeros((TILE, LANES), F32) for _ in range(n_ens)]
    for i in range(n_ens):
        for j in range(i + 1, n_ens):
            t = jnp.tanh((fc[i] - fc[j]) / (2.0 * BREADTH))
            sums[i] = sums[i] + t
            sums[j] = sums[j] - t
    for i in range(n_ens):
        t = jnp.tanh((fc[i] - target) / (2.0 * BREADTH))
        gf_ref[i * TILE : (i + 1) * TILE, :] = (lw * (t - sums[i] / (n_ens - 1)) * factor).astype(BF16)
    others = jnp.zeros((TILE, LANES), F32)
    for j in range(1, n_ens):
        others = others + sabs(fc[0] - fc[j])
    terms = lw * (sabs(fc[0] - target) - others / (2.0 * (n_ens - 1)))
    loss = jnp.full((16, LANES), jnp.sum(terms), F32)
    for i in range(con_ref.shape[1] // LANES):
        part = loss.astype(BF16)
        con_ref[3 * TILE :, i * LANES : (i + 1) * LANES] = part
        loss = loss - part.astype(F32)
    grad_hidden = dot(gf_ref[:TILE, :], read_ref[...], NT).astype(BF16)
    grad_att = dot(grad_hidden, wo_ref[...]).astype(BF16)
    lane = lax.broadcasted_iota(jnp.int32, (TILE, LANES), 1)
    zero = jnp.zeros((), BF16)
    for g in range(HEADS // 2):
        cols = slice(g * LANES, (g + 1) * LANES)
        pair = grad_att[:, cols]
        pair = jnp.concatenate([jnp.where(lane < HD, pair, zero), jnp.where(lane < HD, zero, pair)], axis=0)
        both = dot(w_ref[2 * g : 2 * g + 2].reshape(2 * TILE, 3 * TILE), pair, TN)
        for i in range(3):
            rows = slice(i * TILE, (i + 1) * TILE)
            con_ref[rows, cols] = (both[rows] * rows_ref[1:2, rows]).astype(BF16)


def own_value_body(keep_ref, own_con, term_ref):
    term_ref[...] = dot(keep_ref[...], own_con[: 3 * TILE, :])


def value_body(blocks, dsh, rows, own_term, sib_ref, own_con, sib_con, v_ref, loss_ref):
    keys = 3 * TILE
    term = own_term[...] + dot(sib_ref[...], sib_con[:keys, :])
    parts = []
    for ref in (own_con, sib_con):
        part = ref[keys:, :].astype(F32)
        parts.append(part[:, :LANES] + part[:, LANES : 2 * LANES] + part[:, 2 * LANES : 3 * LANES])
    loss_ref[...] = (parts[0] + parts[1])[:8]
    for b in range(blocks):
        for cb in range(term.shape[1] // LANES):
            for first in range(0, dsh, rows):
                piece = (cb * dsh + first) // rows
                part = term[b * dsh + first : b * dsh + first + rows, cb * LANES : (cb + 1) * LANES]
                v_ref[b, piece % 2, piece // 2 * rows : (piece // 2 + 1) * rows, :] = part


def output_body(n_ens, dsh, gf_ref, read_ref, *refs):
    att_refs = refs[:n_ens]
    o_ref, scratch = refs[n_ens:]
    start = pl.multiple_of(lax.axis_index("ens") * dsh, dsh)
    for j in range(n_ens):
        scratch[j * TILE : (j + 1) * TILE, :] = att_refs[j][...]
    turned = dot(read_ref[pl.ds(start, dsh), :], gf_ref[...], NT).astype(BF16)
    term = dot(turned, scratch[...])
    for cb in range(term.shape[1] // LANES):
        o_ref[cb * dsh : (cb + 1) * dsh, :] = term[:, cb * LANES : (cb + 1) * LANES]


def finish_body(n_pix, dsh, scale, *refs):
    top = n_pix // 2
    pieces = refs[:top]
    total_ref, gv_ref, go_ref, loss_ref, scratch = refs[top:]
    loss_ref[...] = total_ref[:1, :1] * scale
    rows = scratch.shape[1] // n_pix
    position = lax.axis_index("pix") % top
    for j, ref in enumerate(pieces):
        for side in (0, 1):
            start = pl.multiple_of(((position ^ j) + side * top) * rows, rows)
            scratch[:, pl.ds(start, rows), :] = ref[:, side * rows : (side + 1) * rows, :].astype(F32)
    for cb in range(scratch.shape[1] // dsh):
        gv_ref[:, cb * LANES : (cb + 1) * LANES] = scratch[0, cb * dsh : (cb + 1) * dsh, :]
        go_ref[cb * LANES : (cb + 1) * LANES, :] = scratch[1, cb * dsh : (cb + 1) * dsh, :].T


def in_parts(total):
    first = lax.reduce_precision(total, 8, 7)
    return [first.astype(BF16), (total - first).astype(BF16)]


def with_loss(block, total):
    return jnp.concatenate([block.reshape(-1, LANES).astype(BF16)] + in_parts(total), axis=0)


def split_loss(message):
    parts = message[-16:].astype(F32).reshape(2, 8, LANES)
    return message[:-16], parts[0] + parts[1]


def gathered(value, axis, bits):
    pieces = {0: value}
    for bit in bits:
        held = lax.optimization_barrier(pieces)
        pieces = held | {j ^ bit: xor_permute(piece, axis, bit) for j, piece in held.items()}
    return pieces


def in_order(pieces):
    return [pieces[j] for j in sorted(pieces)]


def joined(arrays):
    return arrays[0] if len(arrays) == 1 else jnp.concatenate(arrays)


def both_cores(pieces):
    held = lax.optimization_barrier(pieces)
    return in_order(held | {j ^ 1: xor_permute(piece, "ens", 1) for j, piece in held.items()})


def at(blocks, index):
    return lax.dynamic_index_in_dim(blocks, index, 0, keepdims=False)


def part_of(split, index):
    return lax.dynamic_index_in_dim(split, index, 1, keepdims=False).reshape(-1, LANES)


def per_device(
    sample_layer_feed,
    gain,
    w_query,
    w_key,
    w_value,
    w_out,
    readout_matrix,
    target,
    pixel_weight,
    pix_mask,
    neighbours,
    neighbour_mask,
):
    n_ens, n_pix = lax.axis_size("ens"), lax.axis_size("pix")
    dsh, inner = w_query.shape
    d_model = dsh * n_ens
    n_out = readout_matrix.shape[1]
    ens_bits = [1 << b for b in reversed(range(n_ens.bit_length() - 1))]
    e, p = lax.axis_index("ens"), lax.axis_index("pix")
    rows = sample_layer_feed.shape[1]
    assert rows == TILE and n_out == LANES

    far = ens_bits[:-1]
    mask_rows = pix_mask.reshape(n_pix, TILE)
    half, side = dsh // 2, (p // 2) % 2
    w_vo = jnp.concatenate([w_value, w_out.T])

    def half_of(w):
        return jnp.where(side == 0, w[:half], w[half:])

    qk_far = gathered(jnp.concatenate([w_query, half_of(w_key)]), "ens", far)
    vo_far = gathered(w_vo, "ens", far)
    up = lax.ppermute(sample_layer_feed, "pix", [(i, i + 1) for i in range(n_pix - 1)])
    down = lax.ppermute(sample_layer_feed, "pix", [(i + 1, i) for i in range(n_pix - 1)])
    w_qk = jnp.concatenate([w_query, w_key])
    qk_near = xor_permute(w_qk, "ens", 1)
    turned = ((d_model // 2, 3 * TILE), BF16)
    normed, turned_keep, turned_send, lw, key_rows = call(
        functools.partial(normed_body, n_ens, dsh),
        [((3 * TILE, d_model), BF16), turned, turned, ((TILE, LANES), F32), ((8, 3 * TILE), F32)],
        [("v", sample_layer_feed), ("v", up), ("v", down), ("v", gain.reshape(1, -1))]
        + [("v", pixel_weight.reshape(1, TILE)), ("v", mask_rows), ("s", neighbours), ("s", neighbour_mask)],
        10**7,
        "normed",
        scratch=[pltpu.VMEM((d_model, 3 * TILE), BF16)],
    )

    shards = sorted(j for j in qk_far if j)
    qk_far = [qk_far[j] for j in shards]
    k_far = joined([rows[dsh:] for rows in qk_far])
    k_other = xor_permute(k_far, "pix", 2)
    normed, qk_near, k_far, k_other, qk_far = lax.optimization_barrier((normed, qk_near, k_far, k_other, qk_far))
    q_far = joined([rows[:dsh] for rows in qk_far])
    q_cross = [xor_permute(part, "ens", 1) for part in jnp.split(q_far, 2 * len(shards))]
    k_cross, k_other_cross = xor_permute(k_far, "ens", 1), xor_permute(k_other, "ens", 1)
    parts = [q_far, k_far, k_other, k_cross, k_other_cross] + q_cross
    q_layout, k_layout = ([(0, m * dsh, dsh, 0, 0), (1, m * dsh, dsh, 1, 0)] for m in (0, 1))
    for i, j in enumerate(shards):
        q_layout.append((2, i * dsh, dsh, j, 0))
        q_layout += [(7 + 2 * i + m, 0, half, j ^ 1, m) for m in (0, 1)]
        k_layout += [(3 + m, i * half, half, j, 2 + m) for m in (0, 1)]
        k_layout += [(5 + m, i * half, half, j ^ 1, 2 + m) for m in (0, 1)]

    def layout(first):
        table = [(0, first, dsh, 0, 0), (1, 0, dsh, 1, 0)]
        for i, j in enumerate(shards):
            table += [(2, i * dsh, dsh, j, 0), (3, i * dsh, dsh, j ^ 1, 0)]
        return table

    full = pltpu.VMEM((d_model, inner), BF16)
    (weights,) = call(
        functools.partial(weights_body, q_layout, k_layout, dsh),
        [((HEADS, TILE, 3 * TILE), BF16)],
        [("v", normed), ("v", key_rows)]
        + [("v", a) for a in [w_qk, qk_near] + parts],
        10**3,
        "weights",
        scratch=[full],
    )
    weights, vo_far, turned_send, w_vo = lax.optimization_barrier((weights, vo_far, turned_send, w_vo))
    vo_near = [xor_permute(w_vo[:dsh], "ens", 1), xor_permute(w_vo[dsh:], "ens", 1)]
    vo_far = [joined([vo_far[j][m * dsh : (m + 1) * dsh] for j in shards]) for m in (0, 1)]
    vo_cross = [xor_permute(part, "ens", 1) for part in vo_far]
    turned_sib = xor_permute(turned_send, "ens", 1)
    (attended,) = call(
        functools.partial(attend_body, layout(0), dsh),
        [((TILE, inner), BF16)],
        [("v", normed), ("v", weights), ("v", key_rows)]
        + [("v", a) for a in (w_vo, vo_near[0], vo_far[0], vo_cross[0])],
        10**9,
        "attend",
        scratch=[full],
    )
    forecast, w_out_full = call(
        functools.partial(forecast_body, layout(dsh), dsh),
        [((TILE, LANES), BF16), ((d_model, inner), BF16)],
        [("v", sample_layer_feed), ("v", attended), ("v", readout_matrix)]
        + [("v", a) for a in (w_vo, vo_near[1], vo_far[1], vo_cross[1])],
        10**9,
        "forecast",
    )
    forecasts = in_order(gathered(forecast, "ens", ens_bits))
    forecast, attended = lax.optimization_barrier((forecast, attended))
    forecasts, turned_sib = lax.optimization_barrier((forecasts, turned_sib))
    attended_near = gathered(attended, "ens", far)

    factor = 1.0 / math.sqrt(n_ens * n_pix * TILE)
    grads, contrib = call(
        functools.partial(backward_body, n_ens, factor),
        [((n_ens * TILE, LANES), BF16), ((3 * TILE + 16, inner), BF16)],
        [("v", a) for a in forecasts + [w_out_full]]
        + [("v", target), ("v", lw), ("v", readout_matrix)]
        + [("v", weights), ("v", key_rows)],
        10**9,
        "backward",
    )
    contrib, attended_near = lax.optimization_barrier((contrib, attended_near))
    contrib_sib = xor_permute(contrib, "ens", 1)
    attended_all = both_cores(attended_near)
    blocks = n_ens // 2
    (own_term,) = call(
        own_value_body,
        [((d_model // 2, inner), F32)],
        [("v", turned_keep), ("v", contrib)],
        10**3,
        "own_value",
    )
    value_term, loss = call(
        functools.partial(value_body, blocks, dsh, dsh * inner // (LANES * n_pix)),
        [((blocks, 2, dsh * inner // (2 * LANES), LANES), F32), ((8, LANES), F32)],
        [("v", own_term), ("v", turned_sib), ("v", contrib), ("v", contrib_sib)],
        10**9,
        "value_term",
    )
    value_term, loss, grads = lax.optimization_barrier((value_term, loss, grads))
    (output_term,) = call(
        functools.partial(output_body, n_ens, dsh),
        [((dsh * inner // LANES, LANES), F32)],
        [("v", grads), ("v", readout_matrix)] + [("v", a) for a in attended_all],
        10**9,
        "output_term",
        scratch=[pltpu.VMEM((n_ens * TILE, inner), BF16)],
    )

    for bit in far[:-1]:
        upper = (e // bit) % 2
        halves = value_term.reshape(2, -1, LANES)
        got, other = split_loss(xor_permute(with_loss(at(halves, 1 - upper), loss), "ens", bit))
        value_term = at(halves, upper) + got.astype(F32)
        loss = loss + other

    n_bits = n_pix.bit_length() - 1
    groups = [[1]] + [[1 << b for b in range(s, min(s + 2, n_bits))] for s in range(1, n_bits, 2)]

    def pieces_of(term, group, higher=None):
        size = 1 << len(group)
        higher = n_pix // (group[0] * size) if higher is None else higher
        return term.reshape(higher, size, -1, LANES)

    def exchanged(messages, group):
        return [xor_permute(m, "pix", (d + 1) * group[0]) for d, m in enumerate(messages)]

    def sent(term, group, total=None, higher=None):
        size, pos = 1 << len(group), (p // group[0]) % (1 << len(group))
        split = pieces_of(term, group, higher)
        messages = [part_of(split, pos ^ d).astype(BF16) for d in range(1, size)]
        if total is not None:
            messages = [with_loss(m, total) for m in messages]
        return part_of(split, pos), exchanged(messages, group)

    def added(kept, received):
        return functools.reduce(jnp.add, [m.astype(F32) for m in received], kept)

    later = [bit for group in groups[1:] for bit in group]
    for bit in later[:-2]:
        output_term = added(*sent(output_term, [bit]))
    output_kept, output_got = sent(output_term, [later[-2]])
    upper, low = (e // far[-1]) % 2, p % 2
    quarters = value_term.reshape(4, -1, LANES)
    pos = 2 * upper + low
    received = []
    for d in (2, 1, 3):
        pairs = [
            (i * n_pix + k, (i ^ (far[-1] * (d // 2))) * n_pix + (k ^ (d % 2)))
            for i in range(n_ens)
            for k in range(n_pix)
        ]
        message = with_loss(at(quarters, pos ^ d), loss)
        received.append((d, split_loss(lax.ppermute(message, ("ens", "pix"), pairs))))
    value_term = at(quarters, pos)
    losses = {0: loss}
    for d, (block, other) in received:
        value_term = value_term + block.astype(F32)
        losses[d] = other
    losses = jnp.stack([losses[d] for d in range(4)])
    loss = functools.reduce(jnp.add, [at(losses, pos ^ i) for i in range(4)])

    value_term, output_got = lax.optimization_barrier((value_term, output_got))
    output_kept, output_got = sent(added(output_kept, output_got), groups[0], higher=2)
    for bit in later[:-1]:
        kept, received = sent(value_term, [bit], loss)
        block, other = split_loss(received[0])
        value_term, loss = added(kept, [block]), loss + other
    output_term = added(output_kept, output_got)
    both = jnp.concatenate([value_term, output_term]).astype(BF16)
    block, other = split_loss(xor_permute(with_loss(both, loss), "pix", later[-1]))
    loss = loss + other
    both = (both.astype(F32) + block.astype(F32)).astype(BF16)
    pieces = {0: both.reshape(2, -1, LANES)}
    rest = [1] + later[:-1]
    for stage in reversed([rest[i : i + 2] for i in range(0, len(rest), 2)]):
        keys = sorted(pieces)
        stack = pieces[0][None] if len(keys) == 1 else jnp.stack([pieces[j] for j in keys])
        for d in range(1, 1 << len(stage)):
            got = xor_permute(stack, "pix", d * stage[0])
            pieces.update({j ^ (d * stage[0]): got[i] for i, j in enumerate(keys)})
    scale = 1.0 / (n_ens * n_pix * TILE * n_out)
    grad_w_value, grad_w_out, loss = call(
        functools.partial(finish_body, n_pix, dsh, scale),
        [((dsh, inner), F32), ((inner, dsh), F32), ((1, 1), F32)],
        [("v", pieces[j]) for j in sorted(pieces)] + [("v", loss)],
        10**6,
        "finish",
        scratch=[pltpu.VMEM((2, dsh * inner // LANES, LANES), F32)],
    )
    return (loss.reshape(()), grad_w_out, grad_w_value)


def solution(mesh):
    in_specs = (
        P("ens", "pix", None),
        P(),
        P("ens", None),
        P("ens", None),
        P("ens", None),
        P(None, "ens"),
        P(),
        P("pix", None),
        P("pix"),
        P(),
        P("pix", None),
        P("pix", None),
    )
    out_specs = (P(), P(None, "ens"), P("ens", None))
    return jax.shard_map(
        per_device, mesh=mesh, in_specs=in_specs, out_specs=out_specs, check_vma=False
    )
```

```python
import functools
import math

import jax
import jax.numpy as jnp
from jax import lax
from jax.experimental import pallas as pl
from jax.experimental.pallas import tpu as pltpu
from jax.sharding import PartitionSpec as P

HEADS = 8
HD = 64
TILE = 128
NB = 9
LANES = 128
EPS = 1e-06
BREADTH = 0.1

F32 = jnp.float32
BF16 = jnp.bfloat16
VMEM = pl.BlockSpec(memory_space=pltpu.VMEM)
SMEM = pl.BlockSpec(memory_space=pltpu.SMEM)
NN = (((1,), (0,)), ((), ()))
NT = (((1,), (1,)), ((), ()))
TN = (((0,), (0,)), ((), ()))


def dot(a, b, dims=NN):
    return lax.dot_general(a, b, dims, preferred_element_type=F32)


def call(body, outs, ins, flops, name, scratch=(), vmem=32):
    specs = [SMEM if s == "s" else VMEM for s, _ in ins]
    return pl.pallas_call(
        body,
        out_shape=[jax.ShapeDtypeStruct(s, d) for s, d in outs],
        in_specs=specs,
        out_specs=[VMEM] * len(outs),
        scratch_shapes=list(scratch),
        compiler_params=pltpu.CompilerParams(vmem_limit_bytes=vmem * 2**20),
        cost_estimate=pl.CostEstimate(flops=flops, bytes_accessed=flops // 1000, transcendentals=0),
        name=name,
    )(*[a for _, a in ins])


def xor_permute(value, axis, mask):
    size = lax.axis_size(axis)
    return lax.ppermute(value, axis, [(i, i ^ mask) for i in range(size)])


def counts_of(nb_ref, nm_ref, position):
    counts = []
    for d in (-1, 0, 1):
        total = jnp.int32(0)
        for s in range(NB):
            hit = (nb_ref[0, s] == position + d) & (nm_ref[0, s] > 0)
            total = total + jnp.where(hit, 1, 0)
        counts.append(total.astype(F32))
    return counts


def normed_body(
    n_ens, dsh, x_ref, up_ref, down_ref, gain_ref, pw_ref, mask_ref, nb_ref, nm_ref, *refs
):
    n_ref, keep_ref, send_ref, lw_ref, rows_ref, turned_ref = refs
    core, position = lax.axis_index("ens") % 2, lax.axis_index("pix")
    counts = counts_of(nb_ref, nm_ref, position)
    for i, d in enumerate((-1, 0, 1)):
        row = jnp.clip(position + d, 0, mask_ref.shape[0] - 1)
        named = jnp.full((1, TILE), counts[i], F32)
        cols = slice(i * TILE, (i + 1) * TILE)
        rows_ref[0:1, cols] = jnp.where(mask_ref[pl.ds(row, 1), :] > 0, named, 0.0)
        rows_ref[1:2, cols] = named
    rows_ref[2:, :] = jnp.zeros((6, 3 * TILE), F32)
    live = jnp.where(mask_ref[pl.ds(position, 1), :] > 0, 1.0, 0.0)
    lw_ref[...] = jnp.broadcast_to(pw_ref[...] * live, (LANES, TILE)).T
    gain = gain_ref[...]
    for i, ref in enumerate((up_ref, x_ref, down_ref)):
        rows = ref[0].astype(F32)
        inv = lax.rsqrt(jnp.mean(rows * rows, axis=-1, keepdims=True) + EPS)
        n_ref[i * TILE : (i + 1) * TILE, :] = (rows * inv * gain).astype(BF16)
    turned_ref[...] = n_ref[...].T
    for b in range(n_ens // 2):
        mine = pl.multiple_of((2 * b + core) * dsh, dsh)
        theirs = pl.multiple_of((2 * b + 1 - core) * dsh, dsh)
        keep_ref[b * dsh : (b + 1) * dsh, :] = turned_ref[pl.ds(mine, dsh), :]
        send_ref[b * dsh : (b + 1) * dsh, :] = turned_ref[pl.ds(theirs, dsh), :]


def assembled(refs, layout, scratch, dsh):
    me, side = lax.axis_index("ens"), (lax.axis_index("pix") // 2) % 2
    for which, first, rows, j, place in layout:
        offset = place * rows if place < 2 else (side ^ (place - 2)) * rows
        start = pl.multiple_of((me ^ j) * dsh + offset, rows)
        scratch[pl.ds(start, rows), :] = refs[which][first : first + rows, :]
    return scratch[...]


def weights_body(q_layout, k_layout, dsh, n_ref, rows_ref, *refs):
    pieces, (w_ref, scratch) = refs[:-2], refs[-2:]
    times = rows_ref[0:1, :]
    bias = jnp.where(times > 0, 0.0, -1e30)
    queries = dot(n_ref[TILE : 2 * TILE, :], assembled(pieces, q_layout, scratch, dsh)).astype(BF16)
    keys = dot(n_ref[...], assembled(pieces, k_layout, scratch, dsh)).astype(BF16)
    lane = lax.broadcasted_iota(jnp.int32, (TILE, LANES), 1)
    zero = jnp.zeros((), BF16)
    for g in range(HEADS // 2):
        cols = slice(g * LANES, (g + 1) * LANES)
        pair = queries[:, cols]
        pair = jnp.concatenate([jnp.where(lane < HD, pair, zero), jnp.where(lane < HD, zero, pair)], axis=0)
        scores = dot(pair, keys[:, cols], NT) * HD ** (-0.5) + bias
        top = jnp.max(scores, axis=-1, keepdims=True)
        expos = jnp.exp(scores - top)
        total = jnp.sum(expos * times, axis=-1, keepdims=True)
        w_ref[2 * g : 2 * g + 2] = (expos / total).astype(BF16).reshape(2, TILE, 3 * TILE)


def attend_body(layout, dsh, n_ref, w_ref, rows_ref, *refs):
    pieces, (att_ref, scratch) = refs[:-2], refs[-2:]
    values = dot(n_ref[...], assembled(pieces, layout, scratch, dsh)).astype(BF16)
    lane = lax.broadcasted_iota(jnp.int32, (TILE, LANES), 1)
    for g in range(HEADS // 2):
        cols = slice(g * LANES, (g + 1) * LANES)
        pair = w_ref[2 * g : 2 * g + 2].reshape(2 * TILE, 3 * TILE)
        total = jnp.zeros((2 * TILE, LANES), F32)
        for i in range(3):
            rows = slice(i * TILE, (i + 1) * TILE)
            total = total + rows_ref[1:2, rows] * dot(pair[:, rows], values[rows, cols])
        att_ref[:, cols] = jnp.where(lane < HD, total[:TILE], total[TILE:]).astype(BF16)


def forecast_body(layout, dsh, x_ref, att_ref, read_ref, *refs):
    pieces, (f_ref, wo_ref) = refs[:-2], refs[-2:]
    hidden = x_ref[0].astype(F32) + dot(att_ref[...], assembled(pieces, layout, wo_ref, dsh), NT)
    f_ref[...] = dot(hidden.astype(BF16), read_ref[...]).astype(BF16)


def sabs(a):
    mag = jnp.abs(a)
    return mag + 2.0 * BREADTH * jnp.log1p(jnp.exp(mag * (-1.0 / BREADTH)))


def backward_body(n_ens, factor, *refs):
    f_refs = refs[:n_ens]
    wo_ref, target_ref, lw_ref, read_ref, w_ref, rows_ref, con_ref = refs[n_ens:]
    lw = lw_ref[...]
    target = target_ref[...]
    fc = [ref[...].astype(F32) for ref in f_refs]
    tangents = jnp.zeros((TILE, LANES), F32)
    for j in range(1, n_ens):
        tangents = tangents + jnp.tanh((fc[0] - fc[j]) / (2.0 * BREADTH))
    own = jnp.tanh((fc[0] - target) / (2.0 * BREADTH)) - tangents / (n_ens - 1)
    own = (lw * own * factor).astype(BF16)
    others = jnp.zeros((TILE, LANES), F32)
    for j in range(1, n_ens):
        others = others + sabs(fc[0] - fc[j])
    terms = lw * (sabs(fc[0] - target) - others / (2.0 * (n_ens - 1)))
    loss = jnp.full((16, LANES), jnp.sum(terms), F32)
    for i in range(con_ref.shape[1] // LANES):
        part = loss.astype(BF16)
        con_ref[3 * TILE :, i * LANES : (i + 1) * LANES] = part
        loss = loss - part.astype(F32)
    grad_hidden = dot(own, read_ref[...], NT).astype(BF16)
    grad_att = dot(grad_hidden, wo_ref[...]).astype(BF16)
    lane = lax.broadcasted_iota(jnp.int32, (TILE, LANES), 1)
    zero = jnp.zeros((), BF16)
    for g in range(HEADS // 2):
        cols = slice(g * LANES, (g + 1) * LANES)
        pair = grad_att[:, cols]
        pair = jnp.concatenate([jnp.where(lane < HD, pair, zero), jnp.where(lane < HD, zero, pair)], axis=0)
        both = dot(w_ref[2 * g : 2 * g + 2].reshape(2 * TILE, 3 * TILE), pair, TN)
        for i in range(3):
            rows = slice(i * TILE, (i + 1) * TILE)
            con_ref[rows, cols] = (both[rows] * rows_ref[1:2, rows]).astype(BF16)


def own_value_body(keep_ref, own_con, term_ref):
    term_ref[...] = dot(keep_ref[...], own_con[: 3 * TILE, :])


def value_body(blocks, dsh, rows, own_term, sib_ref, own_con, sib_con, v_ref, loss_ref):
    keys = 3 * TILE
    term = own_term[...] + dot(sib_ref[...], sib_con[:keys, :])
    parts = []
    for ref in (own_con, sib_con):
        part = ref[keys:, :].astype(F32)
        parts.append(part[:, :LANES] + part[:, LANES : 2 * LANES] + part[:, 2 * LANES : 3 * LANES])
    loss_ref[...] = (parts[0] + parts[1])[:8]
    for b in range(blocks):
        for cb in range(term.shape[1] // LANES):
            for first in range(0, dsh, rows):
                piece = (cb * dsh + first) // rows
                part = term[b * dsh + first : b * dsh + first + rows, cb * LANES : (cb + 1) * LANES]
                v_ref[b, piece % 2, piece // 2 * rows : (piece // 2 + 1) * rows, :] = part


def output_body(n_ens, dsh, factor, target_ref, lw_ref, read_ref, *refs):
    f_refs, att_refs = refs[:n_ens], refs[n_ens : 2 * n_ens]
    o_ref, scratch, gf_ref = refs[2 * n_ens :]
    lw, target = lw_ref[...], target_ref[...]
    fc = [ref[...].astype(F32) for ref in f_refs]
    sums = [jnp.zeros((TILE, LANES), F32) for _ in range(n_ens)]
    for i in range(n_ens):
        for j in range(i + 1, n_ens):
            t = jnp.tanh((fc[i] - fc[j]) / (2.0 * BREADTH))
            sums[i] = sums[i] + t
            sums[j] = sums[j] - t
    for i in range(n_ens):
        t = jnp.tanh((fc[i] - target) / (2.0 * BREADTH))
        gf_ref[i * TILE : (i + 1) * TILE, :] = (lw * (t - sums[i] / (n_ens - 1)) * factor).astype(BF16)
    start = pl.multiple_of(lax.axis_index("ens") * dsh, dsh)
    for j in range(n_ens):
        scratch[j * TILE : (j + 1) * TILE, :] = att_refs[j][...]
    turned = dot(read_ref[pl.ds(start, dsh), :], gf_ref[...], NT).astype(BF16)
    term = dot(turned, scratch[...])
    for cb in range(term.shape[1] // LANES):
        o_ref[cb * dsh : (cb + 1) * dsh, :] = term[:, cb * LANES : (cb + 1) * LANES]


def finish_body(n_pix, dsh, scale, *refs):
    top = n_pix // 2
    pieces = refs[:top]
    total_ref, gv_ref, go_ref, loss_ref, scratch = refs[top:]
    loss_ref[...] = total_ref[:1, :1] * scale
    rows = scratch.shape[1] // n_pix
    position = lax.axis_index("pix") % top
    for j, ref in enumerate(pieces):
        for side in (0, 1):
            start = pl.multiple_of(((position ^ j) + side * top) * rows, rows)
            scratch[:, pl.ds(start, rows), :] = ref[:, side * rows : (side + 1) * rows, :].astype(F32)
    for cb in range(scratch.shape[1] // dsh):
        gv_ref[:, cb * LANES : (cb + 1) * LANES] = scratch[0, cb * dsh : (cb + 1) * dsh, :]
        go_ref[cb * LANES : (cb + 1) * LANES, :] = scratch[1, cb * dsh : (cb + 1) * dsh, :].T


def in_parts(total):
    first = lax.reduce_precision(total, 8, 7)
    return [first.astype(BF16), (total - first).astype(BF16)]


def with_loss(block, total):
    return jnp.concatenate([block.reshape(-1, LANES).astype(BF16)] + in_parts(total), axis=0)


def split_loss(message):
    parts = message[-16:].astype(F32).reshape(2, 8, LANES)
    return message[:-16], parts[0] + parts[1]


def gathered(value, axis, bits):
    pieces = {0: value}
    for bit in bits:
        held = lax.optimization_barrier(pieces)
        pieces = held | {j ^ bit: xor_permute(piece, axis, bit) for j, piece in held.items()}
    return pieces


def in_order(pieces):
    return [pieces[j] for j in sorted(pieces)]


def joined(arrays):
    return arrays[0] if len(arrays) == 1 else jnp.concatenate(arrays)


def both_cores(pieces):
    held = lax.optimization_barrier(pieces)
    return in_order(held | {j ^ 1: xor_permute(piece, "ens", 1) for j, piece in held.items()})


def at(blocks, index):
    return lax.dynamic_index_in_dim(blocks, index, 0, keepdims=False)


def part_of(split, index):
    return lax.dynamic_index_in_dim(split, index, 1, keepdims=False).reshape(-1, LANES)


def per_device(
    sample_layer_feed,
    gain,
    w_query,
    w_key,
    w_value,
    w_out,
    readout_matrix,
    target,
    pixel_weight,
    pix_mask,
    neighbours,
    neighbour_mask,
):
    n_ens, n_pix = lax.axis_size("ens"), lax.axis_size("pix")
    dsh, inner = w_query.shape
    d_model = dsh * n_ens
    n_out = readout_matrix.shape[1]
    ens_bits = [1 << b for b in reversed(range(n_ens.bit_length() - 1))]
    e, p = lax.axis_index("ens"), lax.axis_index("pix")
    rows = sample_layer_feed.shape[1]
    assert rows == TILE and n_out == LANES

    far = ens_bits[:-1]
    mask_rows = pix_mask.reshape(n_pix, TILE)
    half, side = dsh // 2, (p // 2) % 2
    w_vo = jnp.concatenate([w_value, w_out.T])

    def half_of(w):
        return jnp.where(side == 0, w[:half], w[half:])

    qk_far = gathered(jnp.concatenate([w_query, half_of(w_key)]), "ens", far)
    vo_far = gathered(w_vo, "ens", far)
    up = lax.ppermute(sample_layer_feed, "pix", [(i, i + 1) for i in range(n_pix - 1)])
    down = lax.ppermute(sample_layer_feed, "pix", [(i + 1, i) for i in range(n_pix - 1)])
    w_qk = jnp.concatenate([w_query, w_key])
    qk_near = xor_permute(w_qk, "ens", 1)
    turned = ((d_model // 2, 3 * TILE), BF16)
    normed, turned_keep, turned_send, lw, key_rows = call(
        functools.partial(normed_body, n_ens, dsh),
        [((3 * TILE, d_model), BF16), turned, turned, ((TILE, LANES), F32), ((8, 3 * TILE), F32)],
        [("v", sample_layer_feed), ("v", up), ("v", down), ("v", gain.reshape(1, -1))]
        + [("v", pixel_weight.reshape(1, TILE)), ("v", mask_rows), ("s", neighbours), ("s", neighbour_mask)],
        10**7,
        "normed",
        scratch=[pltpu.VMEM((d_model, 3 * TILE), BF16)],
    )

    shards = sorted(j for j in qk_far if j)
    qk_far = [qk_far[j] for j in shards]
    k_far = joined([rows[dsh:] for rows in qk_far])
    k_other = xor_permute(k_far, "pix", 2)
    normed, qk_near, k_far, k_other, qk_far = lax.optimization_barrier((normed, qk_near, k_far, k_other, qk_far))
    q_far = joined([rows[:dsh] for rows in qk_far])
    q_cross = [xor_permute(part, "ens", 1) for part in jnp.split(q_far, 2 * len(shards))]
    k_cross, k_other_cross = xor_permute(k_far, "ens", 1), xor_permute(k_other, "ens", 1)
    parts = [q_far, k_far, k_other, k_cross, k_other_cross] + q_cross
    q_layout, k_layout = ([(0, m * dsh, dsh, 0, 0), (1, m * dsh, dsh, 1, 0)] for m in (0, 1))
    for i, j in enumerate(shards):
        q_layout.append((2, i * dsh, dsh, j, 0))
        q_layout += [(7 + 2 * i + m, 0, half, j ^ 1, m) for m in (0, 1)]
        k_layout += [(3 + m, i * half, half, j, 2 + m) for m in (0, 1)]
        k_layout += [(5 + m, i * half, half, j ^ 1, 2 + m) for m in (0, 1)]

    def layout(first):
        table = [(0, first, dsh, 0, 0), (1, 0, dsh, 1, 0)]
        for i, j in enumerate(shards):
            table += [(2, i * dsh, dsh, j, 0), (3, i * dsh, dsh, j ^ 1, 0)]
        return table

    full = pltpu.VMEM((d_model, inner), BF16)
    (weights,) = call(
        functools.partial(weights_body, q_layout, k_layout, dsh),
        [((HEADS, TILE, 3 * TILE), BF16)],
        [("v", normed), ("v", key_rows)]
        + [("v", a) for a in [w_qk, qk_near] + parts],
        10**3,
        "weights",
        scratch=[full],
    )
    weights, vo_far, turned_send, w_vo = lax.optimization_barrier((weights, vo_far, turned_send, w_vo))
    vo_near = [xor_permute(w_vo[:dsh], "ens", 1), xor_permute(w_vo[dsh:], "ens", 1)]
    vo_far = [joined([vo_far[j][m * dsh : (m + 1) * dsh] for j in shards]) for m in (0, 1)]
    vo_cross = [xor_permute(part, "ens", 1) for part in vo_far]
    turned_sib = xor_permute(turned_send, "ens", 1)
    (attended,) = call(
        functools.partial(attend_body, layout(0), dsh),
        [((TILE, inner), BF16)],
        [("v", normed), ("v", weights), ("v", key_rows)]
        + [("v", a) for a in (w_vo, vo_near[0], vo_far[0], vo_cross[0])],
        10**9,
        "attend",
        scratch=[full],
    )
    forecast, w_out_full = call(
        functools.partial(forecast_body, layout(dsh), dsh),
        [((TILE, LANES), BF16), ((d_model, inner), BF16)],
        [("v", sample_layer_feed), ("v", attended), ("v", readout_matrix)]
        + [("v", a) for a in (w_vo, vo_near[1], vo_far[1], vo_cross[1])],
        10**9,
        "forecast",
    )
    forecasts = in_order(gathered(forecast, "ens", ens_bits))
    forecast, attended = lax.optimization_barrier((forecast, attended))
    forecasts, turned_sib = lax.optimization_barrier((forecasts, turned_sib))
    attended_near = gathered(attended, "ens", far)

    factor = 1.0 / math.sqrt(n_ens * n_pix * TILE)
    (contrib,) = call(
        functools.partial(backward_body, n_ens, factor),
        [((3 * TILE + 16, inner), BF16)],
        [("v", a) for a in forecasts + [w_out_full]]
        + [("v", target), ("v", lw), ("v", readout_matrix)]
        + [("v", weights), ("v", key_rows)],
        10**9,
        "backward",
    )
    contrib, attended_near = lax.optimization_barrier((contrib, attended_near))
    contrib_sib = xor_permute(contrib, "ens", 1)
    attended_all = both_cores(attended_near)
    blocks = n_ens // 2
    (own_term,) = call(
        own_value_body,
        [((d_model // 2, inner), F32)],
        [("v", turned_keep), ("v", contrib)],
        10**3,
        "own_value",
    )
    value_term, loss = call(
        functools.partial(value_body, blocks, dsh, dsh * inner // (LANES * n_pix)),
        [((blocks, 2, dsh * inner // (2 * LANES), LANES), F32), ((8, LANES), F32)],
        [("v", own_term), ("v", turned_sib), ("v", contrib), ("v", contrib_sib)],
        10**9,
        "value_term",
    )
    value_term, loss, lw = lax.optimization_barrier((value_term, loss, lw))
    (output_term,) = call(
        functools.partial(output_body, n_ens, dsh, factor),
        [((dsh * inner // LANES, LANES), F32)],
        [("v", target), ("v", lw), ("v", readout_matrix)] + [("v", a) for a in forecasts + attended_all],
        10**9,
        "output_term",
        scratch=[pltpu.VMEM((n_ens * TILE, inner), BF16), pltpu.VMEM((n_ens * TILE, LANES), BF16)],
    )

    for bit in far[:-1]:
        upper = (e // bit) % 2
        halves = value_term.reshape(2, -1, LANES)
        got, other = split_loss(xor_permute(with_loss(at(halves, 1 - upper), loss), "ens", bit))
        value_term = at(halves, upper) + got.astype(F32)
        loss = loss + other

    n_bits = n_pix.bit_length() - 1
    groups = [[1]] + [[1 << b for b in range(s, min(s + 2, n_bits))] for s in range(1, n_bits, 2)]

    def pieces_of(term, group, higher=None):
        size = 1 << len(group)
        higher = n_pix // (group[0] * size) if higher is None else higher
        return term.reshape(higher, size, -1, LANES)

    def exchanged(messages, group):
        return [xor_permute(m, "pix", (d + 1) * group[0]) for d, m in enumerate(messages)]

    def sent(term, group, total=None, higher=None):
        size, pos = 1 << len(group), (p // group[0]) % (1 << len(group))
        split = pieces_of(term, group, higher)
        messages = [part_of(split, pos ^ d).astype(BF16) for d in range(1, size)]
        if total is not None:
            messages = [with_loss(m, total) for m in messages]
        return part_of(split, pos), exchanged(messages, group)

    def added(kept, received):
        return functools.reduce(jnp.add, [m.astype(F32) for m in received], kept)

    later = [bit for group in groups[1:] for bit in group]
    for bit in later[:-2]:
        output_term = added(*sent(output_term, [bit]))
    output_kept, output_got = sent(output_term, [later[-2]])
    upper, low = (e // far[-1]) % 2, p % 2
    quarters = value_term.reshape(4, -1, LANES)
    pos = 2 * upper + low
    received = []
    for d in (2, 1, 3):
        pairs = [
            (i * n_pix + k, (i ^ (far[-1] * (d // 2))) * n_pix + (k ^ (d % 2)))
            for i in range(n_ens)
            for k in range(n_pix)
        ]
        message = with_loss(at(quarters, pos ^ d), loss)
        received.append((d, split_loss(lax.ppermute(message, ("ens", "pix"), pairs))))
    value_term = at(quarters, pos)
    losses = {0: loss}
    for d, (block, other) in received:
        value_term = value_term + block.astype(F32)
        losses[d] = other
    losses = jnp.stack([losses[d] for d in range(4)])
    loss = functools.reduce(jnp.add, [at(losses, pos ^ i) for i in range(4)])

    value_term, output_got = lax.optimization_barrier((value_term, output_got))
    output_kept, output_got = sent(added(output_kept, output_got), groups[0], higher=2)
    for bit in later[:-1]:
        kept, received = sent(value_term, [bit], loss)
        block, other = split_loss(received[0])
        value_term, loss = added(kept, [block]), loss + other
    output_term = added(output_kept, output_got)
    both = jnp.concatenate([value_term, output_term]).astype(BF16)
    block, other = split_loss(xor_permute(with_loss(both, loss), "pix", later[-1]))
    loss = loss + other
    both = (both.astype(F32) + block.astype(F32)).astype(BF16)
    pieces = {0: both.reshape(2, -1, LANES)}
    rest = [1] + later[:-1]
    for stage in reversed([rest[i : i + 2] for i in range(0, len(rest), 2)]):
        keys = sorted(pieces)
        stack = pieces[0][None] if len(keys) == 1 else jnp.stack([pieces[j] for j in keys])
        for d in range(1, 1 << len(stage)):
            got = xor_permute(stack, "pix", d * stage[0])
            pieces.update({j ^ (d * stage[0]): got[i] for i, j in enumerate(keys)})
    scale = 1.0 / (n_ens * n_pix * TILE * n_out)
    grad_w_value, grad_w_out, loss = call(
        functools.partial(finish_body, n_pix, dsh, scale),
        [((dsh, inner), F32), ((inner, dsh), F32), ((1, 1), F32)],
        [("v", pieces[j]) for j in sorted(pieces)] + [("v", loss)],
        10**6,
        "finish",
        scratch=[pltpu.VMEM((2, dsh * inner // LANES, LANES), F32)],
    )
    return (loss.reshape(()), grad_w_out, grad_w_value)


def solution(mesh):
    in_specs = (
        P("ens", "pix", None),
        P(),
        P("ens", None),
        P("ens", None),
        P("ens", None),
        P(None, "ens"),
        P(),
        P("pix", None),
        P("pix"),
        P(),
        P("pix", None),
        P("pix", None),
    )
    out_specs = (P(), P(None, "ens"), P("ens", None))
    return jax.shard_map(
        per_device, mesh=mesh, in_specs=in_specs, out_specs=out_specs, check_vma=False
    )
```
